32 devices in a mesh: batch: 8 (over z, x), blk: 4 (over y, core).
Axes of the slice: x: 2, y: 2, z: 4, core: 2. Of those that a mesh axis runs over, the one named last changes fastest.
Arguments:
- tokens: bfloat16 [48, 512, 768], P('batch', 'blk'), may hold values from -6 to 6
- segment_ids: int32 [48, 512], P('batch'), may hold values from 0 to 2, as said below
- query_weight: bfloat16 [768, 768], replicated, may hold values from -0.21875 to 0.21875
- query_bias: bfloat16 [768], replicated, may hold values from -3 to 3
- key_weight: bfloat16 [768, 768], replicated, may hold values from -0.21875 to 0.21875
- value_weight: bfloat16 [768, 768], replicated, may hold values from -0.21875 to 0.21875
- value_bias: bfloat16 [768], replicated, may hold values from -3 to 3
- output_weight: bfloat16 [768, 768], replicated, may hold values from -0.625 to 0.625
- output_bias: bfloat16 [768], replicated, may hold values from -3 to 3
- attn_gain: bfloat16 [768], replicated, may hold values from 0.25 to 1.75
- attn_shift: bfloat16 [768], replicated, may hold values from -3 to 3
- inner_weight: bfloat16 [768, 3072], replicated, may hold values from -0.21875 to 0.21875
- inner_bias: bfloat16 [3072], replicated, may hold values from -3 to 3
- outer_weight: bfloat16 [3072, 768], replicated, may hold values from -0.15625 to 0.15625
- outer_bias: bfloat16 [768], replicated, may hold values from -3 to 3
- final_gain: bfloat16 [768], replicated, may hold values from 0.25 to 1.75
- final_shift: bfloat16 [768], replicated, may hold values from -3 to 3
- cotangent: bfloat16 [48, 512, 768], P('batch', 'blk'), may hold values from -6 to 6
Outputs:
- layer_output: bfloat16 [48, 512, 768], P('batch', 'blk')
- input_grad: bfloat16 [48, 512, 768], P('batch', 'blk')
- query_weight_grad: float32 [768, 768], P('batch')
- query_bias_grad: float32 [768], P('batch')
- key_weight_grad: float32 [768, 768], P('batch')
- value_weight_grad: float32 [768, 768], P('batch')
- value_bias_grad: float32 [768], P('batch')
- output_weight_grad: float32 [768, 768], P('batch')
- output_bias_grad: float32 [768], P('batch')
- attn_gain_grad: float32 [768], P('batch')
- attn_shift_grad: float32 [768], P('batch')
- inner_weight_grad: float32 [768, 3072], P('batch')
- inner_bias_grad: float32 [3072], P('batch')
- outer_weight_grad: float32 [3072, 768], P('batch')
- outer_bias_grad: float32 [768], P('batch')
- final_gain_grad: float32 [768], P('batch')
- final_shift_grad: float32 [768], P('batch')
The draws below stay inside these ranges and needn't reach their ends.
Inputs may be any that keep to these rules, and one draw needn't show every extreme that they name: `segment_ids`: every row holds the ids 0, 1 and 2 in that order, each as one run of positions; positions attend only within their own id. Id 1 covers the positions from some position below 128 to some position at or past 512 - 128.
All inputs are finite; a program needn't handle non-finite values.
Results may differ from the reference program's by a relative error of at most 0.02.
Values may be sent and summed in bfloat16 or wider, within the bound.
No kernel may reach another device: no remote copies, remote signals or barrier semaphores. Data moves between devices by JAX's collectives and lax.ppermute only.
A program may use at most 192 MiB of HBM per device.

```python
import math
import jax
import jax.numpy as jnp
from jax import lax

D = 768
H = 12
HD = 64
FF = 3072
LEN = 512
STRETCH = 128
ROWS = 48


def draw_segment_ids(key, part):
    key = jax.random.fold_in(key, 11)
    first_key, second_key = jax.random.split(key, 2)
    begin = jax.random.randint(first_key, (ROWS, 1), 1, STRETCH)
    finish = jax.random.randint(second_key, (ROWS, 1), LEN - STRETCH + 1, LEN)
    places = jnp.arange(LEN, dtype=jnp.int32)[None, :]
    cuts = (places >= begin).astype(jnp.int32) + (places >= finish).astype(jnp.int32)
    return cuts.astype(jnp.int32)


def block_scale(key, extent, cuts, low, top_value):
    level = 1.0
    for position, parts in cuts:
        steps = jax.random.uniform(jax.random.fold_in(jax.random.fold_in(key, 6), position), (parts,), jnp.float32, low / len(cuts), top_value / len(cuts))
        level = level * jnp.repeat(jnp.exp(steps), extent[position] // parts).reshape((-1,) + (1,) * (len(extent) - 1 - position))
    return level


def bell_draw(stream_key, extent, scale, reach, pieces=(), kind=jnp.bfloat16):
    entries = scale * jax.random.normal(stream_key, extent, jnp.float32)
    if pieces:
        entries = entries * block_scale(stream_key, extent, pieces, -0.22, 0.18)
    return jnp.clip(entries, -reach, reach).astype(kind)


def setup_inputs(seed: int = 0) -> dict:
    arg_keys = jax.random.split(jax.random.key(seed), 19)
    tokens = bell_draw(arg_keys[0], (ROWS, LEN, D), 1.0, 6.0, ((0, 8), (1, 4)))
    segment_ids = draw_segment_ids(jax.random.fold_in(arg_keys[18], 71), 0)
    query_weight = bell_draw(arg_keys[2], (D, D), D ** -0.5, 0.21875)
    query_bias = bell_draw(arg_keys[3], (D,), 0.5, 3.0)
    key_weight = bell_draw(arg_keys[4], (D, D), D ** -0.5, 0.21875)
    value_weight = bell_draw(arg_keys[5], (D, D), D ** -0.5, 0.21875)
    value_bias = bell_draw(arg_keys[6], (D,), 0.5, 3.0)
    output_weight = bell_draw(arg_keys[7], (D, D), (D // 8) ** -0.5, 0.625)
    output_bias = bell_draw(arg_keys[8], (D,), 0.5, 3.0)
    attn_gain = jnp.clip(1.0 + 0.15 * jax.random.normal(arg_keys[9], (D,), jnp.float32), 0.25, 1.75).astype(jnp.bfloat16)
    attn_shift = bell_draw(arg_keys[10], (D,), 0.5, 3.0)
    inner_weight = bell_draw(arg_keys[11], (D, FF), D ** -0.5, 0.21875)
    inner_bias = bell_draw(arg_keys[12], (FF,), 0.5, 3.0)
    outer_weight = bell_draw(arg_keys[13], (FF, D), (FF // 2) ** -0.5, 0.15625)
    outer_bias = bell_draw(arg_keys[14], (D,), 0.5, 3.0)
    final_gain = jnp.clip(1.0 + 0.15 * jax.random.normal(arg_keys[15], (D,), jnp.float32), 0.25, 1.75).astype(jnp.bfloat16)
    final_shift = bell_draw(arg_keys[16], (D,), 0.5, 3.0)
    cotangent = bell_draw(arg_keys[17], (ROWS, LEN, D), 1.0, 6.0, ((0, 8), (1, 4)))
    return dict(tokens=tokens, segment_ids=segment_ids, query_weight=query_weight, query_bias=query_bias, key_weight=key_weight, value_weight=value_weight, value_bias=value_bias, output_weight=output_weight, output_bias=output_bias, attn_gain=attn_gain, attn_shift=attn_shift, inner_weight=inner_weight, inner_bias=inner_bias, outer_weight=outer_weight, outer_bias=outer_bias, final_gain=final_gain, final_shift=final_shift, cotangent=cotangent)


@jax.custom_vjp
def low(v):
    return lax.optimization_barrier(v.astype(jnp.bfloat16)).astype(jnp.float32)

@jax.custom_vjp
def low_back(v):
    return v

def low_keep(v):
    return (low(v), None)

def low_pass(kept, grad):
    return (grad,)

def back_keep(v):
    return (v, None)

def back_low(kept, grad):
    return (low(grad),)
low.defvjp(low_keep, low_pass)
low_back.defvjp(back_keep, back_low)
EPSILON = 1e-12
NEGATIVE = -1e+30
HIGHEST = lax.Precision.HIGHEST

def norm_rows(hidden, gain, shift):
    center = hidden - lax.optimization_barrier(jnp.mean(hidden, axis=-1, keepdims=True))
    spread = lax.optimization_barrier(jnp.mean(center * center, axis=-1, keepdims=True))
    return center * lax.rsqrt(spread + EPSILON) * gain + shift

def project(inputs, matrix):
    return jnp.einsum('rtd,de->rte', inputs, matrix, precision=HIGHEST)

def layer_rows(inputs, segments, params):
    query_weight, query_bias, key_weight, value_weight, value_bias, output_weight, output_bias, attn_gain, attn_shift, inner_weight, inner_bias, outer_weight, outer_bias, final_gain, final_shift = params
    count, length, width = inputs.shape
    query = low(low_back(project(inputs, query_weight) + query_bias))
    key = low(low_back(project(inputs, key_weight)))
    value = low(low_back(project(inputs, value_weight) + value_bias))
    query_heads = query.reshape(count, length, H, HD)
    key_heads = key.reshape(count, length, H, HD)
    value_heads = value.reshape(count, length, H, HD)
    scores = low_back(jnp.einsum('rqhd,rkhd->rhqk', query_heads, key_heads, precision=HIGHEST) * HD ** (-0.5))
    allowed = segments[:, None, :, None] == segments[:, None, None, :]
    masked = jnp.where(allowed, scores, NEGATIVE)
    probs = low(jax.nn.softmax(masked, axis=-1))
    mixed = jnp.einsum('rhqk,rkhd->rqhd', probs, value_heads, precision=HIGHEST).reshape(count, length, width)
    mixed = low(low_back(mixed))
    branch = low_back(project(mixed, output_weight) + output_bias)
    first = norm_rows(inputs + branch, attn_gain, attn_shift)
    inner = low_back(project(low(first), inner_weight) + inner_bias)
    act = low(jax.nn.gelu(inner, approximate=False))
    outer = low_back(project(act, outer_weight) + outer_bias)
    return norm_rows(first + outer, final_gain, final_shift)

def reference(tokens, segment_ids, query_weight, query_bias, key_weight, value_weight, value_bias, output_weight, output_bias, attn_gain, attn_shift, inner_weight, inner_bias, outer_weight, outer_bias, final_gain, final_shift, cotangent):
    params = tuple((p.astype(jnp.float32) for p in (query_weight, query_bias, key_weight, value_weight, value_bias, output_weight, output_bias, attn_gain, attn_shift, inner_weight, inner_bias, outer_weight, outer_bias, final_gain, final_shift)))
    inputs = tokens.astype(jnp.float32)
    group = math.gcd(ROWS, 8)
    segments = segment_ids.reshape(ROWS // group, group, LEN)

    def forward(values, weights):
        blocks = values.reshape(ROWS // group, group, LEN, D)

        def one_group(pair):
            return layer_rows(pair[0], pair[1], weights)
        outputs = lax.map(jax.checkpoint(one_group), (blocks, segments))
        return outputs.reshape(ROWS, LEN, D)
    outputs, pull = jax.vjp(forward, inputs, params)
    input_grad, grads = pull(cotangent.astype(jnp.float32))
    return (outputs.astype(jnp.bfloat16), input_grad.astype(jnp.bfloat16), grads[0], grads[1], grads[2], grads[3], grads[4], grads[5], grads[6], grads[7], grads[8], grads[9], grads[10], grads[11], grads[12], grads[13], grads[14])
```

```python
import functools

import jax
import jax.numpy as jnp
from jax import lax
from jax.experimental import pallas as pl
from jax.experimental.pallas import tpu as pltpu
from jax.sharding import PartitionSpec as P

H = 12
HD = 64
EPSILON = 1e-12
NEGATIVE = -1e30
LOW = jnp.bfloat16
F32 = jnp.float32
LOG2E = 1.4426950408889634
MIB = 1024 * 1024


def dot_nn(a, b):
    return lax.dot_general(a, b, (((1,), (0,)), ((), ())), preferred_element_type=F32)


def dot_nt(a, b):
    return lax.dot_general(a, b, (((1,), (1,)), ((), ())), preferred_element_type=F32)


def dot_tn(a, b):
    return lax.dot_general(a, b, (((0,), (0,)), ((), ())), preferred_element_type=F32)


def params(mib):
    return pltpu.CompilerParams(vmem_limit_bytes=mib * MIB)


def attend_kernel(
    where, own, sib, seg_row, seg_col, wq, wk, wv, bq, bv,
    q_out, k_out, v_out, e_out, inv_out, mix_own, mix_sib,
):
    half = own.shape[1]
    x = jnp.concatenate([own[0], sib[0]], axis=0)
    q = (dot_nn(x, wq[...]) + bq[...].astype(F32)).astype(LOW)
    k = dot_nn(x, wk[...]).astype(LOW)
    v = (dot_nn(x, wv[...]) + bv[...].astype(F32)).astype(LOW)
    q_out[0] = q
    k_out[0] = k
    v_out[0] = v
    bias = jnp.where(seg_col[0] == seg_row[0], 0.0, NEGATIVE)
    heads = q.shape[1] // HD
    parts = []
    for h in range(heads):
        cols = slice(h * HD, (h + 1) * HD)
        s = dot_nt(q[:, cols], k[:, cols]) + bias
        top = jnp.max(s, axis=1, keepdims=True)
        e = jnp.exp2((s - top) * (LOG2E * HD**-0.5))
        low = e.astype(LOW)
        total = jnp.sum(e, axis=1, keepdims=True)
        inv = 1.0 / total
        e_out[0, h] = low
        inv_out[0, :, h : h + 1] = inv
        parts.append(dot_nn(low, v[:, cols]) * inv)
    mixed = jnp.concatenate(parts, axis=1).astype(LOW)
    mix_own[0] = mixed[:half]
    mix_sib[0] = mixed[half:]


def attend(c, own, sib, seg_row, seg_col, wq, wk, wv, bq, bv):
    rows, half, width = own.shape
    length = 2 * half
    cols = width // 2
    heads = cols // HD
    row3 = lambda shape: pl.BlockSpec((1,) + shape, lambda r, w: (r, 0, 0))
    weight = pl.BlockSpec((width, cols), lambda r, w: (0, w[0]))
    bias = pl.BlockSpec((1, cols), lambda r, w: (0, w[0]))
    sds = jax.ShapeDtypeStruct
    return pl.pallas_call(
        attend_kernel,
        grid_spec=pltpu.PrefetchScalarGridSpec(
            num_scalar_prefetch=1,
            grid=(rows,),
            in_specs=[
                row3((half, width)), row3((half, width)), row3((1, length)), row3((length, 1)),
                weight, weight, weight, bias, bias,
            ],
            out_specs=[
                row3((length, cols)), row3((length, cols)), row3((length, cols)),
                pl.BlockSpec((1, heads, length, length), lambda r, w: (r, 0, 0, 0)),
                row3((length, heads)), row3((half, cols)), row3((half, cols)),
            ],
        ),
        out_shape=[
            sds((rows, length, cols), LOW), sds((rows, length, cols), LOW),
            sds((rows, length, cols), LOW), sds((rows, heads, length, length), LOW),
            sds((rows, length, heads), F32), sds((rows, half, cols), LOW),
            sds((rows, half, cols), LOW),
        ],
        compiler_params=params(56),
        name="attend",
    )(c, own, sib, seg_row, seg_col, wq, wk, wv, bq, bv)


def norm_parts(v):
    center = v - jnp.mean(v, axis=1, keepdims=True)
    spread = jnp.mean(center * center, axis=1, keepdims=True)
    scale = lax.rsqrt(spread + EPSILON)
    return center * scale, scale


def norm_back(dn, n, scale):
    return scale * (
        dn - jnp.mean(dn, axis=1, keepdims=True) - n * jnp.mean(dn * n, axis=1, keepdims=True)
    )


def gelu_parts(v):
    phi_core = jnp.exp2(v * v * (-0.5 * LOG2E))
    t = 1.0 / (1.0 + (0.3275911 * 0.7071067811865476) * jnp.abs(v))
    poly = t * (
        0.5 * 0.254829592
        + t * (-0.5 * 0.284496736 + t * (0.5 * 1.421413741 + t * (-0.5 * 1.453152027 + t * (0.5 * 1.061405429))))
    )
    tail = poly * phi_core
    big = jnp.where(v >= 0, 1.0 - tail, tail)
    return v * big, big + v * (phi_core * 0.3989422804014327)


def col_sum(v):
    return jnp.sum(v, axis=0, keepdims=True)


def middle_kernel(
    where, own, mix_own, mix_sib, cot, wo_own, wo_sib, w1, w2, bo, ag, ash, b1, b2, fg, fsh,
    out, act, dinner, firstT, douterT, dattn, dbranch, dmix_own, dmix_sib,
    v_ob, v_b1, v_b2, v_ag, v_as, v_fg, v_fs,
    slope,
):
    i = pl.program_id(0)
    x = own[0].astype(F32)
    branch = dot_nn(mix_own[0], wo_own[...]) + dot_nn(mix_sib[0], wo_sib[...])
    n1, s1 = norm_parts(x + (branch + bo[...].astype(F32)))
    first = n1 * ag[...].astype(F32) + ash[...].astype(F32)
    first_low = first.astype(LOW)
    firstT[...] = first_low.T
    second = first + b2[...].astype(F32)
    hidden = w1.shape[1]
    step = 512
    for j in range(0, hidden, step):
        cols = slice(j, j + step)
        inner = dot_nn(first_low, w1[:, cols]) + b1[:, cols].astype(F32)
        a, d = gelu_parts(inner)
        a_low = a.astype(LOW)
        act[0, :, cols] = a_low
        slope[:, cols] = d
        second = second + dot_nn(a_low, w2[cols, :])
    n2, s2 = norm_parts(second)
    gain = fg[...].astype(F32)
    out[0] = (n2 * gain + fsh[...].astype(F32)).astype(LOW)
    g = cot[0].astype(F32)
    d_second = norm_back(g * gain, n2, s2)
    d_outer = d_second.astype(LOW)
    douterT[...] = d_outer.T
    sums = {}
    sums[0] = (v_fg, col_sum(g * n2))
    sums[1] = (v_fs, col_sum(g))
    sums[2] = (v_b2, col_sum(d_outer.astype(F32)))
    d_first = d_second
    parts = []
    for j in range(0, hidden, step):
        cols = slice(j, j + step)
        di = (dot_nt(d_outer, w2[cols, :]) * slope[:, cols]).astype(LOW)
        dinner[0, :, cols] = di
        parts.append(col_sum(di.astype(F32)))
        d_first = d_first + dot_nt(di, w1[:, cols])
    sums[3] = (v_b1, jnp.concatenate(parts, axis=1))
    sums[4] = (v_ag, col_sum(d_first * n1))
    sums[5] = (v_as, col_sum(d_first))
    d_attn = norm_back(d_first * ag[...].astype(F32), n1, s1)
    dattn[0] = d_attn
    d_branch = d_attn.astype(LOW)
    dbranch[0] = d_branch
    sums[6] = (v_ob, col_sum(d_branch.astype(F32)))
    dmix_own[0] = dot_nt(d_branch, wo_own[...]).astype(LOW)
    dmix_sib[0] = dot_nt(d_branch, wo_sib[...]).astype(LOW)

    @pl.when(i == 0)
    def _():
        for ref, value in sums.values():
            ref[...] = value

    @pl.when(i > 0)
    def _():
        for ref, value in sums.values():
            ref[...] += value


def middle(c, own, mix_own, mix_sib, cot, wo, w1, w2, bo, ag, ash, b1, b2, fg, fsh):
    rows, half, width = own.shape
    hidden = w1.shape[1]
    cols = width // 2
    row3 = lambda n: pl.BlockSpec((1, half, n), lambda r, w: (r, 0, 0))
    one = pl.Buffered(1)
    fixed = lambda *s: pl.BlockSpec(s, lambda r, w: (0,) * len(s), pipeline_mode=one)
    tr = pl.BlockSpec((width, half), lambda r, w: (0, r))
    vec = lambda n: pl.BlockSpec((1, n), lambda r, w: (0, 0))
    sds = jax.ShapeDtypeStruct
    tokens = rows * half
    return pl.pallas_call(
        middle_kernel,
        grid_spec=pltpu.PrefetchScalarGridSpec(
            num_scalar_prefetch=1,
            grid=(rows,),
            in_specs=[
                row3(width), row3(cols), row3(cols), row3(width),
                pl.BlockSpec((cols, width), lambda r, w: (w[0], 0), pipeline_mode=one),
                pl.BlockSpec((cols, width), lambda r, w: (1 - w[0], 0), pipeline_mode=one),
                fixed(width, hidden), fixed(hidden, width),
                vec(width), vec(width), vec(width), vec(hidden), vec(width), vec(width), vec(width),
            ],
            out_specs=[
                row3(width), row3(hidden), row3(hidden), tr, tr, row3(width), row3(width),
                row3(cols), row3(cols),
                vec(width), vec(hidden), vec(width), vec(width), vec(width), vec(width), vec(width),
            ],
            scratch_shapes=[pltpu.VMEM((half, hidden), F32)],
        ),
        out_shape=[
            sds((rows, half, width), LOW), sds((rows, half, hidden), LOW),
            sds((rows, half, hidden), LOW), sds((width, tokens), LOW), sds((width, tokens), LOW),
            sds((rows, half, width), F32), sds((rows, half, width), LOW),
            sds((rows, half, cols), LOW), sds((rows, half, cols), LOW),
            sds((1, width), F32), sds((1, hidden), F32), sds((1, width), F32),
            sds((1, width), F32), sds((1, width), F32), sds((1, width), F32), sds((1, width), F32),
        ],
        compiler_params=params(60),
        name="middle",
    )(c, own, mix_own, mix_sib, cot, wo, wo, w1, w2, bo, ag, ash, b1, b2, fg, fsh)


def attend_back_kernel(
    where, own, sib, q_ref, k_ref, v_ref, e_ref, inv_ref, mix_own, mix_sib, dm_own, dm_sib,
    wq, wk, wv,
    in_own, in_sib, gq, gk, gv, v_qb, v_vb,
    aq, ak, av,
):
    i = pl.program_id(0)
    half = own.shape[1]
    scale = HD**-0.5
    q, k, v = q_ref[0], k_ref[0], v_ref[0]
    mixed = jnp.concatenate([mix_own[0], mix_sib[0]], axis=0)
    dm = jnp.concatenate([dm_own[0], dm_sib[0]], axis=0)
    heads = q.shape[1] // HD
    dq, dk, dv = [], [], []
    for h in range(heads):
        cols = slice(h * HD, (h + 1) * HD)
        inv = inv_ref[0, :, h : h + 1]
        d_out = dm[:, cols].astype(F32) * inv
        delta = jnp.sum(d_out * mixed[:, cols].astype(F32), axis=1, keepdims=True)
        d_low = d_out.astype(LOW)
        e = e_ref[0, h]
        dp = dot_nt(d_low, v[:, cols])
        ds = (e.astype(F32) * (dp - delta)).astype(LOW)
        dq.append(dot_nn(ds, k[:, cols]) * scale)
        dk.append(dot_tn(ds, q[:, cols]) * scale)
        dv.append(dot_tn(e, d_low))
    dq = jnp.concatenate(dq, axis=1).astype(LOW)
    dk = jnp.concatenate(dk, axis=1).astype(LOW)
    dv = jnp.concatenate(dv, axis=1).astype(LOW)
    back = dot_nt(dq, wq[...]) + dot_nt(dk, wk[...]) + dot_nt(dv, wv[...])
    in_own[0] = back[:half]
    in_sib[0] = back[half:].astype(LOW)
    x = jnp.concatenate([own[0], sib[0]], axis=0)
    tq, tk, tv = dot_tn(x, dq), dot_tn(x, dk), dot_tn(x, dv)
    sq, sv = col_sum(dq.astype(F32)), col_sum(dv.astype(F32))

    @pl.when(i == 0)
    def _():
        aq[...] = tq
        ak[...] = tk
        av[...] = tv
        v_qb[...] = sq
        v_vb[...] = sv

    @pl.when(i > 0)
    def _():
        aq[...] += tq
        ak[...] += tk
        av[...] += tv
        v_qb[...] += sq
        v_vb[...] += sv

    @pl.when(i == pl.num_programs(0) - 1)
    def _():
        shards, size = gq.shape[0], gq.shape[1]
        for s in range(shards):
            at = where[1 + s]
            part = slice(s * size, (s + 1) * size)
            gq[at] = aq[part].astype(LOW)
            gk[at] = ak[part].astype(LOW)
            gv[at] = av[part].astype(LOW)


def attend_back(where, shards, own, sib, q, k, v, e, inv, mix_own, mix_sib, dm_own, dm_sib, wq, wk, wv):
    rows, half, width = own.shape
    length = 2 * half
    cols = width // 2
    heads = cols // HD
    row3 = lambda a, n: pl.BlockSpec((1, a, n), lambda r, w: (r, 0, 0))
    weight = pl.BlockSpec((width, cols), lambda r, w: (0, w[0]))
    sds = jax.ShapeDtypeStruct
    size = width // shards
    grad = pl.BlockSpec((shards, size, cols), lambda r, w: (0, 0, 0))
    vec = pl.BlockSpec((1, cols), lambda r, w: (0, 0))
    return pl.pallas_call(
        attend_back_kernel,
        grid_spec=pltpu.PrefetchScalarGridSpec(
            num_scalar_prefetch=1,
            grid=(rows,),
            in_specs=[
                row3(half, width), row3(half, width),
                row3(length, cols), row3(length, cols), row3(length, cols),
                pl.BlockSpec((1, heads, length, length), lambda r, w: (r, 0, 0, 0)),
                row3(length, heads),
                row3(half, cols), row3(half, cols), row3(half, cols), row3(half, cols),
                weight, weight, weight,
            ],
            out_specs=[row3(half, width), row3(half, width), grad, grad, grad, vec, vec],
            scratch_shapes=[pltpu.VMEM((width, cols), F32)] * 3,
        ),
        out_shape=[
            sds((rows, half, width), F32), sds((rows, half, width), LOW),
            sds((shards, size, cols), LOW), sds((shards, size, cols), LOW),
            sds((shards, size, cols), LOW), sds((1, cols), F32), sds((1, cols), F32),
        ],
        compiler_params=params(60),
        name="attend_back",
    )(where, own, sib, q, k, v, e, inv, mix_own, mix_sib, dm_own, dm_sib, wq, wk, wv)


def rows_kernel(where, left, right, keep, send, *, base):
    h = pl.program_id(0)
    value = dot_nn(left[...], right[...])
    shards, size = keep.shape[0], keep.shape[1]

    def put(ref):
        for s in range(shards):
            ref[where[1 + s]] = value[s * size : (s + 1) * size].astype(LOW)

    pl.when(h == 1)(lambda: put(keep))
    pl.when(h == 0)(lambda: put(send))


def rows_grad(where, shards, left, right, tile):
    m, tokens = left.shape
    n = right.shape[1]
    half = n // 2
    tiles = half // tile
    size = m // shards
    sds = jax.ShapeDtypeStruct

    def right_at(h, j, w):
        return (0, jnp.where(h == 1, w[0], 1 - w[0]) * tiles + j)

    return pl.pallas_call(
        functools.partial(rows_kernel, base=0),
        grid_spec=pltpu.PrefetchScalarGridSpec(
            num_scalar_prefetch=1,
            grid=(2, tiles),
            in_specs=[
                pl.BlockSpec((m, tokens), lambda h, j, w: (0, 0)),
                pl.BlockSpec((tokens, tile), right_at),
            ],
            out_specs=[
                pl.BlockSpec((shards, size, tile), lambda h, j, w: (0, 0, jnp.where(h == 1, j, 0))),
                pl.BlockSpec((shards, size, tile), lambda h, j, w: (0, 0, jnp.where(h == 0, j, tiles - 1))),
            ],
        ),
        out_shape=[sds((shards, size, half), LOW)] * 2,
        compiler_params=params(48),
        name="rows_grad",
    )(where, left, right)


def cols_kernel(where, left, right, keep, send, *, group):
    h = pl.program_id(0)
    value = dot_nn(left[...], right[...]).astype(LOW)
    size = value.shape[1] // group
    j = pl.program_id(1)

    def put(ref):
        for g in range(group):
            ref[where[1 + j * group + g]] = value[:, g * size : (g + 1) * size]

    pl.when(h == 1)(lambda: put(keep))
    pl.when(h == 0)(lambda: put(send))


def cols_grad(where, shards, left, right):
    m, tokens = left.shape
    n = right.shape[1]
    half = m // 2
    size = n // shards
    group = 2 if shards % 2 == 0 else 1
    sds = jax.ShapeDtypeStruct
    whole = pl.BlockSpec((shards, half, size), lambda h, j, w: (0, 0, 0))
    return pl.pallas_call(
        functools.partial(cols_kernel, group=group),
        grid_spec=pltpu.PrefetchScalarGridSpec(
            num_scalar_prefetch=1,
            grid=(2, shards // group),
            in_specs=[
                pl.BlockSpec((half, tokens), lambda h, j, w: (jnp.where(h == 1, w[0], 1 - w[0]), 0)),
                pl.BlockSpec((tokens, group * size), lambda h, j, w: (0, j)),
            ],
            out_specs=[whole, whole],
        ),
        out_shape=[sds((shards, half, size), LOW)] * 2,
        compiler_params=params(48),
        name="cols_grad",
    )(where, left, right)


def flip_order(v, index, bits):
    rest = v.shape[1:]
    v = v.reshape((2,) * bits + rest)
    for axis in range(bits):
        bit = (index >> (bits - 1 - axis)) & 1
        v = jnp.where(bit == 1, jnp.flip(v, axis), v)
    order = tuple(range(bits))[::-1] + tuple(range(bits, bits + len(rest)))
    return jnp.transpose(v, order).reshape((2**bits,) + rest)


def swap(v, axis, mask, size):
    return lax.ppermute(v, axis, [(i, i ^ mask) for i in range(size)])


def add_low(*terms):
    total = terms[0].astype(F32)
    for t in terms[1:]:
        total = total + t.astype(F32)
    return total.astype(LOW)


def fix(v):
    return lax.optimization_barrier(v)


def solution(mesh):
    batch_size = mesh.shape["batch"]
    blk_size = mesh.shape["blk"]
    bits = batch_size.bit_length() - 1
    direct = batch_size == 2**bits and 768 % (16 * batch_size) == 0 and 3072 % (128 * batch_size) == 0
    shards = batch_size if direct else 1

    def blk_swap(v, mask):
        return swap(v, "blk", mask, blk_size)

    def reduce_batch(g):
        for k in range(bits):
            half = g.shape[0] // 2
            got = swap(g[half:], "batch", 1 << k, batch_size)
            g = fix(add_low(g[:half], got))
        return g[0]

    def reduce_y(g):
        return add_low(g, blk_swap(g, 2))

    def per_device(
        tokens, segment_ids, query_weight, query_bias, key_weight, value_weight, value_bias,
        output_weight, output_bias, attn_gain, attn_shift, inner_weight, inner_bias,
        outer_weight, outer_bias, final_gain, final_shift, cotangent,
    ):
        count, span, width = tokens.shape
        rows = count // 2
        me = lax.axis_index("blk")
        b = lax.axis_index("batch")
        core = me & 1
        y = (me >> 1) & 1
        if direct:
            rel = [b ^ s for s in range(shards)]
            places = [sum(((r >> k) & 1) << (bits - 1 - k) for k in range(bits)) for r in rel]
        else:
            places = [0]
        where = jnp.stack([core] + [jnp.asarray(p) for p in places]).astype(jnp.int32)

        def mine(v):
            return lax.dynamic_slice_in_dim(v, y * rows, rows, 0)

        def other(v):
            return lax.dynamic_slice_in_dim(v, (1 - y) * rows, rows, 0)

        def gather_rows(v):
            return jnp.concatenate([mine(v), blk_swap(other(v), 2)], axis=1)

        def return_rows(v):
            keep, got = v[:, :span], blk_swap(v[:, span:], 2)
            return jnp.where(
                y == 0, jnp.concatenate([keep, got], axis=0), jnp.concatenate([got, keep], axis=0)
            )

        def halves(mine_half, got, axis):
            return jnp.where(
                core == 0,
                jnp.concatenate([mine_half, got], axis=axis),
                jnp.concatenate([got, mine_half], axis=axis),
            )

        own = gather_rows(tokens)
        sib = blk_swap(own, 1)
        cot = gather_rows(cotangent)
        seg = mine(segment_ids).reshape(rows, 4, span)
        seg = jnp.concatenate(
            [lax.dynamic_index_in_dim(seg, me ^ r, 1, keepdims=False) for r in (0, 2, 1, 3)], axis=1
        )
        row = lambda v: v.reshape(1, -1)
        q, k, v, e, inv, mix_own, mix_out = attend(
            where, own, sib, seg[:, None, :], seg[:, :, None],
            query_weight, key_weight, value_weight, row(query_bias), row(value_bias),
        )
        mix_sib = blk_swap(mix_out, 1)
        (
            out, act, dinner, first_t, douter_t, dattn, dbranch, dm_own, dm_out,
            v_ob, v_b1, v_b2, v_ag, v_as, v_fg, v_fs,
        ) = middle(
            where, own, mix_own, mix_sib, cot, output_weight, inner_weight, outer_weight,
            row(output_bias), row(attn_gain), row(attn_shift), row(inner_bias), row(outer_bias),
            row(final_gain), row(final_shift),
        )
        result = return_rows(out)
        dm_sib = blk_swap(dm_out, 1)
        flat = lambda v: v.reshape(-1, v.shape[-1])
        outer_keep, outer_send = cols_grad(where, shards, douter_t, flat(act))
        inner_keep, inner_send = rows_grad(where, shards, first_t, flat(dinner), 512)
        mix_t = halves(flat(mix_own), flat(mix_sib), 1).T
        branch_keep, branch_send = rows_grad(where, shards, mix_t, flat(dbranch), 384)
        outer_part = add_low(outer_keep, blk_swap(outer_send, 1))
        inner_part = add_low(inner_keep, blk_swap(inner_send, 1))
        branch_part = add_low(branch_keep, blk_swap(branch_send, 1))
        in_own, in_out, gq, gk, gv, v_qb, v_vb = attend_back(
            where, shards, own, sib, q, k, v, e, inv, mix_own, mix_out, dm_own, dm_sib,
            query_weight, key_weight, value_weight,
        )
        in_grad = (dattn + in_own + blk_swap(in_out, 1).astype(F32)).astype(LOW)
        input_grad = return_rows(in_grad)

        half_cols = width // 2
        zero = jnp.zeros((1, half_cols), F32)

        def spread(v):
            return jnp.where(
                core == 0, jnp.concatenate([v, zero], axis=1), jnp.concatenate([zero, v], axis=1)
            )

        vectors = [spread(v_qb), spread(v_vb), v_ob, v_ag, v_as, v_b1, v_b2, v_fg, v_fs]
        packed = jnp.concatenate([v.reshape(batch_size, -1) for v in vectors], axis=1)
        extra = packed.shape[1]

        def join(v, axis):
            v = fix(v)
            return halves(v, blk_swap(v, 1), axis).astype(F32)

        if direct:
            size = width // shards
            lanes = half_cols
            extra_rows = -(-extra // lanes)
            padded = -(-extra_rows // 16) * 16
            packed = jnp.pad(packed, ((0, 0), (0, padded * lanes - extra))).astype(LOW)
            packed = flip_order(packed, b, bits).reshape(shards, padded, lanes)
            outer_done = reduce_y(reduce_batch(outer_part))
            inner_done = reduce_y(reduce_batch(inner_part))
            last = jnp.concatenate([gq, gk, gv, packed], axis=1)
            branch_done = reduce_y(reduce_batch(branch_part))
            last_done = reduce_y(reduce_batch(last))
            outer_grad = join(outer_done, 0).T
            inner_grad = join(inner_done, 1)
            output_grad = join(branch_done, 1)
            last_done = fix(last_done)
            last_got = blk_swap(last_done, 1)
            three = halves(last_done[: 3 * size], last_got[: 3 * size], 1).astype(F32)
            query_grad, key_grad, value_grad = three[:size], three[size : 2 * size], three[2 * size :]
            total = last_done[3 * size :].astype(F32) + last_got[3 * size :].astype(F32)
            total = total.reshape(-1)[:extra]
        else:
            def whole(v):
                return reduce_y(lax.psum_scatter(v, "batch", scatter_dimension=0, tiled=True))

            outer_grad = join(whole(outer_part[0].T), 1)
            inner_grad = join(whole(inner_part[0]), 1)
            output_grad = join(whole(branch_part[0]), 1)
            query_grad = join(whole(gq[0]), 1)
            key_grad = join(whole(gk[0]), 1)
            value_grad = join(whole(gv[0]), 1)
            total = lax.psum(lax.psum_scatter(packed, "batch", scatter_dimension=0, tiled=True), "blk")
            total = total.reshape(-1)
        sizes = [v.shape[1] // batch_size for v in vectors]
        pieces = []
        at = 0
        for n in sizes:
            pieces.append(total[at : at + n])
            at += n
        g_qb, g_vb, g_ob, g_ag, g_as, g_b1, g_b2, g_fg, g_fs = pieces
        return (
            result, input_grad, query_grad, g_qb, key_grad, value_grad, g_vb, output_grad, g_ob,
            g_ag, g_as, inner_grad, g_b1, outer_grad, g_b2, g_fg, g_fs,
        )

    tok = P("batch", "blk", None)
    mat = P("batch", None)
    vec = P("batch")
    return jax.shard_map(
        per_device,
        mesh=mesh,
        in_specs=(tok, P("batch", None)) + (P(),) * 15 + (tok,),
        out_specs=(
            tok, tok, mat, vec, mat, mat, vec, mat, vec, vec, vec, mat, vec, mat, vec, vec, vec,
        ),
        check_vma=False,
    )
```

```python
import functools

import jax
import jax.numpy as jnp
from jax import lax
from jax.experimental import pallas as pl
from jax.experimental.pallas import tpu as pltpu
from jax.sharding import PartitionSpec as P

HD = 64
EPSILON = 1e-12
NEGATIVE = -1e30
LOW = jnp.bfloat16
F32 = jnp.float32
LOG2E = 1.4426950408889634
MIB = 1024 * 1024
SDS = jax.ShapeDtypeStruct


def contract(a, b, left, right):
    return lax.dot_general(a, b, (((left,), (right,)), ((), ())), preferred_element_type=F32)


def call(kernel, where, inputs, after, *, grid, in_specs, out_specs, out_shape, us, name, scratch=(), reuse=()):
    count = len(inputs)
    extra = len(after) + len(reuse)

    def body(w, *refs):
        kernel(w, *refs[:count], *refs[count + extra :])

    return pl.pallas_call(
        body,
        grid_spec=pltpu.PrefetchScalarGridSpec(
            num_scalar_prefetch=1,
            grid=grid,
            in_specs=list(in_specs) + [pl.BlockSpec(memory_space=pl.ANY)] * extra,
            out_specs=list(out_specs),
            scratch_shapes=list(scratch),
        ),
        out_shape=list(out_shape),
        compiler_params=pltpu.CompilerParams(vmem_limit_bytes=60 * MIB),
        cost_estimate=pl.CostEstimate(flops=int(us * 1.1e9), bytes_accessed=0, transcendentals=0),
        input_output_aliases={1 + count + i: i for i in range(len(reuse))},
        name=name,
    )(where, *inputs, *reuse, *after)


def col_sum(v):
    return jnp.sum(v, axis=0, keepdims=True)


def as_column(v, rows):
    return jnp.broadcast_to(v[None, :], (rows, v.shape[0])).T


def attend_kernel(
    where, t0, t1, t2, t3, seg_row, seg_col, wq, wk, wv, bq, bv,
    q_out, k_out, v_out, e_out, inv_out, mix_own, mix_sib,
):
    x = jnp.concatenate([t0[0], t1[0], t2[0], t3[0]], axis=0)
    half = mix_own.shape[2]
    cols = mix_own.shape[1]
    core = where[0]
    own_part = lambda ref: jnp.where(core == 0, ref[:cols].astype(F32), ref[cols:].astype(F32))
    qb = as_column(own_part(bq), 128)[:, :1]
    vb = as_column(own_part(bv), 128)[:, :1]
    q = (contract(wq[...], x, 0, 1) + qb).astype(LOW)
    k = contract(wk[...], x, 0, 1).astype(LOW)
    v = (contract(wv[...], x, 0, 1) + vb).astype(LOW)
    q_out[0] = q
    k_out[0] = k
    v_out[0] = v
    bias = jnp.where(seg_col[0] == seg_row[0], 0.0, NEGATIVE)
    for h in range(q.shape[0] // HD):
        part = slice(h * HD, (h + 1) * HD)
        s = contract(k[part], q[part], 0, 0) + bias
        top = jnp.max(s, axis=0, keepdims=True)
        e = jnp.exp2((s - top) * (LOG2E * HD**-0.5))
        low = e.astype(LOW)
        inv = 1.0 / col_sum(e)
        e_out[0, h] = low
        inv_out[0, h : h + 1] = inv
        mixed = (contract(v[part], low, 1, 0) * inv).astype(LOW)
        mix_own[0, part] = mixed[:, :half]
        mix_sib[0, part] = mixed[:, half:]


def attend(where, toks, seg_row, seg_col, wq, wk, wv, bq, bv, after=()):
    rows, span, width = toks[0].shape
    length = 4 * span
    cols = width // 2
    heads = cols // HD
    row3 = lambda *s: pl.BlockSpec((1,) + s, lambda r, w: (r, 0, 0))
    weight = pl.BlockSpec((width, cols), lambda r, w: (0, w[0]))
    bias = pl.BlockSpec((width,), lambda r, w: (0,))
    return call(
        attend_kernel, where, (*toks, seg_row, seg_col, wq, wk, wv, bq, bv), after,
        grid=(rows,),
        in_specs=[row3(span, width)] * 4
        + [row3(1, length), row3(length, 1), weight, weight, weight, bias, bias],
        out_specs=[row3(cols, length)] * 3
        + [
            pl.BlockSpec((1, heads, length, length), lambda r, w: (r, 0, 0, 0)),
            row3(heads, length), row3(cols, length // 2), row3(cols, length // 2),
        ],
        out_shape=[SDS((rows, cols, length), LOW)] * 3
        + [
            SDS((rows, heads, length, length), LOW), SDS((rows, heads, length), F32),
            SDS((rows, cols, length // 2), LOW), SDS((rows, cols, length // 2), LOW),
        ],
        us=17,
        name="attend",
    )


def norm_parts(v):
    center = v - jnp.mean(v, axis=1, keepdims=True)
    spread = jnp.mean(center * center, axis=1, keepdims=True)
    scale = lax.rsqrt(spread + EPSILON)
    return center * scale, scale


def norm_back(dn, n, scale):
    return scale * (
        dn - jnp.mean(dn, axis=1, keepdims=True) - n * jnp.mean(dn * n, axis=1, keepdims=True)
    )


def fold(v):
    return jnp.sum(v.reshape(v.shape[0] // 8, 8, v.shape[1]), axis=0)


TALL = 128


class Puts:
    def __init__(self, sems):
        self.sems = sems
        self.copies = []

    def __call__(self, src, dst):
        copy = pltpu.make_async_copy(src, dst, self.sems.at[len(self.copies)])
        copy.start()
        self.copies.append(copy)

    def shard(self, where, base, s, src, row, rows, cols, dst):
        if dst.shape[1] == rows:
            at = pl.ds(pl.multiple_of(row, 16), rows)
            self(src.at[at, cols], dst.at[where[base + 2 * s]])
            return
        for k in range(2):
            at = pl.ds(pl.multiple_of(row + k * (rows // 2), 16), rows // 2)
            self(src.at[at, cols], dst.at[where[base + 2 * s + k]])

    def wait(self):
        for copy in self.copies:
            copy.wait()


def place(i, cells, span):
    per = span // TALL
    cell = i // per
    return cell // cells, cell % cells, pl.ds(pl.multiple_of((i % per) * TALL, TALL), TALL)


def forward_kernel(
    where, mix_own, mix_sib, bo, ag, ash, b1, b2, fg, fsh,
    x0_hbm, x1_hbm, c0_hbm, c1_hbm, wo_hbm, w1_hbm, w2_hbm,
    sums, out0, out1, slope_out, low_out, norm_out, scale_out, second_out, douter_out,
    keep0, send0, keep1, send1,
    wo, w1, w2, x, cot, result, act, slope, norm1, scale1, first_low, second, douter, bias1, partial,
    in_sem, out_sem, *, shards,
):
    core = where[0]
    rows, cells, span, width = x.shape
    block = cells * span
    half = width // 2
    hidden = w1.shape[1]
    chunks = 3
    step = hidden // chunks
    lines = rows * block // TALL
    vec = lambda ref: ref[...].astype(F32)[None, :]
    own_half = pl.ds(pl.multiple_of(core * half, half), half)
    sib_half = pl.ds(pl.multiple_of((1 - core) * half, half), half)
    loads = [
        pltpu.make_async_copy(wo_hbm, wo, in_sem.at[0]),
        pltpu.make_async_copy(x0_hbm, x.at[:, 0], in_sem.at[1]),
        pltpu.make_async_copy(x1_hbm, x.at[:, 1], in_sem.at[2]),
        pltpu.make_async_copy(c0_hbm, cot.at[:, 0], in_sem.at[3]),
        pltpu.make_async_copy(c1_hbm, cot.at[:, 1], in_sem.at[4]),
    ]
    for j in range(chunks):
        cols = slice(j * step, (j + 1) * step)
        loads.append(pltpu.make_async_copy(w1_hbm.at[:, cols], w1.at[:, cols], in_sem.at[5 + j]))
    loads.append(pltpu.make_async_copy(w2_hbm, w2, in_sem.at[5 + chunks]))
    for k in (0, 1, 2, 5, 6, 7, 8, 3, 4):
        loads[k].start()
    put = Puts(out_sem)
    bias1[...] = vec(b1)
    partial[...] = jnp.zeros_like(partial)
    loads[0].wait()
    for r in range(rows):
        at = slice(r * block, (r + 1) * block)
        second[at] = contract(mix_own[r], wo[own_half, :], 0, 0) + contract(mix_sib[r], wo[sib_half, :], 0, 0)
    loads[1].wait()
    loads[2].wait()

    def norm_first(i, _):
        at = pl.ds(pl.multiple_of(i * TALL, TALL), TALL)
        r, cell, line = place(i, cells, span)
        n1, s1 = norm_parts(x[r, cell, line].astype(F32) + (second[at] + vec(bo)))
        norm1[at] = n1
        scale1[at] = jnp.broadcast_to(s1, (TALL, 128))
        first = n1 * vec(ag) + vec(ash)
        first_low[at] = first.astype(LOW)
        second[at] = first + vec(b2)
        return 0

    lax.fori_loop(0, lines, norm_first, 0, unroll=lines)
    put(norm1, norm_out)
    put(scale1, scale_out)
    put(first_low, low_out)
    for j in range(chunks):
        cols = slice(j * step, (j + 1) * step)
        loads[5 + j].wait()
        inner = contract(first_low[...], w1[:, cols], 1, 0) + bias1[:, cols]
        big = 0.5 + 0.5 * lax.erf(inner * 0.7071067811865476)
        bell = jnp.exp2(inner * inner * (-0.5 * LOG2E)) * 0.3989422804014327
        act[:, cols] = (inner * big).astype(LOW)
        slope[:, cols] = (big + inner * bell).astype(LOW)
        put(slope.at[:, cols], slope_out.at[:, cols])
    loads[5 + chunks].wait()
    second[...] += contract(act[...], w2[...], 1, 0)
    loads[3].wait()
    loads[4].wait()

    def norm_second(i, _):
        at = pl.ds(pl.multiple_of(i * TALL, TALL), TALL)
        r, cell, line = place(i, cells, span)
        n2, s2 = norm_parts(second[at])
        result[r, cell, line] = (n2 * vec(fg) + vec(fsh)).astype(LOW)
        g = cot[r, cell, line].astype(F32)
        d_second = norm_back(g * vec(fg), n2, s2)
        second[at] = d_second
        d_outer = d_second.astype(LOW)
        douter[at] = d_outer
        partial[:, :width] += fold(d_outer.astype(F32))
        partial[:, width : 2 * width] += fold(g * n2)
        partial[:, 2 * width :] += fold(g)
        return 0

    lax.fori_loop(0, lines, norm_second, 0, unroll=lines)
    put(douter, douter_out)
    put(second, second_out)
    put(result.at[:, 0], out0)
    put(result.at[:, 1], out1)
    sums[...] = col_sum(partial[...])

    size = hidden // shards
    part = size // 4
    every = slice(0, width)
    for s in range(shards):
        for piece in range(8 // shards):
            high = hidden // 8
            at = slice(s * size + piece * high, s * size + (piece + 1) * high)
            w2[at, :] = contract(act[:, at], douter[...], 0, 0).astype(LOW)
        for k, (keep, send) in enumerate(((keep0, send0), (keep1, send1))):
            theirs = s * size + (1 - core) * (2 * part) + k * part
            mine = s * size + core * (2 * part) + k * part
            put.shard(where, 2 + 16 * k, s, w2, theirs, part, every, send)
            put.shard(where, 2 + 16 * k, s, w2, mine, part, every, keep)
    put.wait()


def entries(order, shards):
    if shards == 1:
        return 1
    return 2 * shards if order[-1] == "g" else shards


def forward(where, orders, shards, x0, x1, mix_own, mix_sib, c0, c1, wo, w1, w2, bo, ag, ash, b1, b2, fg, fsh, after=()):
    rows, span, width = x0.shape
    half = 2 * span
    hidden = w1.shape[1]
    tokens = rows * half
    whole = lambda v: pl.BlockSpec(v.shape, lambda i, w: (0,) * len(v.shape))
    anywhere = pl.BlockSpec(memory_space=pl.ANY)
    outs = [SDS((1, 3 * width), F32)]
    outs += [SDS((rows, span, width), LOW)] * 2 + [SDS((tokens, hidden), LOW), SDS((tokens, width), LOW)]
    outs += [SDS((tokens, width), F32), SDS((tokens, 128), F32), SDS((tokens, width), F32)]
    outs += [SDS((tokens, width), LOW)]
    for k in range(2):
        n = entries(orders[k], shards)
        outs += [SDS((n, hidden // 4 // n, width), LOW)] * 2
    small = (mix_own, mix_sib, bo, ag, ash, b1, b2, fg, fsh)
    low = lambda *s: pltpu.VMEM(s, LOW)
    wide = lambda *s: pltpu.VMEM(s, F32)
    return call(
        functools.partial(forward_kernel, shards=shards), where, small + (x0, x1, c0, c1, wo, w1, w2), after,
        grid=(1,),
        in_specs=[whole(v) for v in small] + [anywhere] * 7,
        out_specs=[whole(outs[0])] + [anywhere] * (len(outs) - 1),
        out_shape=outs,
        scratch=[
            low(width, width), low(width, hidden), low(hidden, width),
            low(rows, 2, span, width), low(rows, 2, span, width), low(rows, 2, span, width),
            low(tokens, hidden), low(tokens, hidden), wide(tokens, width), wide(tokens, 128),
            low(tokens, width), wide(tokens, width), low(tokens, width), wide(1, hidden), wide(8, 3 * width),
            pltpu.SemaphoreType.DMA((9,)), pltpu.SemaphoreType.DMA((10 + 8 * shards,)),
        ],
        us=27,
        name="forward",
    )


def inner_kernel(
    where, slope_hbm, low_hbm, douter_hbm, w2_hbm,
    sums, dinner_out, keep0, send0, keep1, send1,
    w2, grad, slope, dinner, first_low, douter, partial, in_sem, out_sem, *, shards,
):
    core = where[0]
    hidden, width = w2.shape
    chunks = 3
    step = hidden // chunks
    load_d = pltpu.make_async_copy(douter_hbm, douter, in_sem.at[0])
    load_d.start()
    load_j = []
    for j in range(chunks):
        cols = slice(j * step, (j + 1) * step)
        load_j.append(pltpu.make_async_copy(w2_hbm.at[cols, :], w2.at[cols, :], in_sem.at[1 + 2 * j]))
        load_j.append(pltpu.make_async_copy(slope_hbm.at[:, cols], slope.at[:, cols], in_sem.at[2 + 2 * j]))
        load_j[-2].start()
        load_j[-1].start()
    load_low = pltpu.make_async_copy(low_hbm, first_low, in_sem.at[7])
    load_low.start()
    put = Puts(out_sem)
    load_d.wait()
    for j in range(chunks):
        cols = slice(j * step, (j + 1) * step)
        load_j[2 * j].wait()
        load_j[2 * j + 1].wait()
        di = (contract(douter[...], w2[cols, :], 1, 1) * slope[:, cols].astype(F32)).astype(LOW)
        dinner[:, cols] = di
        partial[:, cols] = fold(di.astype(F32))
        put(dinner.at[:, cols], dinner_out.at[:, cols])
    sums[...] = col_sum(partial[...])
    load_low.wait()
    size = width // shards
    wide = hidden // 4
    for h in range(2):
        side = jnp.where(core == 0, 1 - h, h)
        for k in range(2):
            at = pl.ds(pl.multiple_of(side * (2 * wide) + k * wide, 128), wide)
            grad[:, at] = contract(first_low[...], dinner[:, at], 0, 0).astype(LOW)
            dst = ((send0, send1), (keep0, keep1))[h][k]
            for s in range(shards):
                put.shard(where, 2 + 16 * (2 + k), s, grad, s * size, size, at, dst)
    put.wait()


def inner_grad(where, orders, shards, slope, low_in, douter, w2, after=()):
    hidden, width = w2.shape
    tokens = douter.shape[0]
    whole = lambda v: pl.BlockSpec(v.shape, lambda i, w: (0,) * len(v.shape))
    anywhere = pl.BlockSpec(memory_space=pl.ANY)
    outs = [SDS((1, hidden), F32), SDS((tokens, hidden), LOW)]
    for k in (2, 3):
        n = entries(orders[k], shards)
        outs += [SDS((n, width // n, hidden // 4), LOW)] * 2
    low = lambda *s: pltpu.VMEM(s, LOW)
    return call(
        functools.partial(inner_kernel, shards=shards), where, (slope, low_in, douter, w2), after,
        grid=(1,),
        in_specs=[anywhere] * 4,
        out_specs=[whole(outs[0])] + [anywhere] * (len(outs) - 1),
        out_shape=outs,
        scratch=[
            low(hidden, width), low(width, hidden), low(tokens, hidden), low(tokens, hidden),
            low(tokens, width), low(tokens, width), pltpu.VMEM((8, hidden), F32),
            pltpu.SemaphoreType.DMA((8,)), pltpu.SemaphoreType.DMA((3 + 8 * shards,)),
        ],
        us=11,
        name="inner_grad",
    )


def branch_kernel(
    where, mix_own, mix_sib, ag, sums_outer, sums_inner, dinner_hbm, norm_hbm, scale_hbm, second_hbm,
    wo_hbm, w1_hbm,
    sums, dbranch_out, dm_own, dm_sib, o_keep, o_send,
    wo, w1, dm, dinner, norm1, scale1, second, dbranch, ograd, partial,
    in_sem, out_sem, *, shards,
):
    core = where[0]
    rows = mix_own.shape[0]
    block = mix_own.shape[2]
    width, hidden = w1.shape
    half = width // 2
    chunks = 3
    step = hidden // chunks
    lines = rows * block // TALL
    vec = lambda ref: ref[...].astype(F32)[None, :]
    own_half = pl.ds(pl.multiple_of(core * half, half), half)
    sib_half = pl.ds(pl.multiple_of((1 - core) * half, half), half)
    load_j = []
    for j in range(chunks):
        cols = slice(j * step, (j + 1) * step)
        load_j.append(pltpu.make_async_copy(dinner_hbm.at[:, cols], dinner.at[:, cols], in_sem.at[2 * j]))
        load_j.append(pltpu.make_async_copy(w1_hbm.at[:, cols], w1.at[:, cols], in_sem.at[1 + 2 * j]))
        load_j[-2].start()
        load_j[-1].start()
    pairs = ((second_hbm, second), (norm_hbm, norm1), (scale_hbm, scale1), (wo_hbm, wo))
    late = [pltpu.make_async_copy(src, dst, in_sem.at[6 + k]) for k, (src, dst) in enumerate(pairs)]
    for copy in late:
        copy.start()
    put = Puts(out_sem)
    partial[...] = jnp.zeros_like(partial)
    total = None
    for j in range(chunks):
        cols = slice(j * step, (j + 1) * step)
        load_j[2 * j].wait()
        load_j[2 * j + 1].wait()
        if j == chunks - 1:
            late[0].wait()
        value = contract(dinner[:, cols], w1[:, cols], 1, 1)
        total = value if total is None else total + value
    second[...] += total
    for copy in late[1:]:
        copy.wait()

    def norm_attn(i, _):
        at = pl.ds(pl.multiple_of(i * TALL, TALL), TALL)
        d_first = second[at]
        n1 = norm1[at]
        d_branch = norm_back(d_first * vec(ag), n1, scale1[at][:, :1]).astype(LOW)
        dbranch[at] = d_branch
        partial[:, :width] += fold(d_branch.astype(F32))
        partial[:, width : 2 * width] += fold(d_first * n1)
        partial[:, 2 * width : 3 * width] += fold(d_first)
        return 0

    lax.fori_loop(0, lines, norm_attn, 0, unroll=lines)
    put(dbranch, dbranch_out)
    for r in range(rows):
        at = slice(r * block, (r + 1) * block)
        dm[0, r] = contract(wo[own_half, :], dbranch[at], 1, 1).astype(LOW)
        dm[1, r] = contract(wo[sib_half, :], dbranch[at], 1, 1).astype(LOW)
    put(dm.at[1], dm_sib)
    put(dm.at[0], dm_own)
    sums[:, : 3 * width] = col_sum(partial[...])
    sums[:, 3 * width : 3 * width + hidden] = sums_inner[...]
    sums[:, 3 * width + hidden :] = sums_outer[...]
    size = width // shards
    for k, mix in enumerate((mix_own, mix_sib)):
        value = contract(mix[0], dbranch[:block], 1, 0)
        for r in range(1, rows):
            value += contract(mix[r], dbranch[r * block : (r + 1) * block], 1, 0)
        ograd[own_half if k == 0 else sib_half, :] = value.astype(LOW)
    for s in range(shards):
        put.shard(where, 2 + 16 * 4, s, ograd, s * size, size, sib_half, o_send)
        put.shard(where, 2 + 16 * 4, s, ograd, s * size, size, own_half, o_keep)
    put.wait()


def branch(
    where, orders, shards, mix_own, mix_sib, ag, sums_outer, sums_inner, dinner, norm, scale, second, wo, w1, after=()
):
    rows, cols, half = mix_own.shape
    width, hidden = w1.shape
    tokens = rows * half
    whole = lambda v: pl.BlockSpec(v.shape, lambda i, w: (0,) * len(v.shape))
    anywhere = pl.BlockSpec(memory_space=pl.ANY)
    outs = [SDS((1, 6 * width + hidden), F32), SDS((tokens, width), LOW)] + [SDS((rows, cols, half), LOW)] * 2
    n = entries(orders[4], shards)
    outs += [SDS((n, width // n, cols), LOW)] * 2
    small = (mix_own, mix_sib, ag, sums_outer, sums_inner)
    big = (dinner, norm, scale, second, wo, w1)
    low = lambda *s: pltpu.VMEM(s, LOW)
    wide = lambda *s: pltpu.VMEM(s, F32)
    return call(
        functools.partial(branch_kernel, shards=shards), where, small + big, after,
        grid=(1,),
        in_specs=[whole(v) for v in small] + [anywhere] * len(big),
        out_specs=[whole(outs[0])] + [anywhere] * (len(outs) - 1),
        out_shape=outs,
        scratch=[
            low(width, width), low(width, hidden), low(2, rows, cols, half), low(tokens, hidden),
            wide(tokens, width), wide(tokens, 128), wide(tokens, width), low(tokens, width),
            low(width, width), wide(8, 3 * width),
            pltpu.SemaphoreType.DMA((10,)), pltpu.SemaphoreType.DMA((3 + 4 * shards,)),
        ],
        us=13,
        name="branch",
    )


def attend_back_kernel(
    where, q_ref, k_ref, v_ref, e_ref, inv_ref, mix_own, mix_sib, dm_own, dm_sib,
    dq_out, dk_out, dv_out,
):
    scale = HD**-0.5
    j = pl.program_id(0)
    heads = q_ref.shape[1] // HD
    for h in range(heads):
        part = slice(h * HD, (h + 1) * HD)
        mixed = jnp.concatenate([mix_own[0, part], mix_sib[0, part]], axis=1)
        dm = jnp.concatenate([dm_own[0, part], dm_sib[0, part]], axis=1)
        d_out = dm.astype(F32) * inv_ref[0, pl.ds(j * heads + h, 1)]
        delta = col_sum(d_out * mixed.astype(F32))
        d_low = d_out.astype(LOW)
        e = e_ref[0, h]
        dp = contract(v_ref[0, part], d_low, 0, 0)
        ds = (e.astype(F32) * (dp - delta)).astype(LOW)
        dq_out[0, part] = (contract(k_ref[0, part], ds, 1, 0) * scale).astype(LOW)
        dk_out[0, part] = (contract(q_ref[0, part], ds, 1, 1) * scale).astype(LOW)
        dv_out[0, part] = contract(d_low, e, 1, 1).astype(LOW)


def attend_back(where, r, q, k, v, e, inv, mix_own, mix_sib, dm_own, dm_sib, reuse=(), after=()):
    rows, cols, length = q.shape
    heads = cols // HD
    step = 2
    tall = step * HD
    at = lambda j, w: (r, j, 0)
    big = pl.BlockSpec((1, tall, length), at)
    small = pl.BlockSpec((1, tall, length // 2), at)
    return call(
        attend_back_kernel, where, (q, k, v, e, inv, mix_own, mix_sib, dm_own, dm_sib), after,
        grid=(heads // step,),
        in_specs=[big] * 3
        + [
            pl.BlockSpec((1, step, length, length), lambda j, w: (r, j, 0, 0)),
            pl.BlockSpec((1, heads, length), lambda j, w: (r, 0, 0)),
        ]
        + [small] * 4,
        out_specs=[big] * 3,
        out_shape=[SDS((rows, cols, length), LOW)] * 3,
        us=6,
        reuse=reuse,
        name="attend_back",
    )


def weight_kernel(where, t0, t1, t2, t3, dq_ref, dk_ref, dv_ref, vectors, gq, gk, gv, aq, ak, av, bias, *, orders, shards):
    i = pl.program_id(0)
    core = where[0]
    width, cols = gk.shape
    size = width // shards
    x = jnp.concatenate([t0[0], t1[0], t2[0], t3[0]], axis=0)
    dq, dk, dv = dq_ref[0], dk_ref[0], dv_ref[0]
    tq, tk, tv = (contract(x, d, 0, 1) for d in (dq, dk, dv))
    ones = jnp.ones((8, x.shape[0]), LOW)
    tb = jnp.concatenate([contract(ones, dq, 1, 1), contract(ones, dv, 1, 1)], axis=1)

    @pl.when(i == 0)
    def _():
        aq[...] = tq
        ak[...] = tk
        av[...] = tv
        bias[...] = tb

    @pl.when(i > 0)
    def _():
        aq[...] += tq
        ak[...] += tk
        av[...] += tv
        bias[...] += tb

    def put(ref, acc, n):
        if shards == 1:
            ref[:width] = acc[...].astype(LOW)
            return
        cut = 2 if len(orders[n]) > 4 else 1
        high = size // cut
        for s in range(shards):
            for k in range(cut):
                start = pl.multiple_of(where[2 + 16 * n + 2 * s + k] * high, 16)
                row = s * size + k * high
                ref[pl.ds(start, high)] = acc[row : row + high].astype(LOW)

    @pl.when(i == pl.num_programs(0) - 1)
    def _():
        put(gq, aq, 5)
        put(gk, ak, 6)
        put(gv, av, 7)
        count = vectors.shape[1] // cols
        lines = [vectors[:, n * cols : (n + 1) * cols] for n in range(count)]
        for v in (bias[:1, :cols], bias[:1, cols:]):
            lines += [jnp.where(core == 0, v, 0.0), jnp.where(core == 1, v, 0.0)]
        lines.append(jnp.zeros((gq.shape[0] - width - len(lines), cols), F32))
        gq[width:] = jnp.concatenate(lines, axis=0).astype(LOW)


def weight_grads(where, orders, shards, toks, dq, dk, dv, vectors, after=()):
    rows, span, width = toks[0].shape
    cols, length = dq.shape[1:]
    extra = 32
    row3 = lambda *s: pl.BlockSpec((1,) + s, lambda r, w: (r, 0, 0))
    whole = lambda *s: pl.BlockSpec(s, lambda r, w: (0,) * len(s))
    return call(
        functools.partial(weight_kernel, orders=orders, shards=shards), where, (*toks, dq, dk, dv, vectors), after,
        grid=(rows,),
        in_specs=[row3(span, width)] * 4 + [row3(cols, length)] * 3 + [whole(*vectors.shape)],
        out_specs=[whole(width + extra, cols), whole(width, cols), whole(width, cols)],
        out_shape=[SDS((width + extra, cols), LOW), SDS((width, cols), LOW), SDS((width, cols), LOW)],
        scratch=[pltpu.VMEM((width, cols), F32)] * 3 + [pltpu.VMEM((8, 2 * cols), F32)],
        us=7,
        name="weight_grads",
    )


def input_kernel(where, dq, dk, dv, wq, wk, wv, own, sib):
    half = own.shape[1]
    back = contract(dq[0], wq[...], 0, 1)
    back = back + contract(dk[0], wk[...], 0, 1) + contract(dv[0], wv[...], 0, 1)
    own[0] = back[:half]
    sib[0] = back[half:].astype(LOW)


def input_part(where, dq, dk, dv, wq, wk, wv, after=()):
    rows, cols, length = dq.shape
    width = wq.shape[0]
    row3 = lambda *s: pl.BlockSpec((1,) + s, lambda r, w: (r, 0, 0))
    weight = pl.BlockSpec((width, cols), lambda r, w: (0, w[0]))
    half = length // 2
    return call(
        input_kernel, where, (dq, dk, dv, wq, wk, wv), after,
        grid=(rows,),
        in_specs=[row3(cols, length)] * 3 + [weight] * 3,
        out_specs=[row3(half, width)] * 2,
        out_shape=[SDS((rows, half, width), F32), SDS((rows, half, width), LOW)],
        us=5,
        name="input_part",
    )


def finish_kernel(where, mine, got, gq, gk, gv, *outs):
    core = where[0]
    b = where[1]
    size, width = gq.shape
    cols = width // 2
    for n, ref in enumerate((gq, gk, gv)):
        a = mine[n * size : (n + 1) * size].astype(F32)
        c = got[n * size : (n + 1) * size].astype(F32)
        ref[:, :cols] = jnp.where(core == 0, a, c)
        ref[:, cols:] = jnp.where(core == 0, c, a)
    total = mine[3 * size :].astype(F32) + got[3 * size :].astype(F32)
    row = 0
    for ref in outs:
        n = ref.shape[0]
        parts = n * (width // size) // cols
        line = jnp.concatenate([total[row + i : row + i + 1] for i in range(parts)], axis=1)
        row += parts
        picked = jnp.zeros((1, n), F32)
        for s in range(width // size):
            picked = jnp.where(b == s, line[:, s * n : (s + 1) * n], picked)
        ref[...] = picked[0]


def finish(where, mine, got, size, width, lengths):
    whole = lambda *s: pl.BlockSpec(s, lambda i, w: (0,) * len(s))
    return call(
        finish_kernel, where, (mine, got), (),
        grid=(1,),
        in_specs=[whole(*mine.shape)] * 2,
        out_specs=[whole(size, width)] * 3 + [whole(n) for n in lengths],
        out_shape=[SDS((size, width), F32)] * 3 + [SDS((n,), F32) for n in lengths],
        us=2,
        name="finish",
    )


def swap(v, axis, mask, size):
    return lax.ppermute(v, axis, [(i, i ^ mask) for i in range(size)])


def add_low(a, b):
    return (a.astype(F32) + b.astype(F32)).astype(LOW)


def fix(v):
    return lax.optimization_barrier(v)


ORDERS = ("1x2y", "y1x2g", "xy12g", "1xy2g", "x12y", "x12y", "1xy2g", "yx12g")
BITS = {"x": 0, "1": 1, "2": 2}


def solution(mesh):
    batch_size = mesh.shape["batch"]
    blk_size = mesh.shape["blk"]
    direct = batch_size == 8
    shards = batch_size if direct else 1

    def blk_swap(v, mask):
        return swap(v, "blk", mask, blk_size)

    def reduce_shards(g, order, y, tail=0):
        for place, step in enumerate(order):
            if step == "g":
                got = blk_swap(g, 2)
                return jnp.where(
                    y == 0, jnp.concatenate([g[0], got[0]], axis=0), jnp.concatenate([got[0], g[0]], axis=0)
                )
            if step == "y" and place == len(order) - 1:
                g = fix(add_low(g, blk_swap(g, 2)))
                return g if tail else g[0]
            n = g.shape[0] - tail
            half = n // 2
            send = g[half:]
            if step == "y":
                got = blk_swap(send, 2)
            else:
                got = swap(send, "batch", 1 << BITS[step], batch_size)
            new = add_low(g[:half], got[:half])
            if tail:
                new = jnp.concatenate([new, add_low(g[n:], got[half:])], axis=0)
            g = fix(new)

    def per_device(
        tokens, segment_ids, query_weight, query_bias, key_weight, value_weight, value_bias,
        output_weight, output_bias, attn_gain, attn_shift, inner_weight, inner_bias,
        outer_weight, outer_bias, final_gain, final_shift, cotangent,
    ):
        count, span, width = tokens.shape
        rows = count // 2
        me = lax.axis_index("blk")
        b = lax.axis_index("batch")
        core = me & 1
        y = (me >> 1) & 1

        index = jnp.arange(16, dtype=jnp.int32)
        moved = {k: ((index >> (1 + n)) ^ (b >> n)) & 1 for k, n in BITS.items()}
        moved["y"] = (index & 1) ^ y
        maps = []
        for order in ORDERS:
            steps = order[:-1]
            maps.append(sum(moved[k] << (len(steps) - 1 - i) for i, k in enumerate(steps)))
        if not direct:
            maps = [jnp.zeros_like(v) for v in maps]
        where = jnp.concatenate([jnp.stack([core, b]).astype(jnp.int32)] + maps)

        def mine(v):
            return lax.dynamic_slice_in_dim(v, y * rows, rows, 0)

        def other(v):
            return lax.dynamic_slice_in_dim(v, (1 - y) * rows, rows, 0)

        def halves(own, got, axis):
            return jnp.where(
                core == 0,
                jnp.concatenate([own, got], axis=axis),
                jnp.concatenate([got, own], axis=axis),
            )

        def return_rows(keep, send):
            got = blk_swap(send, 2)
            return jnp.where(
                y == 0, jnp.concatenate([keep, got], axis=0), jnp.concatenate([got, keep], axis=0)
            )

        t1 = blk_swap(other(tokens), 2)
        t0 = mine(tokens)
        t2 = blk_swap(t0, 1)
        t3 = blk_swap(t1, 1)
        toks = (t0, t1, t2, t3)
        c1 = blk_swap(other(cotangent), 2)
        c0 = mine(cotangent)
        seg = mine(segment_ids).reshape(rows, 4, span)
        seg = jnp.concatenate(
            [lax.dynamic_index_in_dim(seg, me ^ r, 1, keepdims=False) for r in (0, 2, 1, 3)], axis=1
        )
        q, k, v, e, inv, mix_own, mix_out = attend(
            where, toks, seg[:, None, :], seg[:, :, None],
            query_weight, key_weight, value_weight, query_bias, value_bias,
        )
        mix_sib = blk_swap(mix_out, 1)
        (
            sums_outer, out0, out1, slope, first_low, norm, scale, second, douter, ok0, os0, ok1, os1,
        ) = forward(
            where, ORDERS, shards, t0, t1, mix_own, mix_sib, c0, c1, output_weight, inner_weight, outer_weight,
            output_bias, attn_gain, attn_shift, inner_bias, outer_bias, final_gain, final_shift,
        )
        sums_inner, dinner, ik0, is0, ik1, is1 = inner_grad(
            where, ORDERS, shards, slope, first_low, douter, outer_weight
        )

        def over_cores(keep, send):
            return fix(add_low(keep, blk_swap(send, 1)))

        outer = [over_cores(ok0, os0), over_cores(ok1, os1)]
        vectors, dbranch, dm_own, dm_out, o_keep, o_send = branch(
            where, ORDERS, shards, mix_own, mix_sib, attn_gain, sums_outer, sums_inner, dinner, norm, scale,
            second, output_weight, inner_weight, after=tuple(outer),
        )
        dm_sib = blk_swap(dm_out, 1)
        inner = [over_cores(ik0, is0), over_cores(ik1, is1)]
        result = return_rows(out0, out1)
        args = (q, k, v, e, inv, mix_own, mix_out, dm_own, dm_sib)
        grads = attend_back(where, 0, *args, after=tuple(inner))
        o_part = over_cores(o_keep, o_send)
        grads = attend_back(where, 1, *args, reuse=grads, after=(o_part,))
        grads = attend_back(where, 2, *args, reuse=grads)
        gq, gk, gv = weight_grads(where, ORDERS, shards, toks, *grads, vectors)
        in_own, in_out = input_part(where, *grads, query_weight, key_weight, value_weight, after=(gq,))
        in_grad = dbranch.reshape(in_own.shape).astype(F32) + in_own + blk_swap(in_out, 1).astype(F32)
        in_grad = in_grad.astype(LOW)
        input_grad = return_rows(in_grad[:, :span], in_grad[:, span:])

        def join(v, axis):
            v = fix(v)
            return halves(v, blk_swap(v, 1), axis).astype(F32)

        def add_y(g):
            return fix(add_low(g, blk_swap(g, 2)))

        if direct:
            size = width // shards
            tail = gq.shape[0] - gk.shape[0]
            cut = lambda g, n: g.reshape(entries(ORDERS[n], shards), -1, g.shape[1])
            outer = [reduce_shards(g, ORDERS[n], y) for n, g in enumerate(outer)]
            inner = [reduce_shards(g, ORDERS[2 + n], y) for n, g in enumerate(inner)]
            o_part = reduce_shards(o_part, ORDERS[4], y)
            gq = reduce_shards(gq, ORDERS[5], y, tail)
            gk = reduce_shards(cut(gk, 6), ORDERS[6], y)
            gv = reduce_shards(cut(gv, 7), ORDERS[7], y)
            outer_done = join(jnp.concatenate(outer, axis=0), 0)
            inner_done = join(jnp.concatenate(inner, axis=1), 1)
            output_done = join(o_part, 1)
            final = fix(jnp.concatenate([gq[:size], gk, gv, gq[size:]], axis=0))
            lengths = [n // shards for n in (width,) * 3 + (inner_weight.shape[1],) + (width,) * 5]
            query_done, key_done, value_done, *vecs = finish(
                where, final, blk_swap(final, 1), size, width, lengths
            )
        else:

            def whole(v):
                return add_y(lax.psum_scatter(v, "batch", scatter_dimension=0, tiled=True))

            outer_part = jnp.concatenate([outer[0][0], outer[1][0]], axis=0)
            outer_done = whole(halves(outer_part, blk_swap(outer_part, 1), 0)).astype(F32)
            inner_done = join(whole(jnp.concatenate([inner[0][0], inner[1][0]], axis=1)), 1)
            output_done = join(whole(o_part[0]), 1)
            total = lax.psum(gq[width:].astype(F32), ("batch", "blk")).reshape(-1)
            query_done, key_done, value_done = (join(whole(g[:width]), 1) for g in (gq, gk, gv))
            vecs = []
            at = 0
            for n in (width,) * 3 + (inner_weight.shape[1],) + (width,) * 5:
                part = total[at : at + n].reshape(batch_size, n // batch_size)
                vecs.append(lax.dynamic_index_in_dim(part, b, 0, keepdims=False))
                at += n
        g_ob, g_ag, g_as, g_b1, g_b2, g_fg, g_fs, g_qb, g_vb = vecs
        return (
            result, input_grad, query_done, g_qb, key_done, value_done, g_vb, output_done, g_ob,
            g_ag, g_as, inner_done, g_b1, outer_done, g_b2, g_fg, g_fs,
        )

    tok = P("batch", "blk", None)
    mat = P("batch", None)
    vec = P("batch")
    return jax.shard_map(
        per_device,
        mesh=mesh,
        in_specs=(tok, P("batch", None)) + (P(),) * 15 + (tok,),
        out_specs=(
            tok, tok, mat, vec, mat, mat, vec, mat, vec, vec, vec, mat, vec, mat, vec, vec, vec,
        ),
        check_vma=False,
    )
```

```python
import functools

import jax
import jax.numpy as jnp
from jax import lax
from jax.experimental import pallas as pl
from jax.experimental.pallas import tpu as pltpu
from jax.sharding import PartitionSpec as P

HD = 64
EPSILON = 1e-12
NEGATIVE = -1e30
LOW = jnp.bfloat16
F32 = jnp.float32
LOG2E = 1.4426950408889634
MIB = 1024 * 1024
COST = 5e7
SDS = jax.ShapeDtypeStruct


def contract(a, b, left, right):
    return lax.dot_general(a, b, (((left,), (right,)), ((), ())), preferred_element_type=F32)


def call(kernel, where, inputs, after, thread=None, *, grid, in_specs, out_specs, out_shape, us, name, scratch=(), mib=63):
    plain = thread is None
    thread = thread or ()
    count = len(inputs)
    extra = len(after) + len(thread)
    outs = len(out_shape)
    anywhere = pl.BlockSpec(memory_space=pl.ANY)

    def body(w, *refs):
        at = count + extra
        kernel(w, *refs[:count], *refs[at : at + outs], *refs[at + outs + len(thread) :])

    got = pl.pallas_call(
        body,
        grid_spec=pltpu.PrefetchScalarGridSpec(
            num_scalar_prefetch=1,
            grid=grid,
            in_specs=list(in_specs) + [anywhere] * extra,
            out_specs=list(out_specs) + [anywhere] * len(thread),
            scratch_shapes=list(scratch),
        ),
        out_shape=list(out_shape) + [SDS(v.shape, v.dtype) for v in thread],
        compiler_params=pltpu.CompilerParams(vmem_limit_bytes=mib * MIB),
        cost_estimate=pl.CostEstimate(flops=int(us * COST), bytes_accessed=0, transcendentals=0),
        input_output_aliases={1 + count + i: outs + i for i in range(len(thread))},
        name=name,
    )(where, *inputs, *thread, *after)
    return got if plain else (got[:outs], tuple(got[outs:]))


def gate(where, thread, after):
    return call(
        lambda where: None, where, (), after, thread, grid=(1,), in_specs=[], out_specs=[], out_shape=[], us=0.1,
        name="gate", mib=16,
    )[1]


def col_sum(v):
    return jnp.sum(v, axis=0, keepdims=True)


def as_column(v, rows):
    return jnp.broadcast_to(v[None, :], (rows, v.shape[0])).T


def attend_kernel(
    where, t0, t1, t2, t3, seg_ref, wq, wk, wv, bq, bv,
    x_out, q_out, k_out, v_out, e_out, inv_out, mix_own, mix_sib, bias,
):
    j = lax.rem(pl.program_id(0), 3)
    cols = q_out.shape[1]
    half = mix_own.shape[2]
    heads = e_out.shape[1]

    @pl.when(j == 0)
    def _():
        core = where[0]
        x = jnp.concatenate([t0[0], t1[0], t2[0], t3[0]], axis=0)
        x_out[0] = x
        own_part = lambda ref: jnp.where(core == 0, ref[:cols].astype(F32), ref[cols:].astype(F32))
        qb = as_column(own_part(bq), 128)[:, :1]
        vb = as_column(own_part(bv), 128)[:, :1]
        q_out[0] = (contract(wq[...], x, 0, 1) + qb).astype(LOW)
        k_out[0] = contract(wk[...], x, 0, 1).astype(LOW)
        v_out[0] = (contract(wv[...], x, 0, 1) + vb).astype(LOW)
        me, row = where[2], where[3] + lax.div(pl.program_id(0), 3)
        span = t0.shape[1]
        line = seg_ref[pl.ds(row, 1), :]
        here = [jnp.bitwise_xor(me, r) for r in (0, 2, 1, 3)]
        parts = [line[:, n * span : (n + 1) * span] for n in range(4)]
        pick = lambda q: sum(jnp.where(q == n, part, 0) for n, part in enumerate(parts))
        seg_row = jnp.concatenate([pick(q) for q in here], axis=1).astype(F32)
        seg_col = jnp.broadcast_to(seg_row, (128, seg_row.shape[1])).T[:, :1]
        bias[...] = jnp.where(seg_col == seg_row, 0.0, NEGATIVE)

    for h in range(heads):
        part = pl.ds(pl.multiple_of((j * heads + h) * HD, HD), HD)
        s = contract(k_out[0, part], q_out[0, part], 0, 0) + bias[...]
        top = jnp.max(s, axis=0, keepdims=True)
        e = jnp.exp2((s - top) * (LOG2E * HD**-0.5))
        low = e.astype(LOW)
        inv = 1.0 / col_sum(e)
        e_out[0, h] = low
        inv_out[0, h : h + 1] = inv
        mixed = (contract(v_out[0, part], low, 1, 0) * inv).astype(LOW)
        mix_own[0, h * HD : (h + 1) * HD] = mixed[:, :half]
        mix_sib[0, h * HD : (h + 1) * HD] = mixed[:, half:]


def attend(where, toks, segments, wq, wk, wv, bq, bv, after=()):
    rows, span, width = toks[0].shape
    length = 4 * span
    cols = width // 2
    heads = cols // HD
    step = 2
    tall = step * HD
    row3 = lambda *s: pl.BlockSpec((1,) + s, lambda t, w: (t // 3,) + (0,) * len(s))
    weight = pl.BlockSpec((width, cols), lambda t, w: (0, w[0]), pipeline_mode=pl.Buffered(1))
    bias = pl.BlockSpec((width,), lambda t, w: (0,))
    mix = pl.BlockSpec((1, tall, length // 2), lambda t, w: (t // 3, t % 3, 0))
    return call(
        attend_kernel, where, (*toks, segments, wq, wk, wv, bq, bv), after,
        grid=(3 * rows,),
        in_specs=[row3(span, width)] * 4
        + [pl.BlockSpec(segments.shape, lambda t, w: (0, 0)), weight, weight, weight, bias, bias],
        out_specs=[row3(length, width)]
        + [row3(cols, length)] * 3
        + [
            pl.BlockSpec((1, step, length, length), lambda t, w: (t // 3, t % 3, 0, 0)),
            pl.BlockSpec((1, 8, length), lambda t, w: (t // 3, t % 3, 0)), mix, mix,
        ],
        out_shape=[SDS((rows, length, width), LOW)]
        + [SDS((rows, cols, length), LOW)] * 3
        + [SDS((rows, heads, length, length), LOW), SDS((rows, 24, length), F32)]
        + [SDS((rows, cols, length // 2), LOW)] * 2,
        scratch=[pltpu.VMEM((length, length), F32)],
        us=18,
        name="attend",
    )


def norm_parts(v):
    center = v - jnp.mean(v, axis=1, keepdims=True)
    spread = jnp.mean(center * center, axis=1, keepdims=True)
    scale = lax.rsqrt(spread + EPSILON)
    return center * scale, scale


def norm_back(dn, n, scale):
    return scale * (
        dn - jnp.mean(dn, axis=1, keepdims=True) - n * jnp.mean(dn * n, axis=1, keepdims=True)
    )


def fold(v):
    return jnp.sum(v.reshape(v.shape[0] // 8, 8, v.shape[1]), axis=0)


TALL = 128
HEAD = 4
TAIL = 32


class Puts:
    def __init__(self, sems):
        self.sems = sems
        self.copies = []

    def __call__(self, src, dst):
        copy = pltpu.make_async_copy(src, dst, self.sems.at[len(self.copies)])
        copy.start()
        self.copies.append(copy)

    def shard(self, where, base, s, src, row, rows, cols, dst):
        if dst.shape[1] == rows:
            at = pl.ds(pl.multiple_of(row, 16), rows)
            self(src.at[at, cols], dst.at[where[base + 2 * s]])
            return
        for k in range(2):
            at = pl.ds(pl.multiple_of(row + k * (rows // 2), 16), rows // 2)
            self(src.at[at, cols], dst.at[where[base + 2 * s + k]])

    def wait(self):
        for copy in self.copies:
            copy.wait()


def place(i, block):
    per = block // TALL
    return i // per, pl.ds(pl.multiple_of((i % per) * TALL, TALL), TALL)


def forward_kernel(
    where, mix_own, mix_sib, bo, ag, ash, b1, b2, fg, fsh,
    x_hbm, c0_hbm, c1_hbm, wo_hbm, w1_hbm, w2_hbm,
    sums, out0, out1, dinner_out, norm_out, scale_out, second_out, keep, send, inner_keep, inner_send,
    wo, w1, w2, x, cot, result, act, slope, dinner, norm1, scale1, first_low, second, douter, bias1, partial,
    in_sem, out_sem, *, shards,
):
    core = where[0]
    rows, block, width = x.shape
    span = block // 2
    half = width // 2
    hidden = w1.shape[1]
    chunks = 3
    step = hidden // chunks
    lines = rows * block // TALL
    vec = lambda ref: ref[...].astype(F32)[None, :]
    own_half = pl.ds(pl.multiple_of(core * half, half), half)
    sib_half = pl.ds(pl.multiple_of((1 - core) * half, half), half)
    loads = [
        pltpu.make_async_copy(wo_hbm, wo, in_sem.at[0]),
        pltpu.make_async_copy(x_hbm.at[:, :block], x, in_sem.at[1]),
        pltpu.make_async_copy(c0_hbm, cot.at[:, :span], in_sem.at[2]),
        pltpu.make_async_copy(c1_hbm, cot.at[:, span:], in_sem.at[3]),
    ]
    for j in range(chunks):
        cols = slice(j * step, (j + 1) * step)
        loads.append(pltpu.make_async_copy(w1_hbm.at[:, cols], w1.at[:, cols], in_sem.at[4 + j]))
    loads.append(pltpu.make_async_copy(w2_hbm, w2, in_sem.at[4 + chunks]))
    for k in (0, 1, 4, 5, 6, 7, 2, 3):
        loads[k].start()
    put = Puts(out_sem)
    bias1[...] = vec(b1)
    partial[...] = jnp.zeros_like(partial)
    loads[0].wait()
    for r in range(rows):
        at = slice(r * block, (r + 1) * block)
        second[at] = contract(mix_own[r], wo[own_half, :], 0, 0) + contract(mix_sib[r], wo[sib_half, :], 0, 0)
    loads[1].wait()

    def norm_first(i, _):
        at = pl.ds(pl.multiple_of(i * TALL, TALL), TALL)
        r, line = place(i, block)
        n1, s1 = norm_parts(x[r, line].astype(F32) + (second[at] + vec(bo)))
        norm1[at] = n1
        scale1[at] = jnp.broadcast_to(s1, (TALL, 128))
        first = n1 * vec(ag) + vec(ash)
        first_low[at] = first.astype(LOW)
        second[at] = first + vec(b2)
        return 0

    lax.fori_loop(0, lines, norm_first, 0, unroll=lines)
    put(norm1, norm_out)
    put(scale1, scale_out)
    for j in range(chunks):
        cols = slice(j * step, (j + 1) * step)
        loads[4 + j].wait()
        inner = contract(first_low[...], w1[:, cols], 1, 0) + bias1[:, cols]
        big = 0.5 + 0.5 * lax.erf(inner * 0.7071067811865476)
        bell = jnp.exp2(inner * inner * (-0.5 * LOG2E)) * 0.3989422804014327
        act[:, cols] = (inner * big).astype(LOW)
        slope[:, cols] = (big + inner * bell).astype(LOW)
    loads[4 + chunks].wait()
    second[...] += contract(act[...], w2[...], 1, 0)
    loads[2].wait()
    loads[3].wait()

    def norm_second(i, _):
        at = pl.ds(pl.multiple_of(i * TALL, TALL), TALL)
        r, line = place(i, block)
        n2, s2 = norm_parts(second[at])
        result[r, line] = (n2 * vec(fg) + vec(fsh)).astype(LOW)
        g = cot[r, line].astype(F32)
        d_second = norm_back(g * vec(fg), n2, s2)
        second[at] = d_second
        d_outer = d_second.astype(LOW)
        douter[at] = d_outer
        partial[:, hidden : hidden + width] += fold(d_outer.astype(F32))
        partial[:, hidden + width : hidden + 2 * width] += fold(g * n2)
        partial[:, hidden + 2 * width :] += fold(g)
        return 0

    lax.fori_loop(0, lines, norm_second, 0, unroll=lines)
    put(second, second_out)
    put(result.at[:, :span], out0)
    put(result.at[:, span:], out1)

    for j in range(chunks):
        cols = slice(j * step, (j + 1) * step)
        di = (contract(douter[...], w2[cols, :], 1, 1) * slope[:, cols].astype(F32)).astype(LOW)
        dinner[:, cols] = di
        partial[:, cols] = fold(di.astype(F32))
        put(dinner.at[:, cols], dinner_out.at[:, cols])
    sums[...] = col_sum(partial[...])

    size = hidden // shards
    part = size // 2
    every = slice(0, width)
    for s in range(shards):
        for piece in range(8 // shards):
            high = hidden // 8
            at = slice(s * size + piece * high, s * size + (piece + 1) * high)
            w2[at, :] = contract(act[:, at], douter[...], 0, 0).astype(LOW)
        put.shard(where, HEAD, s, w2, s * size + (1 - core) * part, part, every, send)
        put.shard(where, HEAD, s, w2, s * size + core * part, part, every, keep)
    wide = hidden // 2
    size = width // shards
    for h in range(2):
        side = jnp.where(core == 0, 1 - h, h)
        at = pl.ds(pl.multiple_of(side * wide, 128), wide)
        w1[:, at] = contract(first_low[...], dinner[:, at], 0, 0).astype(LOW)
        dst = (inner_send, inner_keep)[h]
        pieces = dst.shape[0] // shards
        high = size // pieces
        for s in range(shards):
            for k in range(pieces):
                for n in range(2):
                    cols = pl.ds(pl.multiple_of(side * wide + n * width, 128), width)
                    put(
                        w1.at[pl.ds(s * size + k * high, high), cols],
                        dst.at[where[HEAD + 16 + 2 * s + k], pl.ds(n * high, high)],
                    )
    put.wait()


def entries(order, shards):
    if shards == 1:
        return 1
    return 2 * shards if order[-1] == "g" else shards


def forward(where, orders, shards, x, mix_own, mix_sib, c0, c1, wo, w1, w2, bo, ag, ash, b1, b2, fg, fsh, after=()):
    rows, span, width = c0.shape
    half = 2 * span
    hidden = w1.shape[1]
    tokens = rows * half
    whole = lambda v: pl.BlockSpec(v.shape, lambda i, w: (0,) * len(v.shape))
    anywhere = pl.BlockSpec(memory_space=pl.ANY)
    outs = [SDS((1, hidden + 3 * width), F32)]
    outs += [SDS((rows, span, width), LOW)] * 2 + [SDS((tokens, hidden), LOW)]
    outs += [SDS((tokens, width), F32), SDS((tokens, 128), F32), SDS((tokens, width), F32)]
    n = entries(orders[0], shards)
    outs += [SDS((n, hidden // 2 // n, width), LOW)] * 2
    n = entries(orders[1], shards)
    outs += [SDS((n, 2 * width // n, width), LOW)] * 2
    small = (mix_own, mix_sib, bo, ag, ash, b1, b2, fg, fsh)
    low = lambda *s: pltpu.VMEM(s, LOW)
    wide = lambda *s: pltpu.VMEM(s, F32)
    return call(
        functools.partial(forward_kernel, shards=shards), where, small + (x, c0, c1, wo, w1, w2), after,
        grid=(1,),
        in_specs=[whole(v) for v in small] + [anywhere] * 6,
        out_specs=[whole(outs[0])] + [anywhere] * (len(outs) - 1),
        out_shape=outs,
        scratch=[
            low(width, width), low(width, hidden), low(hidden, width),
            low(rows, half, width), low(rows, half, width), low(rows, half, width),
            low(tokens, hidden), low(tokens, hidden), low(tokens, hidden), wide(tokens, width), wide(tokens, 128),
            low(tokens, width), wide(tokens, width), low(tokens, width), wide(1, hidden), wide(8, hidden + 3 * width),
            pltpu.SemaphoreType.DMA((8,)), pltpu.SemaphoreType.DMA((8 + 12 * shards,)),
        ],
        us=27,
        name="forward",
    )


def branch_kernel(
    where, mix_own, mix_sib, ag, sums_in, dinner_hbm, norm_hbm, scale_hbm, second_hbm,
    wo_hbm, w1_hbm,
    sums, dbranch_out, dm_own, dm_sib, o_keep, o_send,
    wo, w1, dm, dinner, norm1, scale1, second, dbranch, ograd, partial,
    in_sem, out_sem, *, shards,
):
    core = where[0]
    rows = mix_own.shape[0]
    block = mix_own.shape[2]
    width, hidden = w1.shape
    half = width // 2
    chunks = 3
    step = hidden // chunks
    lines = rows * block // TALL
    vec = lambda ref: ref[...].astype(F32)[None, :]
    own_half = pl.ds(pl.multiple_of(core * half, half), half)
    sib_half = pl.ds(pl.multiple_of((1 - core) * half, half), half)
    load_j = []
    for j in range(chunks):
        cols = slice(j * step, (j + 1) * step)
        load_j.append(pltpu.make_async_copy(dinner_hbm.at[:, cols], dinner.at[:, cols], in_sem.at[2 * j]))
        load_j.append(pltpu.make_async_copy(w1_hbm.at[:, cols], w1.at[:, cols], in_sem.at[1 + 2 * j]))
        load_j[-2].start()
        load_j[-1].start()
    pairs = ((second_hbm, second), (norm_hbm, norm1), (scale_hbm, scale1), (wo_hbm, wo))
    late = [pltpu.make_async_copy(src, dst, in_sem.at[6 + k]) for k, (src, dst) in enumerate(pairs)]
    for copy in late:
        copy.start()
    put = Puts(out_sem)
    partial[...] = jnp.zeros_like(partial)
    total = None
    for j in range(chunks):
        cols = slice(j * step, (j + 1) * step)
        load_j[2 * j].wait()
        load_j[2 * j + 1].wait()
        if j == chunks - 1:
            late[0].wait()
        value = contract(dinner[:, cols], w1[:, cols], 1, 1)
        total = value if total is None else total + value
    second[...] += total
    for copy in late[1:]:
        copy.wait()

    def norm_attn(i, _):
        at = pl.ds(pl.multiple_of(i * TALL, TALL), TALL)
        d_first = second[at]
        n1 = norm1[at]
        d_branch = norm_back(d_first * vec(ag), n1, scale1[at][:, :1]).astype(LOW)
        dbranch[at] = d_branch
        partial[:, :width] += fold(d_branch.astype(F32))
        partial[:, width : 2 * width] += fold(d_first * n1)
        partial[:, 2 * width : 3 * width] += fold(d_first)
        return 0

    lax.fori_loop(0, lines, norm_attn, 0, unroll=lines)
    put(dbranch, dbranch_out)
    for r in range(rows):
        at = slice(r * block, (r + 1) * block)
        dm[0, r] = contract(wo[own_half, :], dbranch[at], 1, 1).astype(LOW)
        dm[1, r] = contract(wo[sib_half, :], dbranch[at], 1, 1).astype(LOW)
    put(dm.at[1], dm_sib)
    put(dm.at[0], dm_own)
    sums[:, : 3 * width] = col_sum(partial[...])
    sums[:, 3 * width :] = sums_in[...]
    size = width // shards
    for k, mix in enumerate((mix_own, mix_sib)):
        value = contract(mix[0], dbranch[:block], 1, 0)
        for r in range(1, rows):
            value += contract(mix[r], dbranch[r * block : (r + 1) * block], 1, 0)
        ograd[own_half if k == 0 else sib_half, :] = value.astype(LOW)
    for s in range(shards):
        put.shard(where, HEAD + 16 * 2, s, ograd, s * size, size, sib_half, o_send)
        put.shard(where, HEAD + 16 * 2, s, ograd, s * size, size, own_half, o_keep)
    put.wait()


def branch(
    where, orders, shards, mix_own, mix_sib, ag, sums, dinner, norm, scale, second, wo, w1, after=(), thread=()
):
    rows, cols, half = mix_own.shape
    width, hidden = w1.shape
    tokens = rows * half
    whole = lambda v: pl.BlockSpec(v.shape, lambda i, w: (0,) * len(v.shape))
    anywhere = pl.BlockSpec(memory_space=pl.ANY)
    outs = [SDS((1, 6 * width + hidden), F32), SDS((tokens, width), LOW)] + [SDS((rows, cols, half), LOW)] * 2
    n = entries(orders[2], shards)
    outs += [SDS((n, width // n, cols), LOW)] * 2
    small = (mix_own, mix_sib, ag, sums)
    big = (dinner, norm, scale, second, wo, w1)
    low = lambda *s: pltpu.VMEM(s, LOW)
    wide = lambda *s: pltpu.VMEM(s, F32)
    return call(
        functools.partial(branch_kernel, shards=shards), where, small + big, after, thread,
        grid=(1,),
        in_specs=[whole(v) for v in small] + [anywhere] * len(big),
        out_specs=[whole(outs[0])] + [anywhere] * (len(outs) - 1),
        out_shape=outs,
        scratch=[
            low(width, width), low(width, hidden), low(2, rows, cols, half), low(tokens, hidden),
            wide(tokens, width), wide(tokens, 128), wide(tokens, width), low(tokens, width),
            low(width, width), wide(8, 3 * width),
            pltpu.SemaphoreType.DMA((10,)), pltpu.SemaphoreType.DMA((3 + 4 * shards,)),
        ],
        us=13,
        name="branch",
    )


def spread(where, dst, src, order, n, shards, lanes):
    width = src.shape[0]
    size = width // shards
    if shards == 1:
        dst[:width, lanes] = src[...].astype(LOW)
        return
    cut = 2 if order[-1] == "g" else 1
    high = size // cut
    for s in range(shards):
        for k in range(cut):
            start = pl.multiple_of(where[HEAD + 16 * n + 2 * s + k] * high, 16)
            row = s * size + k * high
            dst[pl.ds(start, high), lanes] = src[row : row + high].astype(LOW)


def pair_back(step_refs, grads, acc, bias, first):
    x_ref, q_ref, k_ref, v_ref, e_ref, inv_ref, mix_own, mix_sib, dm_own, dm_sib = step_refs
    scale = HD**-0.5
    tall = q_ref.shape[1]
    for h in range(tall // HD):
        part = slice(h * HD, (h + 1) * HD)
        mixed = jnp.concatenate([mix_own[0, part], mix_sib[0, part]], axis=1)
        dm = jnp.concatenate([dm_own[0, part], dm_sib[0, part]], axis=1)
        d_out = dm.astype(F32) * inv_ref[0, h : h + 1]
        delta = col_sum(d_out * mixed.astype(F32))
        d_low = d_out.astype(LOW)
        e = e_ref[0, h]
        dp = contract(v_ref[0, part], d_low, 0, 0)
        ds = (e.astype(F32) * (dp - delta)).astype(LOW)
        at = lambda n: slice(n * tall + h * HD, n * tall + (h + 1) * HD)
        grads[at(0)] = (contract(k_ref[0, part], ds, 1, 0) * scale).astype(LOW)
        grads[at(1)] = (contract(q_ref[0, part], ds, 1, 1) * scale).astype(LOW)
        grads[at(2)] = contract(d_low, e, 1, 1).astype(LOW)
    value = contract(x_ref[0], grads[...], 0, 1)
    ones = jnp.ones((8, x_ref.shape[1]), LOW)
    sums = contract(ones, grads[...], 1, 1)
    acc[...] = jnp.where(first, value, acc[...] + value)
    bias[...] = jnp.where(first, sums, bias[...] + sums)


def send_off(packed, keep, send, sems):
    put = Puts(sems)
    half = keep.shape[0]
    put(packed.at[half:], send)
    put(packed.at[:half], keep)
    put.wait()


def pair_kernel(where, *refs, orders, shards, with_o):
    step_refs, refs = refs[:10], refs[10:]
    if with_o:
        o_keep, o_got, *refs = refs
    d_out, bias, keep, send, acc, packed, sems = refs
    r = pl.program_id(0)
    pair_back(step_refs, d_out.at[0], acc, bias, r == 0)

    @pl.when(r == pl.num_programs(0) - 1)
    def _():
        cols = acc.shape[1]
        spread(where, packed, acc, orders[2], 2, shards, slice(0, cols))
        if with_o:
            packed[:, cols:] = (o_keep[...].astype(F32) + o_got[...].astype(F32)).astype(LOW)
        send_off(packed, keep, send, sems)


def last_pair_kernel(
    where, *refs, orders, shards,
):
    step_refs, refs = refs[:10], refs[10:]
    d0, d1, bias0, bias1, dbranch, wq, wk, wv, vectors, *refs = refs
    in_own, in_out, keep, send, grads, dq, dk, dv, acc, bias, packed, sems = refs
    r = pl.program_id(0)
    pair_back(step_refs, grads, acc, bias, r == 0)
    tall = grads.shape[0] // 3
    for n, d in enumerate((dq, dk, dv)):
        part = slice(n * tall, (n + 1) * tall)
        d[:tall] = d0[0, part]
        d[tall : 2 * tall] = d1[0, part]
        d[2 * tall :] = grads[part]
    back = contract(dq[...], wq[...], 0, 1)
    back = back + contract(dk[...], wk[...], 0, 1) + contract(dv[...], wv[...], 0, 1)
    half = back.shape[0] // 2
    in_own[0] = (back[:half] + dbranch[0].astype(F32)).astype(LOW)
    in_out[0] = back[half:].astype(LOW)

    @pl.when(r == pl.num_programs(0) - 1)
    def _():
        core = where[0]
        width, cols = acc.shape
        spread(where, packed, acc, orders[3], 3, shards, slice(0, cols))
        lines = [vectors[:, n * cols : (n + 1) * cols] for n in range(vectors.shape[1] // cols)]
        zero = jnp.zeros((1, cols), F32)
        for n in (2, 0):
            part = slice(n * tall, (n + 1) * tall)
            line = jnp.concatenate([bias0[:1, part], bias1[:1, part], bias[:1, part]], axis=1)
            lines += [jnp.where(core == c, line, zero) for c in range(2)]
        lines.append(jnp.zeros((TAIL - len(lines), cols), F32))
        packed[width:] = jnp.concatenate(lines, axis=0).astype(LOW)
        send_off(packed, keep, send, sems)


def pair_specs(p, x, attention):
    rows, cols, length = attention[0].shape
    width = x.shape[2]
    heads = cols // HD
    step = 2
    tall = step * HD
    row3 = lambda *s: pl.BlockSpec((1,) + s, lambda r, w: (r,) + (0,) * len(s))
    big = pl.BlockSpec((1, tall, length), lambda r, w: (r, p, 0))
    small = pl.BlockSpec((1, tall, length // 2), lambda r, w: (r, p, 0))
    inv = pl.BlockSpec((1, 8, length), lambda r, w: (r, p, 0))
    specs = [row3(length, width)] + [big] * 3
    specs += [pl.BlockSpec((1, step, length, length), lambda r, w: (r, p, 0, 0)), inv]
    return specs + [small] * 4, row3


def pair_grads(where, orders, shards, p, x, attention, o=(), after=(), thread=()):
    rows, cols, length = attention[0].shape
    width = x.shape[2]
    specs, row3 = pair_specs(p, x, attention)
    whole = lambda v: pl.BlockSpec(v.shape, lambda r, w: (0,) * len(v.shape))
    anywhere = pl.BlockSpec(memory_space=pl.ANY)
    total = cols + sum(v.shape[1] for v in o[:1])
    outs = [SDS((rows, cols, length), LOW), SDS((8, cols), F32)] + [SDS((width // 2, total), LOW)] * 2
    return call(
        functools.partial(pair_kernel, orders=orders, shards=shards, with_o=bool(o)), where,
        (x, *attention, *o), after, thread,
        grid=(rows,),
        in_specs=specs + [whole(v) for v in o],
        out_specs=[row3(cols, length), whole(outs[1]), anywhere, anywhere],
        out_shape=outs,
        scratch=[pltpu.VMEM((width, cols), F32), pltpu.VMEM((width, total), LOW), pltpu.SemaphoreType.DMA((2,))],
        us=8,
        name="pair_grads",
    )


def last_pair_grads(where, orders, shards, x, attention, pairs, dbranch, weights, vectors, after=(), thread=()):
    rows, cols, length = attention[0].shape
    width = x.shape[2]
    specs, row3 = pair_specs(2, x, attention)
    whole = lambda v: pl.BlockSpec(v.shape, lambda r, w: (0,) * len(v.shape))
    weight = pl.BlockSpec((width, cols), lambda r, w: (0, w[0]), pipeline_mode=pl.Buffered(1))
    anywhere = pl.BlockSpec(memory_space=pl.ANY)
    low = lambda *s: pltpu.VMEM(s, LOW)
    half = width // 2
    (d0, bias0), (d1, bias1) = pairs
    return call(
        functools.partial(last_pair_kernel, orders=orders, shards=shards), where,
        (x, *attention, d0, d1, bias0, bias1, dbranch, *weights, vectors), after, thread,
        grid=(rows,),
        in_specs=specs
        + [row3(cols, length)] * 2
        + [whole(bias0), whole(bias1), row3(length // 2, width), weight, weight, weight, whole(vectors)],
        out_specs=[row3(length // 2, width)] * 2 + [anywhere] * 2,
        out_shape=[SDS((rows, length // 2, width), LOW)] * 2
        + [SDS((half, cols), LOW), SDS((half + TAIL, cols), LOW)],
        scratch=[low(cols, length)] * 4
        + [pltpu.VMEM((width, cols), F32), pltpu.VMEM((8, cols), F32), low(width + TAIL, cols)]
        + [pltpu.SemaphoreType.DMA((2,))],
        us=10,
        name="last_pair_grads",
    )


def round_kernel(where, *refs, groups):
    add = lambda a, b: (a.astype(F32) + b.astype(F32)).astype(LOW)
    ins = sum(2 * n + tail for n, tail, _ in groups)
    outs = list(refs[ins:])
    refs = list(refs[:ins])
    for n, tail, split in groups:
        keeps, gots = refs[:n], refs[n : 2 * n]
        sent = refs[2 * n] if tail else None
        refs = refs[2 * n + tail :]
        out_keep = outs.pop(0)
        out_send = outs.pop(0) if split or tail else None
        at = 0
        for keep, got in zip(keeps, gots):
            rows, cols = keep.shape
            half = out_keep.shape[0]
            lanes = slice(at, at + cols)
            at += cols
            out_keep[:, lanes] = add(keep[:half], got[:half])
            if split:
                out_send[: rows - half, lanes] = add(keep[half:], got[half:rows])
            elif tail:
                out_send[:rows, lanes] = out_keep[...]
        if tail:
            end = lambda ref: ref[ref.shape[0] - TAIL :]
            out_send[out_send.shape[0] - TAIL :] = add(end(sent), end(gots[0]))


def next_round(where, groups, after=(), thread=()):
    whole = lambda v: pl.BlockSpec(v.shape, lambda i, w: (0,) * len(v.shape))
    ins, outs, form, counts = [], [], [], []
    for keeps, gots, sent, split in groups:
        tail = sent is not None
        ins += [*keeps, *gots] + ([sent] if tail else [])
        rows = keeps[0].shape[0]
        cols = sum(v.shape[1] for v in keeps)
        half = rows // 2 if split else rows
        new = [SDS((half, cols), LOW)]
        if split or tail:
            new.append(SDS((half + (TAIL if tail else 0), cols), LOW))
        outs += new
        counts.append(len(new))
        form.append((len(keeps), int(tail), split))
    got, thread = call(
        functools.partial(round_kernel, groups=tuple(form)), where, ins, after, thread,
        grid=(1,),
        in_specs=[whole(v) for v in ins],
        out_specs=[whole(v) for v in outs],
        out_shape=outs,
        us=1,
        name="next_round",
        mib=16,
    )
    results = []
    for n in counts:
        results.append(tuple(got[:n]))
        got = got[n:]
    return results, thread


def finish_kernel(where, ab_mine, c_mine, ab_got, c_got, gq, gk, gv, go, *outs):
    core = where[0]
    b = where[1]
    size, width = gq.shape
    cols = width // 2
    tall = cols // 3

    def both(ref, at, mine, got):
        mine, got = mine.astype(F32), got.astype(F32)
        n = mine.shape[1]
        ref[:, at : at + n] = jnp.where(core == 0, mine, got)
        ref[:, cols + at : cols + at + n] = jnp.where(core == 0, got, mine)

    for n, ref in enumerate((gq, gk, gv)):
        for p in range(3):
            mine, got = (c_mine, c_got) if p == 2 else (ab_mine, ab_got)
            at = n * tall + (width if p == 1 else 0)
            both(ref, p * tall, mine[:size, at : at + tall], got[:size, at : at + tall])
    both(go, 0, ab_mine[:, cols:width], ab_got[:, cols:width])
    total = c_mine[size:].astype(F32) + c_got[size:].astype(F32)
    row = 0
    for ref in outs:
        n = ref.shape[0]
        parts = n * (width // size) // cols
        line = jnp.concatenate([total[row + i : row + i + 1] for i in range(parts)], axis=1)
        row += parts
        picked = jnp.zeros((1, n), F32)
        for s in range(width // size):
            picked = jnp.where(b == s, line[:, s * n : (s + 1) * n], picked)
        ref[...] = picked[0]


def finish(where, mine, got, lengths):
    whole = lambda *s: pl.BlockSpec(s, lambda i, w: (0,) * len(s))
    size = mine[0].shape[0]
    width = 2 * mine[1].shape[1]
    return call(
        finish_kernel, where, (*mine, *got), (),
        grid=(1,),
        in_specs=[whole(*v.shape) for v in (*mine, *got)],
        out_specs=[whole(size, width)] * 4 + [whole(n) for n in lengths],
        out_shape=[SDS((size, width), F32)] * 4 + [SDS((n,), F32) for n in lengths],
        us=2,
        name="finish",
        mib=16,
    )


def swap(v, axis, mask, size):
    return lax.ppermute(v, axis, [(i, i ^ mask) for i in range(size)])


def add_low(a, b):
    return (a.astype(F32) + b.astype(F32)).astype(LOW)


def fix(v):
    return lax.optimization_barrier(v)


ORDERS = ("x1y2g", "1xy2g", "y1x2g", "x12y")
BITS = {"x": 0, "1": 1, "2": 2}


def solution(mesh):
    batch_size = mesh.shape["batch"]
    blk_size = mesh.shape["blk"]
    direct = batch_size == 8
    shards = batch_size if direct else 1

    def blk_swap(v, mask):
        return swap(v, "blk", mask, blk_size)

    def hop(v, step):
        if step in BITS:
            return swap(v, "batch", 1 << BITS[step], batch_size)
        return blk_swap(v, 2)

    def split_sum(keep, got):
        half = keep.shape[0] // 2
        return fix(add_low(keep[half:], got[half:])), fix(add_low(keep[:half], got[:half]))

    def per_device(
        tokens, segment_ids, query_weight, query_bias, key_weight, value_weight, value_bias,
        output_weight, output_bias, attn_gain, attn_shift, inner_weight, inner_bias,
        outer_weight, outer_bias, final_gain, final_shift, cotangent,
    ):
        count, span, width = tokens.shape
        rows = count // 2
        me = lax.axis_index("blk")
        b = lax.axis_index("batch")
        core = me & 1
        y = (me >> 1) & 1

        index = jnp.arange(16, dtype=jnp.int32)
        moved = {k: ((index >> (1 + n)) ^ (b >> n)) & 1 for k, n in BITS.items()}
        moved["y"] = (index & 1) ^ y
        maps = []
        for order in ORDERS:
            steps = order[:-1]
            maps.append(sum(moved[k] << (len(steps) - 1 - i) for i, k in enumerate(steps)))
        if not direct:
            maps = [jnp.zeros_like(v) for v in maps]
        where = jnp.concatenate([jnp.stack([core, b, me, y * rows]).astype(jnp.int32)] + maps)

        def mine(v):
            return lax.dynamic_slice_in_dim(v, y * rows, rows, 0)

        def other(v):
            return lax.dynamic_slice_in_dim(v, (1 - y) * rows, rows, 0)

        def halves(own, got, axis):
            return jnp.where(
                core == 0,
                jnp.concatenate([own, got], axis=axis),
                jnp.concatenate([got, own], axis=axis),
            )

        def join_rows(keep, got):
            return jnp.where(
                y == 0, jnp.concatenate([keep, got], axis=0), jnp.concatenate([got, keep], axis=0)
            )

        t1 = blk_swap(other(tokens), 2)
        t0 = mine(tokens)
        t2 = blk_swap(t0, 1)
        t3 = blk_swap(t1, 1)
        x, q, k, v, e, inv, mix_own, mix_out = attend(
            where, (t0, t1, t2, t3), segment_ids,
            query_weight, key_weight, value_weight, query_bias, value_bias,
        )
        c1 = blk_swap(other(cotangent), 2)
        c0 = mine(cotangent)
        mix_sib = blk_swap(mix_out, 1)
        flat = lambda g: g.reshape(-1, g.shape[-1])
        (
            sums, out0, out1, dinner, norm, scale, second, outer_keep, outer_send, inner_keep, inner_send,
        ) = forward(
            where, ORDERS, shards, x, mix_own, mix_sib, c0, c1, output_weight, inner_weight, outer_weight,
            output_bias, attn_gain, attn_shift, inner_bias, outer_bias, final_gain, final_shift,
        )
        outer_keep = flat(outer_keep)
        got = blk_swap(flat(outer_send), 1)
        out_got = blk_swap(out1, 2)
        outer = split_sum(outer_keep, got)
        (inner_send,) = gate(where, (flat(inner_send),), outer)
        inner = split_sum(flat(inner_keep), blk_swap(inner_send, 1))

        def hops():
            if not direct:
                return (), ()
            steps = (ORDERS[0][stage], ORDERS[1][stage])
            return (hop(outer[0], steps[0]), hop(inner[0], steps[1])), (outer[1], inner[1])

        stage = 0
        got, keeps = hops()
        (vectors, dbranch, dm_own, dm_out, o_keep, o_send), through = branch(
            where, ORDERS, shards, mix_own, mix_sib, attn_gain, sums, dinner, norm, scale,
            second, output_weight, inner_weight, after=(outer[0], inner[0]), thread=(out0,) + keeps,
        )
        out0, keeps = through[0], through[1:]
        result = join_rows(out0, out_got)
        dm_sib = blk_swap(dm_out, 1)
        o_got = blk_swap(flat(o_send), 1)
        dbranch = dbranch.reshape(rows, 2 * span, width)
        attention = (q, k, v, e, inv, mix_own, mix_out, dm_own, dm_sib)
        (d0, bias0, a_keep, a_send), keeps = pair_grads(
            where, ORDERS, shards, 0, x, attention, (flat(o_keep), o_got), after=(out_got,), thread=keeps
        )
        if direct:
            outer, inner = (split_sum(keep, g) for keep, g in zip(keeps, got))
        stage = 1
        got, keeps = hops()
        if direct:
            got += (hop(a_send, ORDERS[2][0]),)
            keeps += (a_keep,)
        (d1, bias1, b_keep, b_send), keeps = pair_grads(
            where, ORDERS, shards, 1, x, attention, after=(outer[0], inner[0]), thread=keeps
        )
        if direct:
            got += (hop(b_send, ORDERS[2][0]),)
            keeps += (b_keep,)
        (in_own, in_out, c_keep, c_send), keeps = last_pair_grads(
            where, ORDERS, shards, x, attention, ((d0, bias0), (d1, bias1)), dbranch,
            (query_weight, key_weight, value_weight), vectors, thread=keeps,
        )
        in_sum = fix(add_low(in_own, blk_swap(in_out, 1)))

        def join(v, axis):
            v = fix(v)
            return halves(v, blk_swap(v, 1), axis).astype(F32)

        def add_y(g):
            return fix(add_low(g, blk_swap(g, 2)))

        if direct:

            cells = lambda v: v.reshape(4, -1, width)
            pairs = [add_low(cells(keep), cells(g)) for keep, g in zip(keeps[:2], got[:2])]
            both = lambda a, b: fix(jnp.concatenate([p[a:b] for p in pairs], axis=1).reshape(-1, width))
            ffn, ffn_send = both(0, 2), both(2, 4)
            ((ab, ab_send),), (c_send, ffn_send) = next_round(
                where, [(keeps[2:], got[2:], None, True)], after=(ffn,), thread=(c_send, ffn_send)
            )
            c_got, ffn_got, ab_got = hop(c_send, "x"), hop(ffn_send, "y"), hop(ab_send, "1")
            ffn_send, ffn = split_sum(ffn, ffn_got)
            ((c, c_send), (ab, ab_send)), (ffn_send, in_sum) = next_round(
                where, [((c_keep,), (c_got,), c_send, True), ((ab,), (ab_got,), None, True)],
                after=(ffn,), thread=(ffn_send, in_sum),
            )
            in_got = blk_swap(in_sum[:, span:], 2)
            c_got, ffn_got, ab_got = hop(c_send, "1"), hop(ffn_send, "2"), hop(ab_send, "x")
            ((c, c_send), (ab, ab_send)), _ = next_round(
                where, [((c,), (c_got,), c_send, True), ((ab,), (ab_got,), None, True)], after=(in_got,)
            )
            input_grad = join_rows(in_sum[:, :span], in_got)
            ffn = fix(add_low(ffn, ffn_got))
            c_got, ab_got = hop(c_send, "2"), hop(ab_send, "2")
            ((_, c), (ab,)), (ffn,) = next_round(
                where, [((c,), (c_got,), c_send, False), ((ab,), (ab_got,), None, False)], thread=(ffn,)
            )
            c_got, ab_got, ffn_got = hop(c, "y"), hop(ab, "y"), hop(ffn, "y")
            c = fix(add_low(c, c_got))
            ab = fix(jnp.concatenate([jnp.where(y == 0, ab, ab_got), jnp.where(y == 0, ab_got, ab)], axis=0))
            pair = jnp.stack([ffn, ffn_got])
            ffn = fix(jnp.where(y == 0, pair, pair[::-1]))
            ffn_got = blk_swap(ffn, 1)
            high = ffn.shape[1] // 2
            part = lambda v: v[:, :high].reshape(-1, width)
            outer_done = halves(part(ffn), part(ffn_got), 0).astype(F32)

            def columns(v):
                v = v[:, high:].reshape(2, 2, -1, width)
                return jnp.concatenate([v[:, 0], v[:, 1]], axis=2).reshape(-1, 2 * width)

            inner_done = halves(columns(ffn), columns(ffn_got), 1).astype(F32)
            lengths = [n // shards for n in (width,) * 3 + (inner_weight.shape[1],) + (width,) * 5]
            query_done, key_done, value_done, output_done, *vecs = finish(
                where, (ab, c), tuple(blk_swap(g, 1) for g in (ab, c)), lengths
            )
        else:
            input_grad = join_rows(in_sum[:, :span], blk_swap(in_sum[:, span:], 2))

            def whole(v):
                return add_y(lax.psum_scatter(v, "batch", scatter_dimension=0, tiled=True))

            join_halves = lambda pair: jnp.concatenate([pair[1], pair[0]], axis=0)
            outer_part = join_halves(outer)
            outer_done = whole(halves(outer_part, blk_swap(outer_part, 1), 0)).astype(F32)
            inner_part = join_halves(inner)
            inner_part = jnp.concatenate([inner_part[:width], inner_part[width:]], axis=1)
            inner_done = join(whole(inner_part), 1)
            cols = width // 2
            tall = cols // 3
            whole_a = jnp.concatenate([a_keep, a_send], axis=0)
            groups = (whole_a, jnp.concatenate([b_keep, b_send], axis=0))
            groups += (jnp.concatenate([c_keep, c_send[: c_keep.shape[0]]], axis=0),)
            query_done, key_done, value_done = (
                join(whole(jnp.concatenate([g[:, n * tall : (n + 1) * tall] for g in groups], axis=1)), 1)
                for n in range(3)
            )
            output_done = join(whole(whole_a[:, cols:]), 1)
            total = lax.psum(c_send[c_keep.shape[0] :].astype(F32), ("batch", "blk")).reshape(-1)
            vecs = []
            at = 0
            for n in (width,) * 3 + (inner_weight.shape[1],) + (width,) * 5:
                part = total[at : at + n].reshape(batch_size, n // batch_size)
                vecs.append(lax.dynamic_index_in_dim(part, b, 0, keepdims=False))
                at += n
        g_ob, g_ag, g_as, g_b1, g_b2, g_fg, g_fs, g_vb, g_qb = vecs
        return (
            result, input_grad, query_done, g_qb, key_done, value_done, g_vb, output_done, g_ob,
            g_ag, g_as, inner_done, g_b1, outer_done, g_b2, g_fg, g_fs,
        )

    tok = P("batch", "blk", None)
    mat = P("batch", None)
    vec = P("batch")
    return jax.shard_map(
        per_device,
        mesh=mesh,
        in_specs=(tok, P("batch", None)) + (P(),) * 15 + (tok,),
        out_specs=(
            tok, tok, mat, vec, mat, mat, vec, mat, vec, vec, vec, mat, vec, mat, vec, vec, vec,
        ),
        check_vma=False,
    )
```

```python
import functools

import jax
import jax.numpy as jnp
from jax import lax
from jax.experimental import pallas as pl
from jax.experimental.pallas import tpu as pltpu
from jax.sharding import PartitionSpec as P

HD = 64
EPSILON = 1e-12
NEGATIVE = -1e30
LOW = jnp.bfloat16
F32 = jnp.float32
LOG2E = 1.4426950408889634
MIB = 1024 * 1024
COST = 5e7
SDS = jax.ShapeDtypeStruct


def contract(a, b, left, right):
    return lax.dot_general(a, b, (((left,), (right,)), ((), ())), preferred_element_type=F32)


def call(kernel, where, inputs, after, thread=None, *, grid, in_specs, out_specs, out_shape, us, name, scratch=(), mib=63):
    plain = thread is None
    thread = thread or ()
    count = len(inputs)
    extra = len(after) + len(thread)
    outs = len(out_shape)
    anywhere = pl.BlockSpec(memory_space=pl.ANY)

    def body(w, *refs):
        at = count + extra
        kernel(w, *refs[:count], *refs[at : at + outs], *refs[at + outs + len(thread) :])

    got = pl.pallas_call(
        body,
        grid_spec=pltpu.PrefetchScalarGridSpec(
            num_scalar_prefetch=1,
            grid=grid,
            in_specs=list(in_specs) + [anywhere] * extra,
            out_specs=list(out_specs) + [anywhere] * len(thread),
            scratch_shapes=list(scratch),
        ),
        out_shape=list(out_shape) + [SDS(v.shape, v.dtype) for v in thread],
        compiler_params=pltpu.CompilerParams(vmem_limit_bytes=mib * MIB),
        cost_estimate=pl.CostEstimate(flops=int(us * COST), bytes_accessed=0, transcendentals=0),
        input_output_aliases={1 + count + i: outs + i for i in range(len(thread))},
        name=name,
    )(where, *inputs, *thread, *after)
    return got if plain else (got[:outs], tuple(got[outs:]))


def gate(where, thread, after):
    return call(
        lambda where: None, where, (), after, thread, grid=(1,), in_specs=[], out_specs=[], out_shape=[], us=0.1,
        name="gate", mib=16,
    )[1]


def col_sum(v):
    return jnp.sum(v, axis=0, keepdims=True)


def as_column(v, rows):
    return jnp.broadcast_to(v[None, :], (rows, v.shape[0])).T


def attend_kernel(
    where, t0, t1, t2, t3, seg_ref, wq, wk, wv, bq, bv,
    x_out, q_out, k_out, v_out, e_out, inv_out, mix_own, mix_sib, bias,
):
    j = 0
    cols = q_out.shape[1]
    half = mix_own.shape[2]
    heads = e_out.shape[1]

    if True:
        core = where[0]
        x = jnp.concatenate([t0[0], t1[0], t2[0], t3[0]], axis=0)
        x_out[0] = x
        own_part = lambda ref: jnp.where(core == 0, ref[:cols].astype(F32), ref[cols:].astype(F32))
        qb = as_column(own_part(bq), 128)[:, :1]
        vb = as_column(own_part(bv), 128)[:, :1]
        q_out[0] = (contract(wq[...], x, 0, 1) + qb).astype(LOW)
        k_out[0] = contract(wk[...], x, 0, 1).astype(LOW)
        v_out[0] = (contract(wv[...], x, 0, 1) + vb).astype(LOW)
        me, row = where[2], where[3] + pl.program_id(0)
        span = t0.shape[1]
        line = seg_ref[pl.ds(row, 1), :]
        here = [jnp.bitwise_xor(me, r) for r in (0, 2, 1, 3)]
        parts = [line[:, n * span : (n + 1) * span] for n in range(4)]
        pick = lambda q: sum(jnp.where(q == n, part, 0) for n, part in enumerate(parts))
        seg_row = jnp.concatenate([pick(q) for q in here], axis=1).astype(F32)
        seg_col = jnp.broadcast_to(seg_row, (128, seg_row.shape[1])).T[:, :1]
        bias[...] = jnp.where(seg_col == seg_row, 0.0, NEGATIVE)

    for h in range(heads):
        part = slice(h * HD, (h + 1) * HD)
        s = contract(k_out[0, part], q_out[0, part], 0, 0) + bias[...]
        top = jnp.max(s, axis=0, keepdims=True)
        e = jnp.exp2((s - top) * (LOG2E * HD**-0.5))
        low = e.astype(LOW)
        inv = 1.0 / col_sum(e)
        e_out[0, h] = low
        inv_out[0, 8 * (h // 2) + h % 2 : 8 * (h // 2) + h % 2 + 1] = inv
        mixed = (contract(v_out[0, part], low, 1, 0) * inv).astype(LOW)
        mix_own[0, h * HD : (h + 1) * HD] = mixed[:, :half]
        mix_sib[0, h * HD : (h + 1) * HD] = mixed[:, half:]


def attend(where, toks, segments, wq, wk, wv, bq, bv, after=()):
    rows, span, width = toks[0].shape
    length = 4 * span
    cols = width // 2
    heads = cols // HD
    step = heads
    tall = step * HD
    row3 = lambda *s: pl.BlockSpec((1,) + s, lambda t, w: (t,) + (0,) * len(s))
    weight = pl.BlockSpec((width, cols), lambda t, w: (0, w[0]), pipeline_mode=pl.Buffered(1))
    bias = pl.BlockSpec((width,), lambda t, w: (0,))
    mix = pl.BlockSpec((1, tall, length // 2), lambda t, w: (t, 0, 0))
    return call(
        attend_kernel, where, (*toks, segments, wq, wk, wv, bq, bv), after,
        grid=(rows,),
        in_specs=[row3(span, width)] * 4
        + [pl.BlockSpec(segments.shape, lambda t, w: (0, 0)), weight, weight, weight, bias, bias],
        out_specs=[row3(length, width)]
        + [row3(cols, length)] * 3
        + [
            pl.BlockSpec((1, step, length, length), lambda t, w: (t, 0, 0, 0)),
            pl.BlockSpec((1, 24, length), lambda t, w: (t, 0, 0)), mix, mix,
        ],
        out_shape=[SDS((rows, length, width), LOW)]
        + [SDS((rows, cols, length), LOW)] * 3
        + [SDS((rows, heads, length, length), LOW), SDS((rows, 24, length), F32)]
        + [SDS((rows, cols, length // 2), LOW)] * 2,
        scratch=[pltpu.VMEM((length, length), F32)],
        us=18,
        name="attend",
    )


def norm_parts(v):
    center = v - jnp.mean(v, axis=1, keepdims=True)
    spread = jnp.mean(center * center, axis=1, keepdims=True)
    scale = lax.rsqrt(spread + EPSILON)
    return center * scale, scale


def norm_back(dn, n, scale):
    return scale * (
        dn - jnp.mean(dn, axis=1, keepdims=True) - n * jnp.mean(dn * n, axis=1, keepdims=True)
    )


def fold(v):
    return jnp.sum(v.reshape(v.shape[0] // 8, 8, v.shape[1]), axis=0)


TALL = 128
HEAD = 4
TAIL = 16


class Puts:
    def __init__(self, sems):
        self.sems = sems
        self.copies = []

    def __call__(self, src, dst):
        copy = pltpu.make_async_copy(src, dst, self.sems.at[len(self.copies)])
        copy.start()
        self.copies.append(copy)

    def shard(self, where, base, s, src, row, rows, cols, dst):
        if dst.shape[1] == rows:
            at = pl.ds(pl.multiple_of(row, 16), rows)
            self(src.at[at, cols], dst.at[where[base + 2 * s]])
            return
        for k in range(2):
            at = pl.ds(pl.multiple_of(row + k * (rows // 2), 16), rows // 2)
            self(src.at[at, cols], dst.at[where[base + 2 * s + k]])

    def wait(self):
        for copy in self.copies:
            copy.wait()


def place(i, block):
    per = block // TALL
    return i // per, pl.ds(pl.multiple_of((i % per) * TALL, TALL), TALL)


def forward_kernel(
    where, mix_own, mix_sib, bo, ag, ash, b1, b2, fg, fsh,
    x_hbm, c0_hbm, c1_hbm, wo_hbm, w1_hbm, w2_hbm,
    sums, out0, out1, dinner_out, norm_out, scale_out, second_out, keep, send, inner_keep, inner_send,
    wo, w1, w2, x, cot, result, act, slope, dinner, norm1, scale1, first_low, second, douter, bias1, partial,
    in_sem, out_sem, *, shards,
):
    core = where[0]
    rows, block, width = x.shape
    span = block // 2
    half = width // 2
    hidden = w1.shape[1]
    chunks = 3
    step = hidden // chunks
    lines = rows * block // TALL
    vec = lambda ref: ref[...].astype(F32)[None, :]
    own_half = pl.ds(pl.multiple_of(core * half, half), half)
    sib_half = pl.ds(pl.multiple_of((1 - core) * half, half), half)
    loads = [
        pltpu.make_async_copy(wo_hbm, wo, in_sem.at[0]),
        pltpu.make_async_copy(x_hbm.at[:, :block], x, in_sem.at[1]),
        pltpu.make_async_copy(c0_hbm, cot.at[:, :span], in_sem.at[2]),
        pltpu.make_async_copy(c1_hbm, cot.at[:, span:], in_sem.at[3]),
    ]
    for j in range(chunks):
        cols = slice(j * step, (j + 1) * step)
        loads.append(pltpu.make_async_copy(w1_hbm.at[:, cols], w1.at[:, cols], in_sem.at[4 + j]))
    loads.append(pltpu.make_async_copy(w2_hbm, w2, in_sem.at[4 + chunks]))
    for k in (0, 1, 4, 5, 6, 7, 2, 3):
        loads[k].start()
    put = Puts(out_sem)
    bias1[...] = vec(b1)
    partial[...] = jnp.zeros_like(partial)
    loads[0].wait()
    for r in range(rows):
        at = slice(r * block, (r + 1) * block)
        second[at] = contract(mix_own[r], wo[own_half, :], 0, 0) + contract(mix_sib[r], wo[sib_half, :], 0, 0)
    loads[1].wait()

    def norm_first(i, _):
        at = pl.ds(pl.multiple_of(i * TALL, TALL), TALL)
        r, line = place(i, block)
        n1, s1 = norm_parts(x[r, line].astype(F32) + (second[at] + vec(bo)))
        norm1[at] = n1
        scale1[at] = jnp.broadcast_to(s1, (TALL, 128))
        first = n1 * vec(ag) + vec(ash)
        first_low[at] = first.astype(LOW)
        second[at] = first + vec(b2)
        return 0

    lax.fori_loop(0, lines, norm_first, 0, unroll=lines)
    put(norm1, norm_out)
    put(scale1, scale_out)
    for j in range(chunks):
        cols = slice(j * step, (j + 1) * step)
        loads[4 + j].wait()
        inner = contract(first_low[...], w1[:, cols], 1, 0) + bias1[:, cols]
        big = 0.5 + 0.5 * lax.erf(inner * 0.7071067811865476)
        bell = jnp.exp2(inner * inner * (-0.5 * LOG2E)) * 0.3989422804014327
        act[:, cols] = (inner * big).astype(LOW)
        slope[:, cols] = (big + inner * bell).astype(LOW)
    loads[4 + chunks].wait()
    for r in range(rows):
        at = slice(r * block, (r + 1) * block)
        second[at] += contract(act[at], w2[...], 1, 0)
    loads[2].wait()
    loads[3].wait()

    def norm_second(i, _):
        at = pl.ds(pl.multiple_of(i * TALL, TALL), TALL)
        r, line = place(i, block)
        n2, s2 = norm_parts(second[at])
        result[r, line] = (n2 * vec(fg) + vec(fsh)).astype(LOW)
        g = cot[r, line].astype(F32)
        d_second = norm_back(g * vec(fg), n2, s2)
        second[at] = d_second
        d_outer = d_second.astype(LOW)
        douter[at] = d_outer
        partial[:, hidden : hidden + width] += fold(d_outer.astype(F32))
        partial[:, hidden + width : hidden + 2 * width] += fold(g * n2)
        partial[:, hidden + 2 * width :] += fold(g)
        return 0

    lax.fori_loop(0, lines, norm_second, 0, unroll=lines)
    put(second, second_out)
    put(result.at[:, :span], out0)
    put(result.at[:, span:], out1)

    for j in range(chunks):
        cols = slice(j * step, (j + 1) * step)
        di = (contract(douter[...], w2[cols, :], 1, 1) * slope[:, cols].astype(F32)).astype(LOW)
        dinner[:, cols] = di
        partial[:, cols] = fold(di.astype(F32))
        put(dinner.at[:, cols], dinner_out.at[:, cols])
    sums[...] = col_sum(partial[...])

    size = hidden // shards
    part = size // 2
    every = slice(0, width)
    for s in range(shards):
        for piece in range(8 // shards):
            high = hidden // 8
            at = slice(s * size + piece * high, s * size + (piece + 1) * high)
            w2[at, :] = contract(act[:, at], douter[...], 0, 0).astype(LOW)
        put.shard(where, HEAD, s, w2, s * size + (1 - core) * part, part, every, send)
        put.shard(where, HEAD, s, w2, s * size + core * part, part, every, keep)
    wide = hidden // 2
    size = width // shards
    for h in range(2):
        side = jnp.where(core == 0, 1 - h, h)
        at = pl.ds(pl.multiple_of(side * wide, 128), wide)
        w1[:, at] = contract(first_low[...], dinner[:, at], 0, 0).astype(LOW)
        dst = (inner_send, inner_keep)[h]
        pieces = dst.shape[0] // shards
        high = size // pieces
        for s in range(shards):
            for k in range(pieces):
                for n in range(2):
                    cols = pl.ds(pl.multiple_of(side * wide + n * width, 128), width)
                    put(
                        w1.at[pl.ds(s * size + k * high, high), cols],
                        dst.at[where[HEAD + 16 + 2 * s + k], pl.ds(n * high, high)],
                    )
    put.wait()


def entries(order, shards):
    if shards == 1:
        return 1
    return 2 * shards if order[-1] == "g" else shards


def forward(where, orders, shards, x, mix_own, mix_sib, c0, c1, wo, w1, w2, bo, ag, ash, b1, b2, fg, fsh, after=()):
    rows, span, width = c0.shape
    half = 2 * span
    hidden = w1.shape[1]
    tokens = rows * half
    whole = lambda v: pl.BlockSpec(v.shape, lambda i, w: (0,) * len(v.shape))
    anywhere = pl.BlockSpec(memory_space=pl.ANY)
    outs = [SDS((1, hidden + 3 * width), F32)]
    outs += [SDS((rows, span, width), LOW)] * 2 + [SDS((tokens, hidden), LOW)]
    outs += [SDS((tokens, width), F32), SDS((tokens, 128), F32), SDS((tokens, width), F32)]
    n = entries(orders[0], shards)
    outs += [SDS((n, hidden // 2 // n, width), LOW)] * 2
    n = entries(orders[1], shards)
    outs += [SDS((n, 2 * width // n, width), LOW)] * 2
    small = (mix_own, mix_sib, bo, ag, ash, b1, b2, fg, fsh)
    low = lambda *s: pltpu.VMEM(s, LOW)
    wide = lambda *s: pltpu.VMEM(s, F32)
    return call(
        functools.partial(forward_kernel, shards=shards), where, small + (x, c0, c1, wo, w1, w2), after,
        grid=(1,),
        in_specs=[whole(v) for v in small] + [anywhere] * 6,
        out_specs=[whole(outs[0])] + [anywhere] * (len(outs) - 1),
        out_shape=outs,
        scratch=[
            low(width, width), low(width, hidden), low(hidden, width),
            low(rows, half, width), low(rows, half, width), low(rows, half, width),
            low(tokens, hidden), low(tokens, hidden), low(tokens, hidden), wide(tokens, width), wide(tokens, 128),
            low(tokens, width), wide(tokens, width), low(tokens, width), wide(1, hidden), wide(8, hidden + 3 * width),
            pltpu.SemaphoreType.DMA((8,)), pltpu.SemaphoreType.DMA((8 + 12 * shards,)),
        ],
        us=27,
        name="forward",
    )


def branch_kernel(
    where, mix_own, mix_sib, ag, sums_in, dinner_hbm, norm_hbm, scale_hbm, second_hbm,
    wo_hbm, w1_hbm,
    sums, dbranch_out, dm_own, dm_sib, o_keep, o_send,
    wo, w1, dm, dinner, norm1, scale1, second, dbranch, ograd, partial,
    in_sem, out_sem, *, shards,
):
    core = where[0]
    rows = mix_own.shape[0]
    block = mix_own.shape[2]
    width, hidden = w1.shape
    half = width // 2
    chunks = 3
    step = hidden // chunks
    lines = rows * block // TALL
    vec = lambda ref: ref[...].astype(F32)[None, :]
    own_half = pl.ds(pl.multiple_of(core * half, half), half)
    sib_half = pl.ds(pl.multiple_of((1 - core) * half, half), half)
    load_j = []
    for j in range(chunks):
        cols = slice(j * step, (j + 1) * step)
        load_j.append(pltpu.make_async_copy(dinner_hbm.at[:, cols], dinner.at[:, cols], in_sem.at[2 * j]))
        load_j.append(pltpu.make_async_copy(w1_hbm.at[:, cols], w1.at[:, cols], in_sem.at[1 + 2 * j]))
        load_j[-2].start()
        load_j[-1].start()
    pairs = ((second_hbm, second), (norm_hbm, norm1), (scale_hbm, scale1), (wo_hbm, wo))
    late = [pltpu.make_async_copy(src, dst, in_sem.at[6 + k]) for k, (src, dst) in enumerate(pairs)]
    for copy in late:
        copy.start()
    put = Puts(out_sem)
    partial[...] = jnp.zeros_like(partial)
    total = None
    for j in range(chunks):
        cols = slice(j * step, (j + 1) * step)
        load_j[2 * j].wait()
        load_j[2 * j + 1].wait()
        if j == chunks - 1:
            late[0].wait()
        value = contract(dinner[:, cols], w1[:, cols], 1, 1)
        total = value if total is None else total + value
    second[...] += total
    for copy in late[1:]:
        copy.wait()

    def norm_attn(i, _):
        at = pl.ds(pl.multiple_of(i * TALL, TALL), TALL)
        d_first = second[at]
        n1 = norm1[at]
        d_branch = norm_back(d_first * vec(ag), n1, scale1[at][:, :1]).astype(LOW)
        dbranch[at] = d_branch
        partial[:, :width] += fold(d_branch.astype(F32))
        partial[:, width : 2 * width] += fold(d_first * n1)
        partial[:, 2 * width : 3 * width] += fold(d_first)
        return 0

    lax.fori_loop(0, lines, norm_attn, 0, unroll=lines)
    put(dbranch, dbranch_out)
    for r in range(rows):
        at = slice(r * block, (r + 1) * block)
        dm[0, r] = contract(wo[own_half, :], dbranch[at], 1, 1).astype(LOW)
        dm[1, r] = contract(wo[sib_half, :], dbranch[at], 1, 1).astype(LOW)
    put(dm.at[1], dm_sib)
    put(dm.at[0], dm_own)
    sums[:, : 3 * width] = col_sum(partial[...])
    sums[:, 3 * width :] = sums_in[...]
    size = width // shards
    for k, mix in enumerate((mix_own, mix_sib)):
        value = contract(mix[0], dbranch[:block], 1, 0)
        for r in range(1, rows):
            value += contract(mix[r], dbranch[r * block : (r + 1) * block], 1, 0)
        ograd[own_half if k == 0 else sib_half, :] = value.astype(LOW)
    for s in range(shards):
        put.shard(where, HEAD + 16 * 2, s, ograd, s * size, size, sib_half, o_send)
        put.shard(where, HEAD + 16 * 2, s, ograd, s * size, size, own_half, o_keep)
    put.wait()


def branch(
    where, orders, shards, mix_own, mix_sib, ag, sums, dinner, norm, scale, second, wo, w1, after=(), thread=()
):
    rows, cols, half = mix_own.shape
    width, hidden = w1.shape
    tokens = rows * half
    whole = lambda v: pl.BlockSpec(v.shape, lambda i, w: (0,) * len(v.shape))
    anywhere = pl.BlockSpec(memory_space=pl.ANY)
    outs = [SDS((1, 6 * width + hidden), F32), SDS((tokens, width), LOW)] + [SDS((rows, cols, half), LOW)] * 2
    n = entries(orders[2], shards)
    outs += [SDS((n, width // n, cols), LOW)] * 2
    small = (mix_own, mix_sib, ag, sums)
    big = (dinner, norm, scale, second, wo, w1)
    low = lambda *s: pltpu.VMEM(s, LOW)
    wide = lambda *s: pltpu.VMEM(s, F32)
    return call(
        functools.partial(branch_kernel, shards=shards), where, small + big, after, thread,
        grid=(1,),
        in_specs=[whole(v) for v in small] + [anywhere] * len(big),
        out_specs=[whole(outs[0])] + [anywhere] * (len(outs) - 1),
        out_shape=outs,
        scratch=[
            low(width, width), low(width, hidden), low(2, rows, cols, half), low(tokens, hidden),
            wide(tokens, width), wide(tokens, 128), wide(tokens, width), low(tokens, width),
            low(width, width), wide(8, 3 * width),
            pltpu.SemaphoreType.DMA((10,)), pltpu.SemaphoreType.DMA((3 + 4 * shards,)),
        ],
        us=13,
        name="branch",
    )


def spread(where, dst, src, order, n, shards, lanes):
    width = src.shape[0]
    size = width // shards
    if shards == 1:
        dst[:width, lanes] = src[...].astype(LOW)
        return
    cut = 2 if order[-1] == "g" else 1
    high = size // cut
    for s in range(shards):
        for k in range(cut):
            start = pl.multiple_of(where[HEAD + 16 * n + 2 * s + k] * high, 16)
            row = s * size + k * high
            dst[pl.ds(start, high), lanes] = src[row : row + high].astype(LOW)


def pair_back(step_refs, grads, acc, bias, first):
    x_ref, q_ref, k_ref, v_ref, e_ref, inv_ref, mix_own, mix_sib, dm_own, dm_sib = step_refs
    scale = HD**-0.5
    tall = q_ref.shape[1]
    for h in range(tall // HD):
        part = slice(h * HD, (h + 1) * HD)
        mixed = jnp.concatenate([mix_own[0, part], mix_sib[0, part]], axis=1)
        dm = jnp.concatenate([dm_own[0, part], dm_sib[0, part]], axis=1)
        d_out = dm.astype(F32) * inv_ref[0, h : h + 1]
        delta = col_sum(d_out * mixed.astype(F32))
        d_low = d_out.astype(LOW)
        e = e_ref[0, h]
        dp = contract(v_ref[0, part], d_low, 0, 0)
        ds = (e.astype(F32) * (dp - delta)).astype(LOW)
        at = lambda n: slice(n * tall + h * HD, n * tall + (h + 1) * HD)
        grads[at(0)] = (contract(k_ref[0, part], ds, 1, 0) * scale).astype(LOW)
        grads[at(1)] = (contract(q_ref[0, part], ds, 1, 1) * scale).astype(LOW)
        grads[at(2)] = contract(d_low, e, 1, 1).astype(LOW)
    value = contract(x_ref[0], grads[...], 0, 1)
    ones = jnp.ones((8, x_ref.shape[1]), LOW)
    sums = contract(ones, grads[...], 1, 1)
    acc[...] = jnp.where(first, value, acc[...] + value)
    bias[...] = jnp.where(first, sums, bias[...] + sums)


def send_off(packed, keep, send, sems):
    put = Puts(sems)
    half = keep.shape[0]
    put(packed.at[half:], send)
    put(packed.at[:half], keep)
    put.wait()


def pair_kernel(where, *refs, orders, shards, with_o):
    step_refs, refs = refs[:10], refs[10:]
    if with_o:
        o_keep, o_got, *refs = refs
    d_out, bias, keep, send, acc, packed, sems = refs
    r = pl.program_id(0)
    pair_back(step_refs, d_out.at[0], acc, bias, r == 0)

    @pl.when(r == pl.num_programs(0) - 1)
    def _():
        cols = acc.shape[1]
        spread(where, packed, acc, orders[2], 2, shards, slice(0, cols))
        if with_o:
            packed[:, cols:] = (o_keep[...].astype(F32) + o_got[...].astype(F32)).astype(LOW)
        send_off(packed, keep, send, sems)


def join_copies(where, own, got, room, whole, sems):
    rows = own.shape[0]
    mine = pl.ds(where[3], rows)
    theirs = pl.ds(rows - where[3], rows)
    loads = [pltpu.make_async_copy(v, room.at[n], sems.at[n]) for n, v in enumerate((own, got))]
    stores = [pltpu.make_async_copy(room.at[n], whole.at[at], sems.at[2 + n]) for n, at in enumerate((mine, theirs))]
    return loads, stores


def begin(copies, others=()):
    for copy in others:
        copy.wait()
    for copy in copies:
        copy.start()


def last_pairs_kernel(where, *refs, orders, shards):
    step_refs, refs = refs[:10], refs[10:]
    d0, bias0, dbranch, wq, wk, wv, vectors, out_own, out_got, *refs = refs
    in_own, in_out, keep, send, result, grads, dq, dk, dv, acc, bias, packed, sems, room, join_sems = refs
    loads, stores = join_copies(where, out_own, out_got, room, result, join_sems)
    t = pl.program_id(0)
    r = t // 2
    width = acc.shape[1]
    cols = grads.shape[1]
    tall = cols // 3

    pl.when(t == 0)(lambda: begin(loads))
    pl.when(t == 1)(lambda: begin(stores, loads))
    for p in range(2):

        @pl.when(lax.rem(t, 2) == p)
        def _():
            lanes = slice(p * cols, (p + 1) * cols)
            pair_back(step_refs, grads.at[p], acc.at[p], bias.at[:, lanes], r == 0)

    @pl.when(lax.rem(t, 2) == 1)
    def _():
        for n, d in enumerate((dq, dk, dv)):
            part = slice(n * tall, (n + 1) * tall)
            d[:tall] = d0[0, part]
            d[tall : 2 * tall] = grads[0, part]
            d[2 * tall :] = grads[1, part]
        back = contract(dq[...], wq[...], 0, 1)
        back = back + contract(dk[...], wk[...], 0, 1) + contract(dv[...], wv[...], 0, 1)
        half = back.shape[0] // 2
        in_own[0] = (back[:half] + dbranch[0].astype(F32)).astype(LOW)
        in_out[0] = back[half:].astype(LOW)

    @pl.when(t == pl.num_programs(0) - 1)
    def _():
        core = where[0]
        width = acc.shape[1]
        for p in range(2):
            spread(where, packed, acc.at[p], orders[3], 3, shards, slice(p * cols, (p + 1) * cols))
        wide = 2 * cols
        lines = [vectors[:, n * wide : (n + 1) * wide] for n in range(vectors.shape[1] // wide)]
        zero = jnp.zeros((1, cols), F32)
        for n in (2, 0):
            at = lambda p: slice(p * cols + n * tall, p * cols + (n + 1) * tall)
            line = jnp.concatenate([bias0[:1, n * tall : (n + 1) * tall], bias[:1, at(0)], bias[:1, at(1)]], axis=1)
            lines.append(jnp.concatenate([jnp.where(core == c, line, zero) for c in range(2)], axis=1))
        lines.append(jnp.zeros((TAIL - len(lines), wide), F32))
        packed[packed.shape[0] - TAIL :] = jnp.concatenate(lines, axis=0).astype(LOW)
        send_off(packed, keep, send, sems)
        begin((), stores)


def pair_specs(row, pair, x, attention):
    rows, cols, length = attention[0].shape
    width = x.shape[2]
    step = 2
    tall = step * HD
    row3 = lambda *s: pl.BlockSpec((1,) + s, lambda t, w: (row(t),) + (0,) * len(s))
    big = pl.BlockSpec((1, tall, length), lambda t, w: (row(t), pair(t), 0))
    small = pl.BlockSpec((1, tall, length // 2), lambda t, w: (row(t), pair(t), 0))
    inv = pl.BlockSpec((1, 8, length), lambda t, w: (row(t), pair(t), 0))
    specs = [row3(length, width)] + [big] * 3
    specs += [pl.BlockSpec((1, step, length, length), lambda t, w: (row(t), pair(t), 0, 0)), inv]
    return specs + [small] * 4, row3


def pair_grads(where, orders, shards, x, attention, o=(), after=(), thread=()):
    rows, cols, length = attention[0].shape
    width = x.shape[2]
    specs, row3 = pair_specs(lambda t: t, lambda t: 0, x, attention)
    whole = lambda v: pl.BlockSpec(v.shape, lambda r, w: (0,) * len(v.shape))
    anywhere = pl.BlockSpec(memory_space=pl.ANY)
    total = cols + sum(v.shape[1] for v in o[:1])
    outs = [SDS((rows, cols, length), LOW), SDS((8, cols), F32)] + [SDS((width // 2, total), LOW)] * 2
    return call(
        functools.partial(pair_kernel, orders=orders, shards=shards, with_o=bool(o)), where,
        (x, *attention, *o), after, thread,
        grid=(rows,),
        in_specs=specs + [whole(v) for v in o],
        out_specs=[row3(cols, length), whole(outs[1]), anywhere, anywhere],
        out_shape=outs,
        scratch=[pltpu.VMEM((width, cols), F32), pltpu.VMEM((width, total), LOW), pltpu.SemaphoreType.DMA((2,))],
        us=8,
        name="pair_grads",
    )


def last_pair_grads(
    where, orders, shards, x, attention, first, dbranch, weights, vectors, out_own, out_got, after=(), thread=()
):
    rows, cols, length = attention[0].shape
    width = x.shape[2]
    specs, row3 = pair_specs(lambda t: t // 2, lambda t: 1 + t % 2, x, attention)
    whole = lambda v: pl.BlockSpec(v.shape, lambda t, w: (0,) * len(v.shape))
    weight = pl.BlockSpec((width, cols), lambda t, w: (0, w[0]), pipeline_mode=pl.Buffered(1))
    anywhere = pl.BlockSpec(memory_space=pl.ANY)
    low = lambda *s: pltpu.VMEM(s, LOW)
    half = width // 2
    d0, bias0 = first
    return call(
        functools.partial(last_pairs_kernel, orders=orders, shards=shards), where,
        (x, *attention, d0, bias0, dbranch, *weights, vectors, out_own, out_got), after, thread,
        grid=(2 * rows,),
        in_specs=specs
        + [row3(cols, length), whole(bias0), row3(length // 2, width), weight, weight, weight, whole(vectors)]
        + [anywhere] * 2,
        out_specs=[row3(length // 2, width)] * 2 + [anywhere] * 3,
        out_shape=[SDS((rows, length // 2, width), LOW)] * 2
        + [SDS((half, 2 * cols), LOW), SDS((half + TAIL, 2 * cols), LOW)]
        + [SDS((2 * rows,) + out_own.shape[1:], LOW)],
        scratch=[low(2, cols, length)]
        + [low(cols, length)] * 3
        + [pltpu.VMEM((2, width, cols), F32), pltpu.VMEM((8, 2 * cols), F32), low(width + TAIL, 2 * cols)]
        + [pltpu.SemaphoreType.DMA((2,)), low(2, *out_own.shape), pltpu.SemaphoreType.DMA((4,))],
        us=20,
        name="last_pair_grads",
    )


def round_kernel(where, *refs, groups):
    add = lambda a, b: (a.astype(F32) + b.astype(F32)).astype(LOW)
    ins = sum(2 * n + tail for n, tail, _ in groups)
    outs = list(refs[ins:])
    refs = list(refs[:ins])
    for n, tail, split in groups:
        keeps, gots = refs[:n], refs[n : 2 * n]
        sent = refs[2 * n] if tail else None
        refs = refs[2 * n + tail :]
        out_keep = outs.pop(0)
        out_send = outs.pop(0) if split or tail else None
        at = 0
        for keep, got in zip(keeps, gots):
            rows, cols = keep.shape
            half = out_keep.shape[0]
            lanes = slice(at, at + cols)
            at += cols
            out_keep[:, lanes] = add(keep[:half], got[:half])
            if split:
                out_send[: rows - half, lanes] = add(keep[half:], got[half:rows])
            elif tail:
                out_send[:rows, lanes] = out_keep[...]
        if tail:
            end = lambda ref: ref[ref.shape[0] - TAIL :]
            out_send[out_send.shape[0] - TAIL :] = add(end(sent), end(gots[0]))


def next_round(where, groups, after=(), thread=()):
    whole = lambda v: pl.BlockSpec(v.shape, lambda i, w: (0,) * len(v.shape))
    ins, outs, form, counts = [], [], [], []
    for keeps, gots, sent, split in groups:
        tail = sent is not None
        ins += [*keeps, *gots] + ([sent] if tail else [])
        rows = keeps[0].shape[0]
        cols = sum(v.shape[1] for v in keeps)
        half = rows // 2 if split else rows
        new = [SDS((half, cols), LOW)]
        if split or tail:
            new.append(SDS((half + (TAIL if tail else 0), cols), LOW))
        outs += new
        counts.append(len(new))
        form.append((len(keeps), int(tail), split))
    got, thread = call(
        functools.partial(round_kernel, groups=tuple(form)), where, ins, after, thread,
        grid=(1,),
        in_specs=[whole(v) for v in ins],
        out_specs=[whole(v) for v in outs],
        out_shape=outs,
        us=1,
        name="next_round",
        mib=16,
    )
    results = []
    for n in counts:
        results.append(tuple(got[:n]))
        got = got[n:]
    return results, thread


def finish_kernel(where, a_mine, c_mine, a_got, c_got, in_own, in_got, joined, gq, gk, gv, go, *outs):
    *outs, room, sems = outs
    loads, stores = join_copies(where, in_own.at[:, : joined.shape[1]], in_got, room, joined, sems)
    begin(loads)
    begin(stores, loads)
    core = where[0]
    b = where[1]
    size, width = gq.shape
    cols = width // 2
    tall = cols // 3

    def both(ref, at, mine, got):
        mine, got = mine.astype(F32), got.astype(F32)
        n = mine.shape[1]
        ref[:, at : at + n] = jnp.where(core == 0, mine, got)
        ref[:, cols + at : cols + at + n] = jnp.where(core == 0, got, mine)

    for n, ref in enumerate((gq, gk, gv)):
        for p in range(3):
            mine, got = (a_mine, a_got) if p == 0 else (c_mine, c_got)
            at = n * tall + (cols if p == 2 else 0)
            both(ref, p * tall, mine[:size, at : at + tall], got[:size, at : at + tall])
    both(go, 0, a_mine[:, cols:], a_got[:, cols:])
    total = c_mine[size:].astype(F32) + c_got[size:].astype(F32)
    row = 0
    for ref in outs:
        n = ref.shape[0]
        parts = n * (width // size) // width
        line = jnp.concatenate([total[row + i : row + i + 1] for i in range(parts)], axis=1)
        row += parts
        picked = jnp.zeros((1, n), F32)
        for s in range(width // size):
            picked = jnp.where(b == s, line[:, s * n : (s + 1) * n], picked)
        ref[...] = picked[0]
    begin((), stores)


def finish(where, mine, got, in_own, in_got, lengths, after=()):
    whole = lambda *s: pl.BlockSpec(s, lambda i, w: (0,) * len(s))
    anywhere = pl.BlockSpec(memory_space=pl.ANY)
    size = mine[0].shape[0]
    width = mine[1].shape[1]
    rows = in_got.shape[0]
    return call(
        finish_kernel, where, (*mine, *got, in_own, in_got), after,
        grid=(1,),
        in_specs=[whole(*v.shape) for v in (*mine, *got)] + [anywhere] * 2,
        out_specs=[anywhere] + [whole(size, width)] * 4 + [whole(n) for n in lengths],
        out_shape=[SDS((2 * rows,) + in_got.shape[1:], LOW)]
        + [SDS((size, width), F32)] * 4
        + [SDS((n,), F32) for n in lengths],
        scratch=[pltpu.VMEM((2,) + in_got.shape, LOW), pltpu.SemaphoreType.DMA((4,))],
        us=2,
        name="finish",
        mib=16,
    )


def swap(v, axis, mask, size):
    return lax.ppermute(v, axis, [(i, i ^ mask) for i in range(size)])


def add_low(a, b):
    return (a.astype(F32) + b.astype(F32)).astype(LOW)


def fix(v):
    return lax.optimization_barrier(v)


ORDERS = ("x1y2g", "1xy2g", "y1x2g", "x12y")
BITS = {"x": 0, "1": 1, "2": 2}


def solution(mesh):
    batch_size = mesh.shape["batch"]
    blk_size = mesh.shape["blk"]
    direct = batch_size == 8
    shards = batch_size if direct else 1

    def blk_swap(v, mask):
        return swap(v, "blk", mask, blk_size)

    def hop(v, step):
        if step in BITS:
            return swap(v, "batch", 1 << BITS[step], batch_size)
        return blk_swap(v, 2)

    def split_sum(keep, got):
        half = keep.shape[0] // 2
        return fix(add_low(keep[half:], got[half:])), fix(add_low(keep[:half], got[:half]))

    def per_device(
        tokens, segment_ids, query_weight, query_bias, key_weight, value_weight, value_bias,
        output_weight, output_bias, attn_gain, attn_shift, inner_weight, inner_bias,
        outer_weight, outer_bias, final_gain, final_shift, cotangent,
    ):
        count, span, width = tokens.shape
        rows = count // 2
        me = lax.axis_index("blk")
        b = lax.axis_index("batch")
        core = me & 1
        y = (me >> 1) & 1

        index = jnp.arange(16, dtype=jnp.int32)
        moved = {k: ((index >> (1 + n)) ^ (b >> n)) & 1 for k, n in BITS.items()}
        moved["y"] = (index & 1) ^ y
        maps = []
        for order in ORDERS:
            steps = order[:-1]
            maps.append(sum(moved[k] << (len(steps) - 1 - i) for i, k in enumerate(steps)))
        if not direct:
            maps = [jnp.zeros_like(v) for v in maps]
        where = jnp.concatenate([jnp.stack([core, b, me, y * rows]).astype(jnp.int32)] + maps)

        def mine(v):
            return lax.dynamic_slice_in_dim(v, y * rows, rows, 0)

        def other(v):
            return lax.dynamic_slice_in_dim(v, (1 - y) * rows, rows, 0)

        def halves(own, got, axis):
            return jnp.where(
                core == 0,
                jnp.concatenate([own, got], axis=axis),
                jnp.concatenate([got, own], axis=axis),
            )

        def join_rows(keep, got):
            return jnp.where(
                y == 0, jnp.concatenate([keep, got], axis=0), jnp.concatenate([got, keep], axis=0)
            )

        t1 = blk_swap(other(tokens), 2)
        t0 = mine(tokens)
        t2 = blk_swap(t0, 1)
        t3 = blk_swap(t1, 1)
        x, q, k, v, e, inv, mix_own, mix_out = attend(
            where, (t0, t1, t2, t3), segment_ids,
            query_weight, key_weight, value_weight, query_bias, value_bias,
        )
        c1 = blk_swap(other(cotangent), 2)
        c0 = mine(cotangent)
        mix_sib = blk_swap(mix_out, 1)
        flat = lambda g: g.reshape(-1, g.shape[-1])
        (
            sums, out0, out1, dinner, norm, scale, second, outer_keep, outer_send, inner_keep, inner_send,
        ) = forward(
            where, ORDERS, shards, x, mix_own, mix_sib, c0, c1, output_weight, inner_weight, outer_weight,
            output_bias, attn_gain, attn_shift, inner_bias, outer_bias, final_gain, final_shift,
        )
        outer_keep = flat(outer_keep)
        got = blk_swap(flat(outer_send), 1)
        out_got = blk_swap(out1, 2)
        outer = split_sum(outer_keep, got)
        (inner_send,) = gate(where, (flat(inner_send),), (got,))
        inner = split_sum(flat(inner_keep), blk_swap(inner_send, 1))

        def hops():
            if not direct:
                return (), ()
            steps = (ORDERS[0][stage], ORDERS[1][stage])
            return (hop(outer[0], steps[0]), hop(inner[0], steps[1])), (outer[1], inner[1])

        stage = 0
        got, keeps = hops()
        (vectors, dbranch, dm_own, dm_out, o_keep, o_send), through = branch(
            where, ORDERS, shards, mix_own, mix_sib, attn_gain, sums, dinner, norm, scale,
            second, output_weight, inner_weight, after=(outer[0], inner[0]), thread=(out0,) + keeps,
        )
        out0, keeps = through[0], through[1:]
        dm_sib = blk_swap(dm_out, 1)
        o_got = blk_swap(flat(o_send), 1)
        dbranch = dbranch.reshape(rows, 2 * span, width)
        attention = (q, k, v, e, inv, mix_own, mix_out, dm_own, dm_sib)
        (d0, bias0, a_keep, a_send), keeps = pair_grads(
            where, ORDERS, shards, x, attention, (flat(o_keep), o_got), after=(out_got,), thread=keeps
        )
        if direct:
            outer, inner = (split_sum(keep, g) for keep, g in zip(keeps, got))
        stage = 1
        got, keeps = hops()
        if direct:
            got += (hop(a_send, ORDERS[2][0]),)
            keeps += (a_keep,)
        (in_own, in_out, c_keep, c_send, result), keeps = last_pair_grads(
            where, ORDERS, shards, x, attention, (d0, bias0), dbranch,
            (query_weight, key_weight, value_weight), vectors, out0, out_got, after=(outer[0], inner[0]), thread=keeps,
        )
        in_sum = fix(add_low(in_own, blk_swap(in_out, 1)))

        def join(v, axis):
            v = fix(v)
            return halves(v, blk_swap(v, 1), axis).astype(F32)

        def add_y(g):
            return fix(add_low(g, blk_swap(g, 2)))

        if direct:

            cells = lambda v: v.reshape(4, -1, width)
            pairs = [add_low(cells(keep), cells(g)) for keep, g in zip(keeps[:2], got[:2])]
            both = lambda a, b: fix(jnp.concatenate([p[a:b] for p in pairs], axis=1).reshape(-1, width))
            ffn, ffn_send = both(0, 2), both(2, 4)
            ((ab, ab_send),), (c_send, ffn_send) = next_round(
                where, [(keeps[2:], got[2:], None, True)], after=(ffn,), thread=(c_send, ffn_send)
            )
            c_got, ffn_got, ab_got = hop(c_send, "x"), hop(ffn_send, "y"), hop(ab_send, "1")
            ffn_send, ffn = split_sum(ffn, ffn_got)
            ((c, c_send), (ab, ab_send)), (ffn_send, in_sum) = next_round(
                where, [((c_keep,), (c_got,), c_send, True), ((ab,), (ab_got,), None, True)],
                after=(ffn,), thread=(ffn_send, in_sum),
            )
            in_got = blk_swap(in_sum[:, span:], 2)
            c_got, ffn_got, ab_got = hop(c_send, "1"), hop(ffn_send, "2"), hop(ab_send, "x")
            ((c, c_send), (ab, ab_send), (ffn,)), _ = next_round(
                where,
                [((c,), (c_got,), c_send, True), ((ab,), (ab_got,), None, True), ((ffn,), (ffn_got,), None, False)],
                after=(in_got,),
            )
            c_got, ab_got, ffn_got = hop(c_send, "2"), hop(ab_send, "2"), hop(ffn, "y")
            ((_, c), (ab,)), _ = next_round(
                where, [((c,), (c_got,), c_send, False), ((ab,), (ab_got,), None, False)], after=(ffn_got,)
            )
            c_got, ab_got = hop(c, "y"), hop(ab, "y")
            c = fix(add_low(c, c_got))
            ab = fix(jnp.concatenate([jnp.where(y == 0, ab, ab_got), jnp.where(y == 0, ab_got, ab)], axis=0))
            pair = jnp.stack([ffn, ffn_got])
            ffn = fix(jnp.where(y == 0, pair, pair[::-1]))
            ffn_got = blk_swap(ffn, 1)
            high = ffn.shape[1] // 2
            part = lambda v: v[:, :high].reshape(-1, width)
            outer_done = halves(part(ffn), part(ffn_got), 0).astype(F32)

            def columns(v):
                v = v[:, high:].reshape(2, 2, -1, width)
                return jnp.concatenate([v[:, 0], v[:, 1]], axis=2).reshape(-1, 2 * width)

            inner_done = halves(columns(ffn), columns(ffn_got), 1).astype(F32)
            lengths = [n // shards for n in (width,) * 3 + (inner_weight.shape[1],) + (width,) * 5]
            input_grad, query_done, key_done, value_done, output_done, *vecs = finish(
                where, (ab, c), tuple(blk_swap(g, 1) for g in (ab, c)), in_sum, in_got, lengths,
                after=(outer_done, inner_done),
            )
        else:
            input_grad = join_rows(in_sum[:, :span], blk_swap(in_sum[:, span:], 2))

            def whole(v):
                return add_y(lax.psum_scatter(v, "batch", scatter_dimension=0, tiled=True))

            join_halves = lambda pair: jnp.concatenate([pair[1], pair[0]], axis=0)
            outer_part = join_halves(outer)
            outer_done = whole(halves(outer_part, blk_swap(outer_part, 1), 0)).astype(F32)
            inner_part = join_halves(inner)
            inner_part = jnp.concatenate([inner_part[:width], inner_part[width:]], axis=1)
            inner_done = join(whole(inner_part), 1)
            cols = width // 2
            tall = cols // 3
            whole_a = jnp.concatenate([a_keep, a_send], axis=0)
            whole_c = jnp.concatenate([c_keep, c_send[: c_keep.shape[0]]], axis=0)
            groups = (whole_a, whole_c[:, :cols], whole_c[:, cols:])
            query_done, key_done, value_done = (
                join(whole(jnp.concatenate([g[:, n * tall : (n + 1) * tall] for g in groups], axis=1)), 1)
                for n in range(3)
            )
            output_done = join(whole(whole_a[:, cols:]), 1)
            total = lax.psum(c_send[c_keep.shape[0] :].astype(F32), ("batch", "blk")).reshape(-1)
            vecs = []
            at = 0
            for n in (width,) * 3 + (inner_weight.shape[1],) + (width,) * 5:
                part = total[at : at + n].reshape(batch_size, n // batch_size)
                vecs.append(lax.dynamic_index_in_dim(part, b, 0, keepdims=False))
                at += n
        g_ob, g_ag, g_as, g_b1, g_b2, g_fg, g_fs, g_vb, g_qb = vecs
        return (
            result, input_grad, query_done, g_qb, key_done, value_done, g_vb, output_done, g_ob,
            g_ag, g_as, inner_done, g_b1, outer_done, g_b2, g_fg, g_fs,
        )

    tok = P("batch", "blk", None)
    mat = P("batch", None)
    vec = P("batch")
    return jax.shard_map(
        per_device,
        mesh=mesh,
        in_specs=(tok, P("batch", None)) + (P(),) * 15 + (tok,),
        out_specs=(
            tok, tok, mat, vec, mat, mat, vec, mat, vec, vec, vec, mat, vec, mat, vec, vec, vec,
        ),
        check_vma=False,
    )
```

```python
import functools

import jax
import jax.numpy as jnp
from jax import lax
from jax.experimental import pallas as pl
from jax.experimental.pallas import tpu as pltpu
from jax.sharding import PartitionSpec as P

HD = 64
EPSILON = 1e-12
NEGATIVE = -1e30
LOW = jnp.bfloat16
F32 = jnp.float32
LOG2E = 1.4426950408889634
MIB = 1024 * 1024
COST = 5e7
SDS = jax.ShapeDtypeStruct


def contract(a, b, left, right):
    return lax.dot_general(a, b, (((left,), (right,)), ((), ())), preferred_element_type=F32)


def call(kernel, where, inputs, after, thread=None, *, grid, in_specs, out_specs, out_shape, us, name, scratch=(), mib=62):
    plain = thread is None
    thread = thread or ()
    count = len(inputs)
    extra = len(after) + len(thread)
    outs = len(out_shape)
    anywhere = pl.BlockSpec(memory_space=pl.ANY)

    def body(w, *refs):
        at = count + extra
        kernel(w, *refs[:count], *refs[at : at + outs], *refs[at + outs + len(thread) :])

    got = pl.pallas_call(
        body,
        grid_spec=pltpu.PrefetchScalarGridSpec(
            num_scalar_prefetch=1,
            grid=grid,
            in_specs=list(in_specs) + [anywhere] * extra,
            out_specs=list(out_specs) + [anywhere] * len(thread),
            scratch_shapes=list(scratch),
        ),
        out_shape=list(out_shape) + [SDS(v.shape, v.dtype) for v in thread],
        compiler_params=pltpu.CompilerParams(vmem_limit_bytes=mib * MIB),
        cost_estimate=pl.CostEstimate(flops=int(us * COST), bytes_accessed=0, transcendentals=0),
        input_output_aliases={1 + count + i: outs + i for i in range(len(thread))},
        name=name,
    )(where, *inputs, *thread, *after)
    return got if plain else (got[:outs], tuple(got[outs:]))


def gate(where, thread, after):
    return call(
        lambda where: None, where, (), after, thread, grid=(1,), in_specs=[], out_specs=[], out_shape=[], us=0.1,
        name="gate", mib=16,
    )[1]


def col_sum(v):
    return jnp.sum(v, axis=0, keepdims=True)


def as_column(v, rows):
    return jnp.broadcast_to(v[None, :], (rows, v.shape[0])).T


def attend_kernel(
    where, t0, t1, t2, t3, seg_ref, wq, wk, wv, bq, bv,
    x_out, q_out, k_out, v_out, e_out, inv_out, mix_own, mix_sib, bias,
):
    j = 0
    cols = q_out.shape[1]
    half = mix_own.shape[2]
    heads = e_out.shape[1]

    if True:
        core = where[0]
        x = jnp.concatenate([t0[0], t1[0], t2[0], t3[0]], axis=0)
        x_out[0] = x
        own_part = lambda ref: jnp.where(core == 0, ref[:cols].astype(F32), ref[cols:].astype(F32))
        qb = as_column(own_part(bq), 128)[:, :1]
        vb = as_column(own_part(bv), 128)[:, :1]
        q_out[0] = (contract(wq[...], x, 0, 1) + qb).astype(LOW)
        k_out[0] = contract(wk[...], x, 0, 1).astype(LOW)
        v_out[0] = (contract(wv[...], x, 0, 1) + vb).astype(LOW)
        me, row = where[2], where[3] + pl.program_id(0)
        span = t0.shape[1]
        line = seg_ref[pl.ds(row, 1), :]
        here = [jnp.bitwise_xor(me, r) for r in (0, 2, 1, 3)]
        parts = [line[:, n * span : (n + 1) * span] for n in range(4)]
        pick = lambda q: sum(jnp.where(q == n, part, 0) for n, part in enumerate(parts))
        seg_row = jnp.concatenate([pick(q) for q in here], axis=1).astype(F32)
        seg_col = jnp.broadcast_to(seg_row, (128, seg_row.shape[1])).T[:, :1]
        bias[...] = jnp.where(seg_col == seg_row, 0.0, NEGATIVE)

    for h in range(heads):
        part = slice(h * HD, (h + 1) * HD)
        s = contract(k_out[0, part], q_out[0, part], 0, 0) + bias[...]
        top = jnp.max(s, axis=0, keepdims=True)
        e = jnp.exp2((s - top) * (LOG2E * HD**-0.5))
        low = e.astype(LOW)
        inv = 1.0 / col_sum(e)
        e_out[0, h] = low
        inv_out[0, 8 * (h // 2) + h % 2 : 8 * (h // 2) + h % 2 + 1] = inv
        mixed = (contract(v_out[0, part], low, 1, 0) * inv).astype(LOW)
        mix_own[0, h * HD : (h + 1) * HD] = mixed[:, :half]
        mix_sib[0, h * HD : (h + 1) * HD] = mixed[:, half:]


def attend(where, toks, segments, wq, wk, wv, bq, bv, after=()):
    rows, span, width = toks[0].shape
    length = 4 * span
    cols = width // 2
    heads = cols // HD
    step = heads
    tall = step * HD
    row3 = lambda *s: pl.BlockSpec((1,) + s, lambda t, w: (t,) + (0,) * len(s))
    weight = pl.BlockSpec((width, cols), lambda t, w: (0, w[0]), pipeline_mode=pl.Buffered(1))
    bias = pl.BlockSpec((width,), lambda t, w: (0,))
    mix = pl.BlockSpec((1, tall, length // 2), lambda t, w: (t, 0, 0))
    return call(
        attend_kernel, where, (*toks, segments, wq, wk, wv, bq, bv), after,
        grid=(rows,),
        in_specs=[row3(span, width)] * 4
        + [pl.BlockSpec(segments.shape, lambda t, w: (0, 0)), weight, weight, weight, bias, bias],
        out_specs=[row3(length, width)]
        + [row3(cols, length)] * 3
        + [
            pl.BlockSpec((1, step, length, length), lambda t, w: (t, 0, 0, 0)),
            pl.BlockSpec((1, 24, length), lambda t, w: (t, 0, 0)), mix, mix,
        ],
        out_shape=[SDS((rows, length, width), LOW)]
        + [SDS((rows, cols, length), LOW)] * 3
        + [SDS((rows, heads, length, length), LOW), SDS((rows, 24, length), F32)]
        + [SDS((rows, cols, length // 2), LOW)] * 2,
        scratch=[pltpu.VMEM((length, length), F32)],
        us=18,
        name="attend",
    )


def norm_parts(v):
    center = v - jnp.mean(v, axis=1, keepdims=True)
    spread = jnp.mean(center * center, axis=1, keepdims=True)
    scale = lax.rsqrt(spread + EPSILON)
    return center * scale, scale


def norm_back(dn, n, scale):
    return scale * (
        dn - jnp.mean(dn, axis=1, keepdims=True) - n * jnp.mean(dn * n, axis=1, keepdims=True)
    )


def fold(v):
    return jnp.sum(v.reshape(v.shape[0] // 8, 8, v.shape[1]), axis=0)


TALL = 128
HEAD = 4
TAIL = 16


class Puts:
    def __init__(self, sems):
        self.sems = sems
        self.copies = []

    def __call__(self, src, dst):
        copy = pltpu.make_async_copy(src, dst, self.sems.at[len(self.copies)])
        copy.start()
        self.copies.append(copy)

    def shard(self, where, base, s, src, row, rows, cols, dst):
        if dst.shape[1] == rows:
            at = pl.ds(pl.multiple_of(row, 16), rows)
            self(src.at[at, cols], dst.at[where[base + 2 * s]])
            return
        for k in range(2):
            at = pl.ds(pl.multiple_of(row + k * (rows // 2), 16), rows // 2)
            self(src.at[at, cols], dst.at[where[base + 2 * s + k]])

    def wait(self):
        for copy in self.copies:
            copy.wait()


def place(i, block):
    per = block // TALL
    return i // per, pl.ds(pl.multiple_of((i % per) * TALL, TALL), TALL)


def forward_kernel(
    where, mix_own, mix_sib, bo, ag, ash, b1, b2, fg, fsh,
    x_hbm, c0_hbm, c1_hbm, wo_hbm, w1_hbm, w2_hbm,
    sums, out0, out1, dinner_out, norm_out, scale_out, second_out, keep, send, inner_keep, inner_send,
    wo, w1, w2, x, cot, result, act, slope, dinner, norm1, scale1, first_low, second, douter, bias1, partial,
    in_sem, out_sem, *, shards,
):
    core = where[0]
    rows, block, width = x.shape
    span = block // 2
    half = width // 2
    hidden = w1.shape[1]
    chunks = 3
    step = hidden // chunks
    lines = rows * block // TALL
    vec = lambda ref: ref[...].astype(F32)[None, :]
    own_half = pl.ds(pl.multiple_of(core * half, half), half)
    sib_half = pl.ds(pl.multiple_of((1 - core) * half, half), half)
    loads = [
        pltpu.make_async_copy(wo_hbm, wo, in_sem.at[0]),
        pltpu.make_async_copy(x_hbm.at[:, :block], x, in_sem.at[1]),
        pltpu.make_async_copy(c0_hbm, cot.at[:, :span], in_sem.at[2]),
        pltpu.make_async_copy(c1_hbm, cot.at[:, span:], in_sem.at[3]),
    ]
    for j in range(chunks):
        cols = slice(j * step, (j + 1) * step)
        loads.append(pltpu.make_async_copy(w1_hbm.at[:, cols], w1.at[:, cols], in_sem.at[4 + j]))
    loads.append(pltpu.make_async_copy(w2_hbm, w2, in_sem.at[4 + chunks]))
    for k in (0, 1, 4, 5, 6, 7, 2, 3):
        loads[k].start()
    put = Puts(out_sem)
    bias1[...] = vec(b1)
    partial[...] = jnp.zeros_like(partial)
    loads[0].wait()
    for r in range(rows):
        at = slice(r * block, (r + 1) * block)
        second[at] = contract(mix_own[r], wo[own_half, :], 0, 0) + contract(mix_sib[r], wo[sib_half, :], 0, 0)
    loads[1].wait()

    def norm_first(i, _):
        at = pl.ds(pl.multiple_of(i * TALL, TALL), TALL)
        r, line = place(i, block)
        n1, s1 = norm_parts(x[r, line].astype(F32) + (second[at] + vec(bo)))
        norm1[at] = n1
        scale1[at] = jnp.broadcast_to(s1, (TALL, 128))
        first = n1 * vec(ag) + vec(ash)
        first_low[at] = first.astype(LOW)
        second[at] = first + vec(b2)
        return 0

    lax.fori_loop(0, lines, norm_first, 0, unroll=lines)
    put(norm1, norm_out)
    put(scale1, scale_out)
    for j in range(chunks):
        cols = slice(j * step, (j + 1) * step)
        loads[4 + j].wait()
        inner = contract(first_low[...], w1[:, cols], 1, 0) + bias1[:, cols]
        big = 0.5 + 0.5 * lax.erf(inner * 0.7071067811865476)
        bell = jnp.exp2(inner * inner * (-0.5 * LOG2E)) * 0.3989422804014327
        act[:, cols] = (inner * big).astype(LOW)
        slope[:, cols] = (big + inner * bell).astype(LOW)
    loads[4 + chunks].wait()
    for r in range(rows):
        at = slice(r * block, (r + 1) * block)
        second[at] += contract(act[at], w2[...], 1, 0)
    loads[2].wait()
    loads[3].wait()

    def norm_second(i, _):
        at = pl.ds(pl.multiple_of(i * TALL, TALL), TALL)
        r, line = place(i, block)
        n2, s2 = norm_parts(second[at])
        result[r, line] = (n2 * vec(fg) + vec(fsh)).astype(LOW)
        g = cot[r, line].astype(F32)
        d_second = norm_back(g * vec(fg), n2, s2)
        second[at] = d_second
        d_outer = d_second.astype(LOW)
        douter[at] = d_outer
        partial[:, hidden : hidden + width] += fold(d_outer.astype(F32))
        partial[:, hidden + width : hidden + 2 * width] += fold(g * n2)
        partial[:, hidden + 2 * width :] += fold(g)
        return 0

    lax.fori_loop(0, lines, norm_second, 0, unroll=lines)
    put(second, second_out)
    put(result.at[:, :span], out0)
    put(result.at[:, span:], out1)

    for j in range(chunks):
        cols = slice(j * step, (j + 1) * step)
        di = (contract(douter[...], w2[cols, :], 1, 1) * slope[:, cols].astype(F32)).astype(LOW)
        dinner[:, cols] = di
        partial[:, cols] = fold(di.astype(F32))
        put(dinner.at[:, cols], dinner_out.at[:, cols])
    sums[...] = col_sum(partial[...])

    size = hidden // shards
    part = size // 2
    every = slice(0, width)
    for s in range(shards):
        for piece in range(8 // shards):
            high = hidden // 8
            at = slice(s * size + piece * high, s * size + (piece + 1) * high)
            w2[at, :] = contract(act[:, at], douter[...], 0, 0).astype(LOW)
        put.shard(where, HEAD, s, w2, s * size + (1 - core) * part, part, every, send)
        put.shard(where, HEAD, s, w2, s * size + core * part, part, every, keep)
    wide = hidden // 2
    size = width // shards
    for h in range(2):
        side = jnp.where(core == 0, 1 - h, h)
        at = pl.ds(pl.multiple_of(side * wide, 128), wide)
        w1[:, at] = contract(first_low[...], dinner[:, at], 0, 0).astype(LOW)
        dst = (inner_send, inner_keep)[h]
        pieces = dst.shape[0] // shards
        high = size // pieces
        for s in range(shards):
            for k in range(pieces):
                for n in range(2):
                    cols = pl.ds(pl.multiple_of(side * wide + n * width, 128), width)
                    put(
                        w1.at[pl.ds(s * size + k * high, high), cols],
                        dst.at[where[HEAD + 16 + 2 * s + k], pl.ds(n * high, high)],
                    )
    put.wait()


def entries(order, shards):
    if shards == 1:
        return 1
    return 2 * shards if order[-1] == "g" else shards


def forward(where, orders, shards, x, mix_own, mix_sib, c0, c1, wo, w1, w2, bo, ag, ash, b1, b2, fg, fsh, after=()):
    rows, span, width = c0.shape
    half = 2 * span
    hidden = w1.shape[1]
    tokens = rows * half
    whole = lambda v: pl.BlockSpec(v.shape, lambda i, w: (0,) * len(v.shape))
    anywhere = pl.BlockSpec(memory_space=pl.ANY)
    outs = [SDS((1, hidden + 3 * width), F32)]
    outs += [SDS((rows, span, width), LOW)] * 2 + [SDS((tokens, hidden), LOW)]
    outs += [SDS((tokens, width), F32), SDS((tokens, 128), F32), SDS((tokens, width), F32)]
    n = entries(orders[0], shards)
    outs += [SDS((n, hidden // 2 // n, width), LOW)] * 2
    n = entries(orders[1], shards)
    outs += [SDS((n, 2 * width // n, width), LOW)] * 2
    small = (mix_own, mix_sib, bo, ag, ash, b1, b2, fg, fsh)
    low = lambda *s: pltpu.VMEM(s, LOW)
    wide = lambda *s: pltpu.VMEM(s, F32)
    return call(
        functools.partial(forward_kernel, shards=shards), where, small + (x, c0, c1, wo, w1, w2), after,
        grid=(1,),
        in_specs=[whole(v) for v in small] + [anywhere] * 6,
        out_specs=[whole(outs[0])] + [anywhere] * (len(outs) - 1),
        out_shape=outs,
        scratch=[
            low(width, width), low(width, hidden), low(hidden, width),
            low(rows, half, width), low(rows, half, width), low(rows, half, width),
            low(tokens, hidden), low(tokens, hidden), low(tokens, hidden), wide(tokens, width), wide(tokens, 128),
            low(tokens, width), wide(tokens, width), low(tokens, width), wide(1, hidden), wide(8, hidden + 3 * width),
            pltpu.SemaphoreType.DMA((8,)), pltpu.SemaphoreType.DMA((8 + 12 * shards,)),
        ],
        us=27,
        name="forward",
    )


def branch_kernel(
    where, mix_own, mix_sib, ag, sums_in, dinner_hbm, norm_hbm, scale_hbm, second_hbm,
    wo_hbm, w1_hbm,
    sums, dbranch_out, dm_own, dm_sib, o_keep, o_send,
    wo, w1, dm, dinner, norm1, scale1, second, dbranch, ograd, partial,
    in_sem, out_sem, *, shards,
):
    core = where[0]
    rows = mix_own.shape[0]
    block = mix_own.shape[2]
    width, hidden = w1.shape
    half = width // 2
    chunks = 3
    step = hidden // chunks
    lines = rows * block // TALL
    vec = lambda ref: ref[...].astype(F32)[None, :]
    own_half = pl.ds(pl.multiple_of(core * half, half), half)
    sib_half = pl.ds(pl.multiple_of((1 - core) * half, half), half)
    load_j = []
    for j in range(chunks):
        cols = slice(j * step, (j + 1) * step)
        load_j.append(pltpu.make_async_copy(dinner_hbm.at[:, cols], dinner.at[:, cols], in_sem.at[2 * j]))
        load_j.append(pltpu.make_async_copy(w1_hbm.at[:, cols], w1.at[:, cols], in_sem.at[1 + 2 * j]))
        load_j[-2].start()
        load_j[-1].start()
    pairs = ((second_hbm, second), (norm_hbm, norm1), (scale_hbm, scale1), (wo_hbm, wo))
    late = [pltpu.make_async_copy(src, dst, in_sem.at[6 + k]) for k, (src, dst) in enumerate(pairs)]
    for copy in late:
        copy.start()
    put = Puts(out_sem)
    partial[...] = jnp.zeros_like(partial)
    total = None
    for j in range(chunks):
        cols = slice(j * step, (j + 1) * step)
        load_j[2 * j].wait()
        load_j[2 * j + 1].wait()
        if j == chunks - 1:
            late[0].wait()
        value = contract(dinner[:, cols], w1[:, cols], 1, 1)
        total = value if total is None else total + value
    second[...] += total
    for copy in late[1:]:
        copy.wait()

    def norm_attn(i, _):
        at = pl.ds(pl.multiple_of(i * TALL, TALL), TALL)
        d_first = second[at]
        n1 = norm1[at]
        d_branch = norm_back(d_first * vec(ag), n1, scale1[at][:, :1]).astype(LOW)
        dbranch[at] = d_branch
        partial[:, :width] += fold(d_branch.astype(F32))
        partial[:, width : 2 * width] += fold(d_first * n1)
        partial[:, 2 * width : 3 * width] += fold(d_first)
        return 0

    lax.fori_loop(0, lines, norm_attn, 0, unroll=lines)
    put(dbranch, dbranch_out)
    for r in range(rows):
        at = slice(r * block, (r + 1) * block)
        dm[0, r] = contract(wo[own_half, :], dbranch[at], 1, 1).astype(LOW)
        dm[1, r] = contract(wo[sib_half, :], dbranch[at], 1, 1).astype(LOW)
    put(dm.at[1], dm_sib)
    put(dm.at[0], dm_own)
    sums[:, : 3 * width] = col_sum(partial[...])
    sums[:, 3 * width :] = sums_in[...]
    size = width // shards
    for k, mix in enumerate((mix_own, mix_sib)):
        value = contract(mix[0], dbranch[:block], 1, 0)
        for r in range(1, rows):
            value += contract(mix[r], dbranch[r * block : (r + 1) * block], 1, 0)
        ograd[own_half if k == 0 else sib_half, :] = value.astype(LOW)
    for s in range(shards):
        put.shard(where, HEAD + 16 * 2, s, ograd, s * size, size, sib_half, o_send)
        put.shard(where, HEAD + 16 * 2, s, ograd, s * size, size, own_half, o_keep)
    put.wait()


def branch(
    where, orders, shards, mix_own, mix_sib, ag, sums, dinner, norm, scale, second, wo, w1, after=(), thread=()
):
    rows, cols, half = mix_own.shape
    width, hidden = w1.shape
    tokens = rows * half
    whole = lambda v: pl.BlockSpec(v.shape, lambda i, w: (0,) * len(v.shape))
    anywhere = pl.BlockSpec(memory_space=pl.ANY)
    outs = [SDS((1, 6 * width + hidden), F32), SDS((tokens, width), LOW)] + [SDS((rows, cols, half), LOW)] * 2
    n = entries(orders[2], shards)
    outs += [SDS((n, width // n, cols), LOW)] * 2
    small = (mix_own, mix_sib, ag, sums)
    big = (dinner, norm, scale, second, wo, w1)
    low = lambda *s: pltpu.VMEM(s, LOW)
    wide = lambda *s: pltpu.VMEM(s, F32)
    return call(
        functools.partial(branch_kernel, shards=shards), where, small + big, after, thread,
        grid=(1,),
        in_specs=[whole(v) for v in small] + [anywhere] * len(big),
        out_specs=[whole(outs[0])] + [anywhere] * (len(outs) - 1),
        out_shape=outs,
        scratch=[
            low(width, width), low(width, hidden), low(2, rows, cols, half), low(tokens, hidden),
            wide(tokens, width), wide(tokens, 128), wide(tokens, width), low(tokens, width),
            low(width, width), wide(8, 3 * width),
            pltpu.SemaphoreType.DMA((10,)), pltpu.SemaphoreType.DMA((3 + 4 * shards,)),
        ],
        us=13,
        name="branch",
    )


def spread(where, dst, src, order, n, shards, lanes):
    width = src.shape[0]
    size = width // shards
    if shards == 1:
        dst[:width, lanes] = src[...].astype(LOW)
        return
    cut = 2 if order[-1] == "g" else 1
    high = size // cut
    for s in range(shards):
        for k in range(cut):
            start = pl.multiple_of(where[HEAD + 16 * n + 2 * s + k] * high, 16)
            row = s * size + k * high
            dst[pl.ds(start, high), lanes] = src[row : row + high].astype(LOW)


def pair_back(step_refs, grads, acc, bias, first):
    x_ref, q_ref, k_ref, v_ref, e_ref, inv_ref, mix_own, mix_sib, dm_own, dm_sib = step_refs
    scale = HD**-0.5
    tall = q_ref.shape[1]
    for h in range(tall // HD):
        part = slice(h * HD, (h + 1) * HD)
        mixed = jnp.concatenate([mix_own[0, part], mix_sib[0, part]], axis=1)
        dm = jnp.concatenate([dm_own[0, part], dm_sib[0, part]], axis=1)
        line = 8 * (h // 2) + h % 2
        d_out = dm.astype(F32) * inv_ref[0, line : line + 1]
        delta = col_sum(d_out * mixed.astype(F32))
        d_low = d_out.astype(LOW)
        e = e_ref[0, h]
        dp = contract(v_ref[0, part], d_low, 0, 0)
        ds = (e.astype(F32) * (dp - delta)).astype(LOW)
        base = (h // 2) * 6 * HD + (h % 2) * HD
        at = lambda n: slice(base + 2 * n * HD, base + (2 * n + 1) * HD)
        grads[at(0)] = (contract(k_ref[0, part], ds, 1, 0) * scale).astype(LOW)
        grads[at(1)] = (contract(q_ref[0, part], ds, 1, 1) * scale).astype(LOW)
        grads[at(2)] = contract(d_low, e, 1, 1).astype(LOW)
    value = contract(x_ref[0], grads[...], 0, 1)
    ones = jnp.ones((8, x_ref.shape[1]), LOW)
    sums = contract(ones, grads[...], 1, 1)
    acc[...] = jnp.where(first, value, acc[...] + value)
    bias[...] = jnp.where(first, sums, bias[...] + sums)


def send_off(packed, keep, send, sems):
    put = Puts(sems)
    half = keep.shape[0]
    put(packed.at[half:], send)
    put(packed.at[:half], keep)
    put.wait()


def pair_kernel(where, *refs, orders, shards, with_o):
    step_refs, refs = refs[:10], refs[10:]
    if with_o:
        o_keep, o_got, *refs = refs
    d_out, bias, keep, send, acc, packed, sems = refs
    r = pl.program_id(0)
    pair_back(step_refs, d_out.at[0], acc, bias, r == 0)

    @pl.when(r == pl.num_programs(0) - 1)
    def _():
        cols = acc.shape[1]
        spread(where, packed, acc, orders[2], 2, shards, slice(0, cols))
        if with_o:
            packed[:, cols:] = (o_keep[...].astype(F32) + o_got[...].astype(F32)).astype(LOW)
        send_off(packed, keep, send, sems)


def join_copies(where, own, got, room, whole, sems):
    rows = own.shape[0]
    mine = pl.ds(where[3], rows)
    theirs = pl.ds(rows - where[3], rows)
    loads = [pltpu.make_async_copy(v, room.at[n], sems.at[n]) for n, v in enumerate((own, got))]
    stores = [pltpu.make_async_copy(room.at[n], whole.at[at], sems.at[2 + n]) for n, at in enumerate((mine, theirs))]
    return loads, stores


def begin(copies, others=()):
    for copy in others:
        copy.wait()
    for copy in copies:
        copy.start()


def last_pairs_kernel(where, *refs, orders, shards):
    step_refs, refs = refs[:10], refs[10:]
    d0, bias0, dbranch, wq, wk, wv, vectors, out_own, out_got, *refs = refs
    in_own, in_out, keep, send, result, grads, dq, dk, dv, acc, bias, packed, sems, room, join_sems = refs
    loads, stores = join_copies(where, out_own, out_got, room, result, join_sems)
    t = pl.program_id(0)
    cols = acc.shape[1] // 2
    tall = cols // 3
    pl.when(t == 0)(lambda: begin(loads))
    pl.when(t == 1)(lambda: begin(stores, loads))
    pair_back(step_refs, grads, acc, bias, t == 0)
    for n, d in enumerate((dq, dk, dv)):
        for p in range(2):
            d[p * tall : (p + 1) * tall] = grads[p * cols + n * tall : p * cols + (n + 1) * tall]
        d[2 * tall :] = d0[0, n * tall : (n + 1) * tall]
    back = contract(dq[...], wq[...], 0, 1)
    back = back + contract(dk[...], wk[...], 0, 1) + contract(dv[...], wv[...], 0, 1)
    half = back.shape[0] // 2
    in_own[0] = (back[:half] + dbranch[0].astype(F32)).astype(LOW)
    in_out[0] = back[half:].astype(LOW)

    @pl.when(t == pl.num_programs(0) - 1)
    def _():
        core = where[0]
        wide = 2 * cols
        spread(where, packed, acc, orders[3], 3, shards, slice(0, wide))
        lines = [vectors[:, n * wide : (n + 1) * wide] for n in range(vectors.shape[1] // wide)]
        zero = jnp.zeros((1, cols), F32)
        for n in (2, 0):
            at = lambda p: slice(p * cols + n * tall, p * cols + (n + 1) * tall)
            line = jnp.concatenate([bias[:1, at(0)], bias[:1, at(1)], bias0[:1, n * tall : (n + 1) * tall]], axis=1)
            lines.append(jnp.concatenate([jnp.where(core == c, line, zero) for c in range(2)], axis=1))
        lines.append(jnp.zeros((TAIL - len(lines), wide), F32))
        packed[packed.shape[0] - TAIL :] = jnp.concatenate(lines, axis=0).astype(LOW)
        send_off(packed, keep, send, sems)
        begin((), stores)


def pair_specs(pairs, at, x, attention):
    rows, cols, length = attention[0].shape
    width = x.shape[2]
    step = 2 * pairs
    tall = step * HD
    row3 = lambda *s: pl.BlockSpec((1,) + s, lambda t, w: (t,) + (0,) * len(s))
    big = pl.BlockSpec((1, tall, length), lambda t, w: (t, at, 0))
    small = pl.BlockSpec((1, tall, length // 2), lambda t, w: (t, at, 0))
    inv = pl.BlockSpec((1, 8 * pairs, length), lambda t, w: (t, at, 0))
    specs = [row3(length, width)] + [big] * 3
    specs += [pl.BlockSpec((1, step, length, length), lambda t, w: (t, at, 0, 0)), inv]
    return specs + [small] * 4, row3


def pair_grads(where, orders, shards, x, attention, o=(), after=(), thread=()):
    rows, cols, length = attention[0].shape
    width = x.shape[2]
    specs, row3 = pair_specs(1, 2, x, attention)
    whole = lambda v: pl.BlockSpec(v.shape, lambda r, w: (0,) * len(v.shape))
    anywhere = pl.BlockSpec(memory_space=pl.ANY)
    total = cols + sum(v.shape[1] for v in o[:1])
    outs = [SDS((rows, cols, length), LOW), SDS((8, cols), F32)] + [SDS((width // 2, total), LOW)] * 2
    return call(
        functools.partial(pair_kernel, orders=orders, shards=shards, with_o=bool(o)), where,
        (x, *attention, *o), after, thread,
        grid=(rows,),
        in_specs=specs + [whole(v) for v in o],
        out_specs=[row3(cols, length), whole(outs[1]), anywhere, anywhere],
        out_shape=outs,
        scratch=[pltpu.VMEM((width, cols), F32), pltpu.VMEM((width, total), LOW), pltpu.SemaphoreType.DMA((2,))],
        us=8,
        name="pair_grads",
    )


def last_pair_grads(
    where, orders, shards, x, attention, first, dbranch, weights, vectors, out_own, out_got, after=(), thread=()
):
    rows, cols, length = attention[0].shape
    width = x.shape[2]
    specs, row3 = pair_specs(2, 0, x, attention)
    whole = lambda v: pl.BlockSpec(v.shape, lambda t, w: (0,) * len(v.shape))
    weight = pl.BlockSpec((width, cols), lambda t, w: (0, w[0]), pipeline_mode=pl.Buffered(1))
    anywhere = pl.BlockSpec(memory_space=pl.ANY)
    low = lambda *s: pltpu.VMEM(s, LOW)
    half = width // 2
    d0, bias0 = first
    return call(
        functools.partial(last_pairs_kernel, orders=orders, shards=shards), where,
        (x, *attention, d0, bias0, dbranch, *weights, vectors, out_own, out_got), after, thread,
        grid=(rows,),
        in_specs=specs
        + [row3(cols, length), whole(bias0), row3(length // 2, width), weight, weight, weight, whole(vectors)]
        + [anywhere] * 2,
        out_specs=[row3(length // 2, width)] * 2 + [anywhere] * 3,
        out_shape=[SDS((rows, length // 2, width), LOW)] * 2
        + [SDS((half, 2 * cols), LOW), SDS((half + TAIL, 2 * cols), LOW)]
        + [SDS((2 * rows,) + out_own.shape[1:], LOW)],
        scratch=[low(2 * cols, length)]
        + [low(cols, length)] * 3
        + [pltpu.VMEM((width, 2 * cols), F32), pltpu.VMEM((8, 2 * cols), F32), low(width + TAIL, 2 * cols)]
        + [pltpu.SemaphoreType.DMA((2,)), low(2, *out_own.shape), pltpu.SemaphoreType.DMA((4,))],
        us=20,
        name="last_pair_grads",
    )


def round_kernel(where, *refs, groups):
    add = lambda a, b: (a.astype(F32) + b.astype(F32)).astype(LOW)
    ins = sum(2 * n + tail for n, tail, _ in groups)
    outs = list(refs[ins:])
    refs = list(refs[:ins])
    for n, tail, split in groups:
        keeps, gots = refs[:n], refs[n : 2 * n]
        sent = refs[2 * n] if tail else None
        refs = refs[2 * n + tail :]
        out_keep = outs.pop(0)
        out_send = outs.pop(0) if split or tail else None
        at = 0
        for keep, got in zip(keeps, gots):
            rows, cols = keep.shape
            half = out_keep.shape[0]
            lanes = slice(at, at + cols)
            at += cols
            out_keep[:, lanes] = add(keep[:half], got[:half])
            if split:
                out_send[: rows - half, lanes] = add(keep[half:], got[half:rows])
            elif tail:
                out_send[:rows, lanes] = out_keep[...]
        if tail:
            end = lambda ref: ref[ref.shape[0] - TAIL :]
            out_send[out_send.shape[0] - TAIL :] = add(end(sent), end(gots[0]))


def next_round(where, groups, after=(), thread=()):
    whole = lambda v: pl.BlockSpec(v.shape, lambda i, w: (0,) * len(v.shape))
    ins, outs, form, counts = [], [], [], []
    for keeps, gots, sent, split in groups:
        tail = sent is not None
        ins += [*keeps, *gots] + ([sent] if tail else [])
        rows = keeps[0].shape[0]
        cols = sum(v.shape[1] for v in keeps)
        half = rows // 2 if split else rows
        new = [SDS((half, cols), LOW)]
        if split or tail:
            new.append(SDS((half + (TAIL if tail else 0), cols), LOW))
        outs += new
        counts.append(len(new))
        form.append((len(keeps), int(tail), split))
    got, thread = call(
        functools.partial(round_kernel, groups=tuple(form)), where, ins, after, thread,
        grid=(1,),
        in_specs=[whole(v) for v in ins],
        out_specs=[whole(v) for v in outs],
        out_shape=outs,
        us=1,
        name="next_round",
        mib=16,
    )
    results = []
    for n in counts:
        results.append(tuple(got[:n]))
        got = got[n:]
    return results, thread


def finish_kernel(where, a_mine, c_mine, a_got, c_got, in_own, in_got, joined, gq, gk, gv, go, *outs):
    *outs, room, sems = outs
    loads, stores = join_copies(where, in_own.at[:, : joined.shape[1]], in_got, room, joined, sems)
    begin(loads)
    begin(stores, loads)
    core = where[0]
    b = where[1]
    size, width = gq.shape
    cols = width // 2
    tall = cols // 3

    def both(ref, at, mine, got):
        mine, got = mine.astype(F32), got.astype(F32)
        n = mine.shape[1]
        ref[:, at : at + n] = jnp.where(core == 0, mine, got)
        ref[:, cols + at : cols + at + n] = jnp.where(core == 0, got, mine)

    for n, ref in enumerate((gq, gk, gv)):
        for p in range(3):
            mine, got = (a_mine, a_got) if p == 2 else (c_mine, c_got)
            at = n * tall + (cols if p == 1 else 0)
            both(ref, p * tall, mine[:size, at : at + tall], got[:size, at : at + tall])
    both(go, 0, a_mine[:, cols:], a_got[:, cols:])
    total = c_mine[size:].astype(F32) + c_got[size:].astype(F32)
    row = 0
    for ref in outs:
        n = ref.shape[0]
        parts = n * (width // size) // width
        line = jnp.concatenate([total[row + i : row + i + 1] for i in range(parts)], axis=1)
        row += parts
        picked = jnp.zeros((1, n), F32)
        for s in range(width // size):
            picked = jnp.where(b == s, line[:, s * n : (s + 1) * n], picked)
        ref[...] = picked[0]
    begin((), stores)


def finish(where, mine, got, in_own, in_got, lengths, after=()):
    whole = lambda *s: pl.BlockSpec(s, lambda i, w: (0,) * len(s))
    anywhere = pl.BlockSpec(memory_space=pl.ANY)
    size = mine[0].shape[0]
    width = mine[1].shape[1]
    rows = in_got.shape[0]
    return call(
        finish_kernel, where, (*mine, *got, in_own, in_got), after,
        grid=(1,),
        in_specs=[whole(*v.shape) for v in (*mine, *got)] + [anywhere] * 2,
        out_specs=[anywhere] + [whole(size, width)] * 4 + [whole(n) for n in lengths],
        out_shape=[SDS((2 * rows,) + in_got.shape[1:], LOW)]
        + [SDS((size, width), F32)] * 4
        + [SDS((n,), F32) for n in lengths],
        scratch=[pltpu.VMEM((2,) + in_got.shape, LOW), pltpu.SemaphoreType.DMA((4,))],
        us=2,
        name="finish",
        mib=16,
    )


def swap(v, axis, mask, size):
    return lax.ppermute(v, axis, [(i, i ^ mask) for i in range(size)])


def add_low(a, b):
    return (a.astype(F32) + b.astype(F32)).astype(LOW)


def fix(v):
    return lax.optimization_barrier(v)


ORDERS = ("x1y2g", "1xy2g", "y1x2g", "x12y")
BITS = {"x": 0, "1": 1, "2": 2}


def solution(mesh):
    batch_size = mesh.shape["batch"]
    blk_size = mesh.shape["blk"]
    direct = batch_size == 8
    shards = batch_size if direct else 1

    def blk_swap(v, mask):
        return swap(v, "blk", mask, blk_size)

    def hop(v, step):
        if step in BITS:
            return swap(v, "batch", 1 << BITS[step], batch_size)
        return blk_swap(v, 2)

    def split_sum(keep, got):
        half = keep.shape[0] // 2
        return fix(add_low(keep[half:], got[half:])), fix(add_low(keep[:half], got[:half]))

    def per_device(
        tokens, segment_ids, query_weight, query_bias, key_weight, value_weight, value_bias,
        output_weight, output_bias, attn_gain, attn_shift, inner_weight, inner_bias,
        outer_weight, outer_bias, final_gain, final_shift, cotangent,
    ):
        count, span, width = tokens.shape
        rows = count // 2
        me = lax.axis_index("blk")
        b = lax.axis_index("batch")
        core = me & 1
        y = (me >> 1) & 1

        index = jnp.arange(16, dtype=jnp.int32)
        moved = {k: ((index >> (1 + n)) ^ (b >> n)) & 1 for k, n in BITS.items()}
        moved["y"] = (index & 1) ^ y
        maps = []
        for order in ORDERS:
            steps = order[:-1]
            maps.append(sum(moved[k] << (len(steps) - 1 - i) for i, k in enumerate(steps)))
        if not direct:
            maps = [jnp.zeros_like(v) for v in maps]
        where = jnp.concatenate([jnp.stack([core, b, me, y * rows]).astype(jnp.int32)] + maps)

        def mine(v):
            return lax.dynamic_slice_in_dim(v, y * rows, rows, 0)

        def other(v):
            return lax.dynamic_slice_in_dim(v, (1 - y) * rows, rows, 0)

        def halves(own, got, axis):
            return jnp.where(
                core == 0,
                jnp.concatenate([own, got], axis=axis),
                jnp.concatenate([got, own], axis=axis),
            )

        def join_rows(keep, got):
            return jnp.where(
                y == 0, jnp.concatenate([keep, got], axis=0), jnp.concatenate([got, keep], axis=0)
            )

        t1 = blk_swap(other(tokens), 2)
        t0 = mine(tokens)
        t2 = blk_swap(t0, 1)
        t3 = blk_swap(t1, 1)
        x, q, k, v, e, inv, mix_own, mix_out = attend(
            where, (t0, t1, t2, t3), segment_ids,
            query_weight, key_weight, value_weight, query_bias, value_bias,
        )
        c1 = blk_swap(other(cotangent), 2)
        c0 = mine(cotangent)
        mix_sib = blk_swap(mix_out, 1)
        flat = lambda g: g.reshape(-1, g.shape[-1])
        (
            sums, out0, out1, dinner, norm, scale, second, outer_keep, outer_send, inner_keep, inner_send,
        ) = forward(
            where, ORDERS, shards, x, mix_own, mix_sib, c0, c1, output_weight, inner_weight, outer_weight,
            output_bias, attn_gain, attn_shift, inner_bias, outer_bias, final_gain, final_shift,
        )
        outer_keep = flat(outer_keep)
        got = blk_swap(flat(outer_send), 1)
        out_got = blk_swap(out1, 2)
        outer = split_sum(outer_keep, got)
        (inner_send,) = gate(where, (flat(inner_send),), (got,))
        inner = split_sum(flat(inner_keep), blk_swap(inner_send, 1))

        def hops():
            if not direct:
                return (), ()
            steps = (ORDERS[0][stage], ORDERS[1][stage])
            return (hop(outer[0], steps[0]), hop(inner[0], steps[1])), (outer[1], inner[1])

        stage = 0
        got, keeps = hops()
        (vectors, dbranch, dm_own, dm_out, o_keep, o_send), through = branch(
            where, ORDERS, shards, mix_own, mix_sib, attn_gain, sums, dinner, norm, scale,
            second, output_weight, inner_weight, after=(outer[0], inner[0]), thread=(out0,) + keeps,
        )
        out0, keeps = through[0], through[1:]
        dm_sib = blk_swap(dm_out, 1)
        o_got = blk_swap(flat(o_send), 1)
        dbranch = dbranch.reshape(rows, 2 * span, width)
        attention = (q, k, v, e, inv, mix_own, mix_out, dm_own, dm_sib)
        (d0, bias0, a_keep, a_send), keeps = pair_grads(
            where, ORDERS, shards, x, attention, (flat(o_keep), o_got), after=(out_got,), thread=keeps
        )
        if direct:
            outer, inner = (split_sum(keep, g) for keep, g in zip(keeps, got))
        stage = 1
        got, keeps = hops()
        if direct:
            got += (hop(a_send, ORDERS[2][0]),)
            keeps += (a_keep,)
        (in_own, in_out, c_keep, c_send, result), keeps = last_pair_grads(
            where, ORDERS, shards, x, attention, (d0, bias0), dbranch,
            (query_weight, key_weight, value_weight), vectors, out0, out_got, after=(outer[0], inner[0]), thread=keeps,
        )
        in_sum = fix(add_low(in_own, blk_swap(in_out, 1)))

        def join(v, axis):
            v = fix(v)
            return halves(v, blk_swap(v, 1), axis).astype(F32)

        def add_y(g):
            return fix(add_low(g, blk_swap(g, 2)))

        if direct:

            cells = lambda v: v.reshape(4, -1, width)
            pairs = [add_low(cells(keep), cells(g)) for keep, g in zip(keeps[:2], got[:2])]
            both = lambda a, b: fix(jnp.concatenate([p[a:b] for p in pairs], axis=1).reshape(-1, width))
            ffn, ffn_send = both(0, 2), both(2, 4)
            ((ab, ab_send),), (c_send, ffn_send) = next_round(
                where, [(keeps[2:], got[2:], None, True)], after=(ffn,), thread=(c_send, ffn_send)
            )
            c_got, ffn_got, ab_got = hop(c_send, "x"), hop(ffn_send, "y"), hop(ab_send, "1")
            ffn_send, ffn = split_sum(ffn, ffn_got)
            ((c, c_send), (ab, ab_send)), (ffn_send, in_sum) = next_round(
                where, [((c_keep,), (c_got,), c_send, True), ((ab,), (ab_got,), None, True)],
                after=(ffn,), thread=(ffn_send, in_sum),
            )
            in_got = blk_swap(in_sum[:, span:], 2)
            c_got, ffn_got, ab_got = hop(c_send, "1"), hop(ffn_send, "2"), hop(ab_send, "x")
            ((c, c_send), (ab, ab_send), (ffn,)), _ = next_round(
                where,
                [((c,), (c_got,), c_send, True), ((ab,), (ab_got,), None, True), ((ffn,), (ffn_got,), None, False)],
                after=(in_got,),
            )
            c_got, ab_got, ffn_got = hop(c_send, "2"), hop(ab_send, "2"), hop(ffn, "y")
            ((_, c), (ab,)), _ = next_round(
                where, [((c,), (c_got,), c_send, False), ((ab,), (ab_got,), None, False)], after=(ffn_got,)
            )
            c_got, ab_got = hop(c, "y"), hop(ab, "y")
            c = fix(add_low(c, c_got))
            ab = fix(jnp.concatenate([jnp.where(y == 0, ab, ab_got), jnp.where(y == 0, ab_got, ab)], axis=0))
            pair = jnp.stack([ffn, ffn_got])
            ffn = fix(jnp.where(y == 0, pair, pair[::-1]))
            ffn_got = blk_swap(ffn, 1)
            high = ffn.shape[1] // 2
            part = lambda v: v[:, :high].reshape(-1, width)
            outer_done = halves(part(ffn), part(ffn_got), 0).astype(F32)

            def columns(v):
                v = v[:, high:].reshape(2, 2, -1, width)
                return jnp.concatenate([v[:, 0], v[:, 1]], axis=2).reshape(-1, 2 * width)

            inner_done = halves(columns(ffn), columns(ffn_got), 1).astype(F32)
            lengths = [n // shards for n in (width,) * 3 + (inner_weight.shape[1],) + (width,) * 5]
            input_grad, query_done, key_done, value_done, output_done, *vecs = finish(
                where, (ab, c), tuple(blk_swap(g, 1) for g in (ab, c)), in_sum, in_got, lengths,
                after=(outer_done, inner_done),
            )
        else:
            input_grad = join_rows(in_sum[:, :span], blk_swap(in_sum[:, span:], 2))

            def whole(v):
                return add_y(lax.psum_scatter(v, "batch", scatter_dimension=0, tiled=True))

            join_halves = lambda pair: jnp.concatenate([pair[1], pair[0]], axis=0)
            outer_part = join_halves(outer)
            outer_done = whole(halves(outer_part, blk_swap(outer_part, 1), 0)).astype(F32)
            inner_part = join_halves(inner)
            inner_part = jnp.concatenate([inner_part[:width], inner_part[width:]], axis=1)
            inner_done = join(whole(inner_part), 1)
            cols = width // 2
            tall = cols // 3
            whole_a = jnp.concatenate([a_keep, a_send], axis=0)
            whole_c = jnp.concatenate([c_keep, c_send[: c_keep.shape[0]]], axis=0)
            groups = (whole_c[:, :cols], whole_c[:, cols:], whole_a)
            query_done, key_done, value_done = (
                join(whole(jnp.concatenate([g[:, n * tall : (n + 1) * tall] for g in groups], axis=1)), 1)
                for n in range(3)
            )
            output_done = join(whole(whole_a[:, cols:]), 1)
            total = lax.psum(c_send[c_keep.shape[0] :].astype(F32), ("batch", "blk")).reshape(-1)
            vecs = []
            at = 0
            for n in (width,) * 3 + (inner_weight.shape[1],) + (width,) * 5:
                part = total[at : at + n].reshape(batch_size, n // batch_size)
                vecs.append(lax.dynamic_index_in_dim(part, b, 0, keepdims=False))
                at += n
        g_ob, g_ag, g_as, g_b1, g_b2, g_fg, g_fs, g_vb, g_qb = vecs
        return (
            result, input_grad, query_done, g_qb, key_done, value_done, g_vb, output_done, g_ob,
            g_ag, g_as, inner_done, g_b1, outer_done, g_b2, g_fg, g_fs,
        )

    tok = P("batch", "blk", None)
    mat = P("batch", None)
    vec = P("batch")
    return jax.shard_map(
        per_device,
        mesh=mesh,
        in_specs=(tok, P("batch", None)) + (P(),) * 15 + (tok,),
        out_specs=(
            tok, tok, mat, vec, mat, mat, vec, mat, vec, vec, vec, mat, vec, mat, vec, vec, vec,
        ),
        check_vma=False,
    )
```

```python
import functools

import jax
import jax.numpy as jnp
from jax import lax
from jax.experimental import pallas as pl
from jax.experimental.pallas import tpu as pltpu
from jax.sharding import PartitionSpec as P

HD = 64
EPSILON = 1e-12
NEGATIVE = -1e30
LOW = jnp.bfloat16
F32 = jnp.float32
LOG2E = 1.4426950408889634
MIB = 1024 * 1024
COST = 5e7
SDS = jax.ShapeDtypeStruct


def contract(a, b, left, right):
    return lax.dot_general(a, b, (((left,), (right,)), ((), ())), preferred_element_type=F32)


def call(kernel, where, inputs, after, thread=None, *, grid, in_specs, out_specs, out_shape, us, name, scratch=(), mib=62):
    plain = thread is None
    thread = thread or ()
    count = len(inputs)
    extra = len(after) + len(thread)
    outs = len(out_shape)
    anywhere = pl.BlockSpec(memory_space=pl.ANY)

    def body(w, *refs):
        at = count + extra
        kernel(w, *refs[:count], *refs[at : at + outs], *refs[at + outs + len(thread) :])

    got = pl.pallas_call(
        body,
        grid_spec=pltpu.PrefetchScalarGridSpec(
            num_scalar_prefetch=1,
            grid=grid,
            in_specs=list(in_specs) + [anywhere] * extra,
            out_specs=list(out_specs) + [anywhere] * len(thread),
            scratch_shapes=list(scratch),
        ),
        out_shape=list(out_shape) + [SDS(v.shape, v.dtype) for v in thread],
        compiler_params=pltpu.CompilerParams(vmem_limit_bytes=mib * MIB),
        cost_estimate=pl.CostEstimate(flops=int(us * COST), bytes_accessed=0, transcendentals=0),
        input_output_aliases={1 + count + i: outs + i for i in range(len(thread))},
        name=name,
    )(where, *inputs, *thread, *after)
    return got if plain else (got[:outs], tuple(got[outs:]))


def gate(where, thread, after):
    return call(
        lambda where: None, where, (), after, thread, grid=(1,), in_specs=[], out_specs=[], out_shape=[], us=0.1,
        name="gate", mib=16,
    )[1]


def col_sum(v):
    return jnp.sum(v, axis=0, keepdims=True)


def as_column(v, rows):
    return jnp.broadcast_to(v[None, :], (rows, v.shape[0])).T


def attend_kernel(
    where, t0, t1, t2, t3, seg_ref, wq, wk, wv, bq, bv,
    x_out, q_out, k_out, v_out, e_out, inv_out, mix_own, mix_sib, bias,
):
    j = 0
    cols = q_out.shape[1]
    half = mix_own.shape[2]
    heads = e_out.shape[1]

    if True:
        core = where[0]
        x = jnp.concatenate([t0[0], t1[0], t2[0], t3[0]], axis=0)
        x_out[0] = x
        own_part = lambda ref: jnp.where(core == 0, ref[:cols].astype(F32), ref[cols:].astype(F32))
        qb = as_column(own_part(bq), 128)[:, :1]
        vb = as_column(own_part(bv), 128)[:, :1]
        q_out[0] = (contract(wq[...], x, 0, 1) + qb).astype(LOW)
        k_out[0] = contract(wk[...], x, 0, 1).astype(LOW)
        v_out[0] = (contract(wv[...], x, 0, 1) + vb).astype(LOW)
        me, row = where[2], where[3] + pl.program_id(0)
        span = t0.shape[1]
        line = seg_ref[pl.ds(row, 1), :]
        here = [jnp.bitwise_xor(me, r) for r in (0, 2, 1, 3)]
        parts = [line[:, n * span : (n + 1) * span] for n in range(4)]
        pick = lambda q: sum(jnp.where(q == n, part, 0) for n, part in enumerate(parts))
        seg_row = jnp.concatenate([pick(q) for q in here], axis=1).astype(F32)
        seg_col = jnp.broadcast_to(seg_row, (128, seg_row.shape[1])).T[:, :1]
        bias[...] = jnp.where(seg_col == seg_row, 0.0, NEGATIVE)

    for h in range(heads):
        part = slice(h * HD, (h + 1) * HD)
        s = contract(k_out[0, part], q_out[0, part], 0, 0) + bias[...]
        top = jnp.max(s, axis=0, keepdims=True)
        e = jnp.exp2((s - top) * (LOG2E * HD**-0.5))
        low = e.astype(LOW)
        inv = 1.0 / col_sum(e)
        e_out[0, h] = low
        inv_out[0, 8 * (h // 2) + h % 2 : 8 * (h // 2) + h % 2 + 1] = inv
        mixed = (contract(v_out[0, part], low, 1, 0) * inv).astype(LOW)
        mix_own[0, h * HD : (h + 1) * HD] = mixed[:, :half]
        mix_sib[0, h * HD : (h + 1) * HD] = mixed[:, half:]


def attend(where, toks, segments, wq, wk, wv, bq, bv, after=()):
    rows, span, width = toks[0].shape
    length = 4 * span
    cols = width // 2
    heads = cols // HD
    step = heads
    tall = step * HD
    row3 = lambda *s: pl.BlockSpec((1,) + s, lambda t, w: (t,) + (0,) * len(s))
    weight = pl.BlockSpec((width, cols), lambda t, w: (0, w[0]), pipeline_mode=pl.Buffered(1))
    bias = pl.BlockSpec((width,), lambda t, w: (0,))
    mix = pl.BlockSpec((1, tall, length // 2), lambda t, w: (t, 0, 0))
    return call(
        attend_kernel, where, (*toks, segments, wq, wk, wv, bq, bv), after,
        grid=(rows,),
        in_specs=[row3(span, width)] * 4
        + [pl.BlockSpec(segments.shape, lambda t, w: (0, 0)), weight, weight, weight, bias, bias],
        out_specs=[row3(length, width)]
        + [row3(cols, length)] * 3
        + [
            pl.BlockSpec((1, step, length, length), lambda t, w: (t, 0, 0, 0)),
            pl.BlockSpec((1, 24, length), lambda t, w: (t, 0, 0)), mix, mix,
        ],
        out_shape=[SDS((rows, length, width), LOW)]
        + [SDS((rows, cols, length), LOW)] * 3
        + [SDS((rows, heads, length, length), LOW), SDS((rows, 24, length), F32)]
        + [SDS((rows, cols, length // 2), LOW)] * 2,
        scratch=[pltpu.VMEM((length, length), F32)],
        us=18,
        name="attend",
    )


def norm_parts(v):
    center = v - jnp.mean(v, axis=1, keepdims=True)
    spread = jnp.mean(center * center, axis=1, keepdims=True)
    scale = lax.rsqrt(spread + EPSILON)
    return center * scale, scale


def norm_back(dn, n, scale):
    return scale * (
        dn - jnp.mean(dn, axis=1, keepdims=True) - n * jnp.mean(dn * n, axis=1, keepdims=True)
    )


def fold(v):
    return jnp.sum(v.reshape(v.shape[0] // 8, 8, v.shape[1]), axis=0)


TALL = 128
HEAD = 4
TAIL = 16


class Puts:
    def __init__(self, sems):
        self.sems = sems
        self.copies = []

    def __call__(self, src, dst):
        copy = pltpu.make_async_copy(src, dst, self.sems.at[len(self.copies)])
        copy.start()
        self.copies.append(copy)

    def shard(self, where, base, s, src, row, rows, cols, dst):
        if dst.shape[1] == rows:
            at = pl.ds(pl.multiple_of(row, 16), rows)
            self(src.at[at, cols], dst.at[where[base + 2 * s]])
            return
        for k in range(2):
            at = pl.ds(pl.multiple_of(row + k * (rows // 2), 16), rows // 2)
            self(src.at[at, cols], dst.at[where[base + 2 * s + k]])

    def wait(self):
        for copy in self.copies:
            copy.wait()


def place(i, block):
    per = block // TALL
    return i // per, pl.ds(pl.multiple_of((i % per) * TALL, TALL), TALL)


def forward_kernel(
    where, mix_own, mix_sib, bo, ag, ash, b1, b2, fg, fsh,
    x_hbm, c0_hbm, c1_hbm, wo_hbm, w1_hbm, w2_hbm,
    sums, out0, out1, dinner_out, norm_out, scale_out, second_out, keep, send, inner_keep, inner_send,
    wo, w1, w2, x, cot, result, act, slope, dinner, norm1, scale1, first_low, second, douter, bias1, partial,
    in_sem, out_sem, *, shards,
):
    core = where[0]
    rows, block, width = x.shape
    span = block // 2
    half = width // 2
    hidden = w1.shape[1]
    chunks = 3
    step = hidden // chunks
    lines = rows * block // TALL
    vec = lambda ref: ref[...].astype(F32)[None, :]
    own_half = pl.ds(pl.multiple_of(core * half, half), half)
    sib_half = pl.ds(pl.multiple_of((1 - core) * half, half), half)
    loads = [
        pltpu.make_async_copy(wo_hbm, wo, in_sem.at[0]),
        pltpu.make_async_copy(x_hbm.at[:, :block], x, in_sem.at[1]),
        pltpu.make_async_copy(c0_hbm, cot.at[:, :span], in_sem.at[2]),
        pltpu.make_async_copy(c1_hbm, cot.at[:, span:], in_sem.at[3]),
    ]
    for j in range(chunks):
        cols = slice(j * step, (j + 1) * step)
        loads.append(pltpu.make_async_copy(w1_hbm.at[:, cols], w1.at[:, cols], in_sem.at[4 + j]))
    loads.append(pltpu.make_async_copy(w2_hbm, w2, in_sem.at[4 + chunks]))
    for k in (0, 1, 4, 5, 6, 7, 2, 3):
        loads[k].start()
    put = Puts(out_sem)
    bias1[...] = vec(b1)
    partial[...] = jnp.zeros_like(partial)
    loads[0].wait()
    for r in range(rows):
        at = slice(r * block, (r + 1) * block)
        second[at] = contract(mix_own[r], wo[own_half, :], 0, 0) + contract(mix_sib[r], wo[sib_half, :], 0, 0)
    loads[1].wait()

    def norm_first(i, _):
        at = pl.ds(pl.multiple_of(i * TALL, TALL), TALL)
        r, line = place(i, block)
        n1, s1 = norm_parts(x[r, line].astype(F32) + (second[at] + vec(bo)))
        norm1[at] = n1
        scale1[at] = jnp.broadcast_to(s1, (TALL, 128))
        first = n1 * vec(ag) + vec(ash)
        first_low[at] = first.astype(LOW)
        second[at] = first + vec(b2)
        return 0

    lax.fori_loop(0, lines, norm_first, 0, unroll=lines)
    put(norm1, norm_out)
    put(scale1, scale_out)
    for j in range(chunks):
        cols = slice(j * step, (j + 1) * step)
        loads[4 + j].wait()
        inner = contract(first_low[...], w1[:, cols], 1, 0) + bias1[:, cols]
        big = 0.5 + 0.5 * lax.erf(inner * 0.7071067811865476)
        bell = jnp.exp2(inner * inner * (-0.5 * LOG2E)) * 0.3989422804014327
        act[:, cols] = (inner * big).astype(LOW)
        slope[:, cols] = (big + inner * bell).astype(LOW)
    loads[4 + chunks].wait()
    for r in range(rows):
        at = slice(r * block, (r + 1) * block)
        second[at] += contract(act[at], w2[...], 1, 0)
    loads[2].wait()
    loads[3].wait()

    def norm_second(i, _):
        at = pl.ds(pl.multiple_of(i * TALL, TALL), TALL)
        r, line = place(i, block)
        n2, s2 = norm_parts(second[at])
        result[r, line] = (n2 * vec(fg) + vec(fsh)).astype(LOW)
        g = cot[r, line].astype(F32)
        d_second = norm_back(g * vec(fg), n2, s2)
        second[at] = d_second
        d_outer = d_second.astype(LOW)
        douter[at] = d_outer
        partial[:, hidden : hidden + width] += fold(d_outer.astype(F32))
        partial[:, hidden + width : hidden + 2 * width] += fold(g * n2)
        partial[:, hidden + 2 * width :] += fold(g)
        return 0

    lax.fori_loop(0, lines, norm_second, 0, unroll=lines)
    put(second, second_out)
    put(result.at[:, :span], out0)
    put(result.at[:, span:], out1)

    for j in range(chunks):
        cols = slice(j * step, (j + 1) * step)
        di = (contract(douter[...], w2[cols, :], 1, 1) * slope[:, cols].astype(F32)).astype(LOW)
        dinner[:, cols] = di
        partial[:, cols] = fold(di.astype(F32))
        put(dinner.at[:, cols], dinner_out.at[:, cols])
    sums[...] = col_sum(partial[...])

    size = hidden // shards
    part = size // 2
    every = slice(0, width)
    for s in range(shards):
        for piece in range(8 // shards):
            high = hidden // 8
            at = slice(s * size + piece * high, s * size + (piece + 1) * high)
            w2[at, :] = contract(act[:, at], douter[...], 0, 0).astype(LOW)
        put.shard(where, HEAD, s, w2, s * size + (1 - core) * part, part, every, send)
        put.shard(where, HEAD, s, w2, s * size + core * part, part, every, keep)
    wide = hidden // 2
    size = width // shards
    for h in range(2):
        side = jnp.where(core == 0, 1 - h, h)
        at = pl.ds(pl.multiple_of(side * wide, 128), wide)
        w1[:, at] = contract(first_low[...], dinner[:, at], 0, 0).astype(LOW)
        dst = (inner_send, inner_keep)[h]
        pieces = dst.shape[0] // shards
        high = size // pieces
        for s in range(shards):
            for k in range(pieces):
                for n in range(2):
                    cols = pl.ds(pl.multiple_of(side * wide + n * width, 128), width)
                    put(
                        w1.at[pl.ds(s * size + k * high, high), cols],
                        dst.at[where[HEAD + 16 + 2 * s + k], pl.ds(n * high, high)],
                    )
    put.wait()


def entries(order, shards):
    if shards == 1:
        return 1
    return 2 * shards if order[-1] == "g" else shards


def forward(where, orders, shards, x, mix_own, mix_sib, c0, c1, wo, w1, w2, bo, ag, ash, b1, b2, fg, fsh, after=()):
    rows, span, width = c0.shape
    half = 2 * span
    hidden = w1.shape[1]
    tokens = rows * half
    whole = lambda v: pl.BlockSpec(v.shape, lambda i, w: (0,) * len(v.shape))
    anywhere = pl.BlockSpec(memory_space=pl.ANY)
    outs = [SDS((1, hidden + 3 * width), F32)]
    outs += [SDS((rows, span, width), LOW)] * 2 + [SDS((tokens, hidden), LOW)]
    outs += [SDS((tokens, width), F32), SDS((tokens, 128), F32), SDS((tokens, width), F32)]
    n = entries(orders[0], shards)
    outs += [SDS((n, hidden // 2 // n, width), LOW)] * 2
    n = entries(orders[1], shards)
    outs += [SDS((n, 2 * width // n, width), LOW)] * 2
    small = (mix_own, mix_sib, bo, ag, ash, b1, b2, fg, fsh)
    low = lambda *s: pltpu.VMEM(s, LOW)
    wide = lambda *s: pltpu.VMEM(s, F32)
    return call(
        functools.partial(forward_kernel, shards=shards), where, small + (x, c0, c1, wo, w1, w2), after,
        grid=(1,),
        in_specs=[whole(v) for v in small] + [anywhere] * 6,
        out_specs=[whole(outs[0])] + [anywhere] * (len(outs) - 1),
        out_shape=outs,
        scratch=[
            low(width, width), low(width, hidden), low(hidden, width),
            low(rows, half, width), low(rows, half, width), low(rows, half, width),
            low(tokens, hidden), low(tokens, hidden), low(tokens, hidden), wide(tokens, width), wide(tokens, 128),
            low(tokens, width), wide(tokens, width), low(tokens, width), wide(1, hidden), wide(8, hidden + 3 * width),
            pltpu.SemaphoreType.DMA((8,)), pltpu.SemaphoreType.DMA((8 + 12 * shards,)),
        ],
        us=27,
        name="forward",
    )


def branch_kernel(
    where, mix_own, mix_sib, ag, sums_in, dinner_hbm, norm_hbm, scale_hbm, second_hbm,
    wo_hbm, w1_hbm,
    sums, dbranch_out, dm_own, dm_sib, o_keep, o_send,
    wo, w1, dm, dinner, norm1, scale1, second, dbranch, ograd, partial,
    in_sem, out_sem, *, shards,
):
    core = where[0]
    rows = mix_own.shape[0]
    block = mix_own.shape[2]
    width, hidden = w1.shape
    half = width // 2
    chunks = 3
    step = hidden // chunks
    lines = rows * block // TALL
    vec = lambda ref: ref[...].astype(F32)[None, :]
    own_half = pl.ds(pl.multiple_of(core * half, half), half)
    sib_half = pl.ds(pl.multiple_of((1 - core) * half, half), half)
    load_j = []
    for j in range(chunks):
        cols = slice(j * step, (j + 1) * step)
        load_j.append(pltpu.make_async_copy(dinner_hbm.at[:, cols], dinner.at[:, cols], in_sem.at[2 * j]))
        load_j.append(pltpu.make_async_copy(w1_hbm.at[:, cols], w1.at[:, cols], in_sem.at[1 + 2 * j]))
        load_j[-2].start()
        load_j[-1].start()
    pairs = ((second_hbm, second), (norm_hbm, norm1), (scale_hbm, scale1), (wo_hbm, wo))
    late = [pltpu.make_async_copy(src, dst, in_sem.at[6 + k]) for k, (src, dst) in enumerate(pairs)]
    for copy in late:
        copy.start()
    put = Puts(out_sem)
    partial[...] = jnp.zeros_like(partial)
    total = None
    for j in range(chunks):
        cols = slice(j * step, (j + 1) * step)
        load_j[2 * j].wait()
        load_j[2 * j + 1].wait()
        if j == chunks - 1:
            late[0].wait()
        value = contract(dinner[:, cols], w1[:, cols], 1, 1)
        total = value if total is None else total + value
    second[...] += total
    for copy in late[1:]:
        copy.wait()

    def norm_attn(i, _):
        at = pl.ds(pl.multiple_of(i * TALL, TALL), TALL)
        d_first = second[at]
        n1 = norm1[at]
        d_branch = norm_back(d_first * vec(ag), n1, scale1[at][:, :1]).astype(LOW)
        dbranch[at] = d_branch
        partial[:, :width] += fold(d_branch.astype(F32))
        partial[:, width : 2 * width] += fold(d_first * n1)
        partial[:, 2 * width : 3 * width] += fold(d_first)
        return 0

    lax.fori_loop(0, lines, norm_attn, 0, unroll=lines)
    put(dbranch, dbranch_out)
    for r in range(rows):
        at = slice(r * block, (r + 1) * block)
        dm[0, r] = contract(wo[own_half, :], dbranch[at], 1, 1).astype(LOW)
        dm[1, r] = contract(wo[sib_half, :], dbranch[at], 1, 1).astype(LOW)
    put(dm.at[1], dm_sib)
    put(dm.at[0], dm_own)
    sums[:, : 3 * width] = col_sum(partial[...])
    sums[:, 3 * width :] = sums_in[...]
    size = width // shards
    for k, mix in enumerate((mix_own, mix_sib)):
        value = contract(mix[0], dbranch[:block], 1, 0)
        for r in range(1, rows):
            value += contract(mix[r], dbranch[r * block : (r + 1) * block], 1, 0)
        ograd[own_half if k == 0 else sib_half, :] = value.astype(LOW)
    for s in range(shards):
        put.shard(where, HEAD + 16 * 2, s, ograd, s * size, size, sib_half, o_send)
        put.shard(where, HEAD + 16 * 2, s, ograd, s * size, size, own_half, o_keep)
    put.wait()


def branch(
    where, orders, shards, mix_own, mix_sib, ag, sums, dinner, norm, scale, second, wo, w1, after=(), thread=()
):
    rows, cols, half = mix_own.shape
    width, hidden = w1.shape
    tokens = rows * half
    whole = lambda v: pl.BlockSpec(v.shape, lambda i, w: (0,) * len(v.shape))
    anywhere = pl.BlockSpec(memory_space=pl.ANY)
    outs = [SDS((1, 6 * width + hidden), F32), SDS((tokens, width), LOW)] + [SDS((rows, cols, half), LOW)] * 2
    n = entries(orders[2], shards)
    outs += [SDS((n, width // n, cols), LOW)] * 2
    small = (mix_own, mix_sib, ag, sums)
    big = (dinner, norm, scale, second, wo, w1)
    low = lambda *s: pltpu.VMEM(s, LOW)
    wide = lambda *s: pltpu.VMEM(s, F32)
    return call(
        functools.partial(branch_kernel, shards=shards), where, small + big, after, thread,
        grid=(1,),
        in_specs=[whole(v) for v in small] + [anywhere] * len(big),
        out_specs=[whole(outs[0])] + [anywhere] * (len(outs) - 1),
        out_shape=outs,
        scratch=[
            low(width, width), low(width, hidden), low(2, rows, cols, half), low(tokens, hidden),
            wide(tokens, width), wide(tokens, 128), wide(tokens, width), low(tokens, width),
            low(width, width), wide(8, 3 * width),
            pltpu.SemaphoreType.DMA((10,)), pltpu.SemaphoreType.DMA((3 + 4 * shards,)),
        ],
        us=13,
        name="branch",
    )


def spread(where, dst, src, order, n, shards, lanes):
    width = src.shape[0]
    size = width // shards
    if shards == 1:
        dst[:width, lanes] = src[...].astype(LOW)
        return
    cut = 2 if order[-1] == "g" else 1
    high = size // cut
    for s in range(shards):
        for k in range(cut):
            start = pl.multiple_of(where[HEAD + 16 * n + 2 * s + k] * high, 16)
            row = s * size + k * high
            dst[pl.ds(start, high), lanes] = src[row : row + high].astype(LOW)


def pair_back(step_refs, grads, acc, bias, first):
    x_ref, q_ref, k_ref, v_ref, e_ref, inv_ref, mix_own, mix_sib, dm_own, dm_sib = step_refs
    scale = HD**-0.5
    tall = q_ref.shape[1]
    for h in range(tall // HD):
        part = slice(h * HD, (h + 1) * HD)
        mixed = jnp.concatenate([mix_own[0, part], mix_sib[0, part]], axis=1)
        dm = jnp.concatenate([dm_own[0, part], dm_sib[0, part]], axis=1)
        line = 8 * (h // 2) + h % 2
        d_out = dm.astype(F32) * inv_ref[0, line : line + 1]
        delta = col_sum(d_out * mixed.astype(F32))
        d_low = d_out.astype(LOW)
        e = e_ref[0, h]
        dp = contract(v_ref[0, part], d_low, 0, 0)
        ds = (e.astype(F32) * (dp - delta)).astype(LOW)
        base = (h // 2) * 6 * HD + (h % 2) * HD
        at = lambda n: slice(base + 2 * n * HD, base + (2 * n + 1) * HD)
        grads[at(0)] = (contract(k_ref[0, part], ds, 1, 0) * scale).astype(LOW)
        grads[at(1)] = (contract(q_ref[0, part], ds, 1, 1) * scale).astype(LOW)
        grads[at(2)] = contract(d_low, e, 1, 1).astype(LOW)
    value = contract(x_ref[0], grads[...], 0, 1)
    ones = jnp.ones((8, x_ref.shape[1]), LOW)
    sums = contract(ones, grads[...], 1, 1)
    acc[...] = jnp.where(first, value, acc[...] + value)
    bias[...] = jnp.where(first, sums, bias[...] + sums)


def send_off(packed, keep, send, sems):
    put = Puts(sems)
    half = keep.shape[0]
    put(packed.at[half:], send)
    put(packed.at[:half], keep)
    put.wait()


def pair_kernel(where, *refs, orders, shards, with_o):
    step_refs, refs = refs[:10], refs[10:]
    if with_o:
        o_keep, o_got, *refs = refs
    d_out, bias, keep, send, acc, packed, sems = refs
    r = pl.program_id(0)
    pair_back(step_refs, d_out.at[0], acc, bias, r == 0)

    @pl.when(r == pl.num_programs(0) - 1)
    def _():
        cols = acc.shape[1]
        spread(where, packed, acc, orders[2], 2, shards, slice(0, cols))
        if with_o:
            packed[:, cols:] = (o_keep[...].astype(F32) + o_got[...].astype(F32)).astype(LOW)
        send_off(packed, keep, send, sems)


def join_copies(where, own, got, room, whole, sems):
    rows = own.shape[0]
    mine = pl.ds(where[3], rows)
    theirs = pl.ds(rows - where[3], rows)
    loads = [pltpu.make_async_copy(v, room.at[n], sems.at[n]) for n, v in enumerate((own, got))]
    stores = [pltpu.make_async_copy(room.at[n], whole.at[at], sems.at[2 + n]) for n, at in enumerate((mine, theirs))]
    return loads, stores


def begin(copies, others=()):
    for copy in others:
        copy.wait()
    for copy in copies:
        copy.start()


def last_pairs_kernel(where, *refs, orders, shards):
    step_refs, refs = refs[:10], refs[10:]
    d0, bias0, dbranch, wq, wk, wv, vectors, out_own, out_got, *refs = refs
    in_own, in_out, keep, send, result, grads, dq, dk, dv, acc, bias, packed, sems, room, join_sems = refs
    loads, stores = join_copies(where, out_own, out_got, room, result, join_sems)
    t = pl.program_id(0)
    cols = acc.shape[1] // 2
    tall = cols // 3
    pl.when(t == 0)(lambda: begin(loads))
    pl.when(t == 1)(lambda: begin(stores, loads))
    pair_back(step_refs, grads, acc, bias, t == 0)
    for n, d in enumerate((dq, dk, dv)):
        for p in range(2):
            d[p * tall : (p + 1) * tall] = grads[p * cols + n * tall : p * cols + (n + 1) * tall]
        d[2 * tall :] = d0[0, n * tall : (n + 1) * tall]
    back = contract(dq[...], wq[...], 0, 1)
    back = back + contract(dk[...], wk[...], 0, 1) + contract(dv[...], wv[...], 0, 1)
    half = back.shape[0] // 2
    in_own[0] = (back[:half] + dbranch[0].astype(F32)).astype(LOW)
    in_out[0] = back[half:].astype(LOW)

    @pl.when(t == pl.num_programs(0) - 1)
    def _():
        core = where[0]
        wide = 2 * cols
        spread(where, packed, acc, orders[3], 3, shards, slice(0, wide))
        lines = [vectors[:, n * wide : (n + 1) * wide] for n in range(vectors.shape[1] // wide)]
        zero = jnp.zeros((1, cols), F32)
        for n in (2, 0):
            at = lambda p: slice(p * cols + n * tall, p * cols + (n + 1) * tall)
            line = jnp.concatenate([bias[:1, at(0)], bias[:1, at(1)], bias0[:1, n * tall : (n + 1) * tall]], axis=1)
            lines.append(jnp.concatenate([jnp.where(core == c, line, zero) for c in range(2)], axis=1))
        lines.append(jnp.zeros((TAIL - len(lines), wide), F32))
        packed[packed.shape[0] - TAIL :] = jnp.concatenate(lines, axis=0).astype(LOW)
        send_off(packed, keep, send, sems)
        begin((), stores)


def pair_specs(pairs, at, x, attention):
    rows, cols, length = attention[0].shape
    width = x.shape[2]
    step = 2 * pairs
    tall = step * HD
    row3 = lambda *s: pl.BlockSpec((1,) + s, lambda t, w: (t,) + (0,) * len(s))
    big = pl.BlockSpec((1, tall, length), lambda t, w: (t, at, 0))
    small = pl.BlockSpec((1, tall, length // 2), lambda t, w: (t, at, 0))
    inv = pl.BlockSpec((1, 8 * pairs, length), lambda t, w: (t, at, 0))
    specs = [row3(length, width)] + [big] * 3
    specs += [pl.BlockSpec((1, step, length, length), lambda t, w: (t, at, 0, 0)), inv]
    return specs + [small] * 4, row3


def pair_grads(where, orders, shards, x, attention, o=(), after=(), thread=()):
    rows, cols, length = attention[0].shape
    width = x.shape[2]
    specs, row3 = pair_specs(1, 2, x, attention)
    whole = lambda v: pl.BlockSpec(v.shape, lambda r, w: (0,) * len(v.shape))
    anywhere = pl.BlockSpec(memory_space=pl.ANY)
    total = cols + sum(v.shape[1] for v in o[:1])
    outs = [SDS((rows, cols, length), LOW), SDS((8, cols), F32)] + [SDS((width // 2, total), LOW)] * 2
    return call(
        functools.partial(pair_kernel, orders=orders, shards=shards, with_o=bool(o)), where,
        (x, *attention, *o), after, thread,
        grid=(rows,),
        in_specs=specs + [whole(v) for v in o],
        out_specs=[row3(cols, length), whole(outs[1]), anywhere, anywhere],
        out_shape=outs,
        scratch=[pltpu.VMEM((width, cols), F32), pltpu.VMEM((width, total), LOW), pltpu.SemaphoreType.DMA((2,))],
        us=8,
        name="pair_grads",
    )


def last_pair_grads(
    where, orders, shards, x, attention, first, dbranch, weights, vectors, out_own, out_got, after=(), thread=()
):
    rows, cols, length = attention[0].shape
    width = x.shape[2]
    specs, row3 = pair_specs(2, 0, x, attention)
    whole = lambda v: pl.BlockSpec(v.shape, lambda t, w: (0,) * len(v.shape))
    weight = pl.BlockSpec((width, cols), lambda t, w: (0, w[0]), pipeline_mode=pl.Buffered(1))
    anywhere = pl.BlockSpec(memory_space=pl.ANY)
    low = lambda *s: pltpu.VMEM(s, LOW)
    half = width // 2
    d0, bias0 = first
    return call(
        functools.partial(last_pairs_kernel, orders=orders, shards=shards), where,
        (x, *attention, d0, bias0, dbranch, *weights, vectors, out_own, out_got), after, thread,
        grid=(rows,),
        in_specs=specs
        + [row3(cols, length), whole(bias0), row3(length // 2, width), weight, weight, weight, whole(vectors)]
        + [anywhere] * 2,
        out_specs=[row3(length // 2, width)] * 2 + [anywhere] * 3,
        out_shape=[SDS((rows, length // 2, width), LOW)] * 2
        + [SDS((half, 2 * cols), LOW), SDS((half + TAIL, 2 * cols), LOW)]
        + [SDS((2 * rows,) + out_own.shape[1:], LOW)],
        scratch=[low(2 * cols, length)]
        + [low(cols, length)] * 3
        + [pltpu.VMEM((width, 2 * cols), F32), pltpu.VMEM((8, 2 * cols), F32), low(width + TAIL, 2 * cols)]
        + [pltpu.SemaphoreType.DMA((2,)), low(2, *out_own.shape), pltpu.SemaphoreType.DMA((4,))],
        us=20,
        name="last_pair_grads",
    )


def round_kernel(where, *refs, groups):
    add = lambda a, b: (a.astype(F32) + b.astype(F32)).astype(LOW)
    ins = sum(2 * n + tail for n, tail, _ in groups)
    outs = list(refs[ins:])
    refs = list(refs[:ins])
    for n, tail, split in groups:
        keeps, gots = refs[:n], refs[n : 2 * n]
        sent = refs[2 * n] if tail else None
        refs = refs[2 * n + tail :]
        out_keep = outs.pop(0)
        out_send = outs.pop(0) if split or tail else None
        at = 0
        for keep, got in zip(keeps, gots):
            rows, cols = keep.shape
            half = out_keep.shape[0]
            lanes = slice(at, at + cols)
            at += cols
            out_keep[:, lanes] = add(keep[:half], got[:half])
            if split:
                out_send[: rows - half, lanes] = add(keep[half:], got[half:rows])
            elif tail:
                out_send[:rows, lanes] = out_keep[...]
        if tail:
            end = lambda ref: ref[ref.shape[0] - TAIL :]
            out_send[out_send.shape[0] - TAIL :] = add(end(sent), end(gots[0]))


def next_round(where, groups, after=(), thread=()):
    whole = lambda v: pl.BlockSpec(v.shape, lambda i, w: (0,) * len(v.shape))
    ins, outs, form, counts = [], [], [], []
    for keeps, gots, sent, split in groups:
        tail = sent is not None
        ins += [*keeps, *gots] + ([sent] if tail else [])
        rows = keeps[0].shape[0]
        cols = sum(v.shape[1] for v in keeps)
        half = rows // 2 if split else rows
        new = [SDS((half, cols), LOW)]
        if split or tail:
            new.append(SDS((half + (TAIL if tail else 0), cols), LOW))
        outs += new
        counts.append(len(new))
        form.append((len(keeps), int(tail), split))
    got, thread = call(
        functools.partial(round_kernel, groups=tuple(form)), where, ins, after, thread,
        grid=(1,),
        in_specs=[whole(v) for v in ins],
        out_specs=[whole(v) for v in outs],
        out_shape=outs,
        us=1,
        name="next_round",
        mib=16,
    )
    results = []
    for n in counts:
        results.append(tuple(got[:n]))
        got = got[n:]
    return results, thread


def finish_kernel(where, a_mine, c_mine, a_got, c_got, in_own, in_got, joined, gq, gk, gv, go, *outs):
    *outs, room, sems = outs
    loads, stores = join_copies(where, in_own.at[:, : joined.shape[1]], in_got, room, joined, sems)
    begin(loads)
    begin(stores, loads)
    core = where[0]
    b = where[1]
    size, width = gq.shape
    cols = width // 2
    tall = cols // 3

    def both(ref, at, mine, got):
        mine, got = mine.astype(F32), got.astype(F32)
        n = mine.shape[1]
        ref[:, at : at + n] = jnp.where(core == 0, mine, got)
        ref[:, cols + at : cols + at + n] = jnp.where(core == 0, got, mine)

    for n, ref in enumerate((gq, gk, gv)):
        for p in range(3):
            mine, got = (a_mine, a_got) if p == 2 else (c_mine, c_got)
            at = n * tall + (cols if p == 1 else 0)
            both(ref, p * tall, mine[:size, at : at + tall], got[:size, at : at + tall])
    both(go, 0, a_mine[:, cols:], a_got[:, cols:])
    total = c_mine[size:].astype(F32) + c_got[size:].astype(F32)
    row = 0
    for ref in outs:
        n = ref.shape[0]
        parts = n * (width // size) // width
        line = jnp.concatenate([total[row + i : row + i + 1] for i in range(parts)], axis=1)
        row += parts
        picked = jnp.zeros((1, n), F32)
        for s in range(width // size):
            picked = jnp.where(b == s, line[:, s * n : (s + 1) * n], picked)
        ref[...] = picked[0]
    begin((), stores)


def finish(where, mine, got, in_own, in_got, lengths, after=()):
    whole = lambda *s: pl.BlockSpec(s, lambda i, w: (0,) * len(s))
    anywhere = pl.BlockSpec(memory_space=pl.ANY)
    size = mine[0].shape[0]
    width = mine[1].shape[1]
    rows = in_got.shape[0]
    return call(
        finish_kernel, where, (*mine, *got, in_own, in_got), after,
        grid=(1,),
        in_specs=[whole(*v.shape) for v in (*mine, *got)] + [anywhere] * 2,
        out_specs=[anywhere] + [whole(size, width)] * 4 + [whole(n) for n in lengths],
        out_shape=[SDS((2 * rows,) + in_got.shape[1:], LOW)]
        + [SDS((size, width), F32)] * 4
        + [SDS((n,), F32) for n in lengths],
        scratch=[pltpu.VMEM((2,) + in_got.shape, LOW), pltpu.SemaphoreType.DMA((4,))],
        us=2,
        name="finish",
        mib=16,
    )


def swap(v, axis, mask, size):
    return lax.ppermute(v, axis, [(i, i ^ mask) for i in range(size)])


def add_low(a, b):
    return (a.astype(F32) + b.astype(F32)).astype(LOW)


def fix(v):
    return lax.optimization_barrier(v)


ORDERS = ("x1y2g", "1xy2g", "y1x2g", "x12y")
BITS = {"x": 0, "1": 1, "2": 2}


def solution(mesh):
    batch_size = mesh.shape["batch"]
    blk_size = mesh.shape["blk"]
    direct = batch_size == 8
    shards = batch_size if direct else 1

    def blk_swap(v, mask):
        return swap(v, "blk", mask, blk_size)

    def hop(v, step):
        if step in BITS:
            return swap(v, "batch", 1 << BITS[step], batch_size)
        return blk_swap(v, 2)

    def split_sum(keep, got):
        half = keep.shape[0] // 2
        return fix(add_low(keep[half:], got[half:])), fix(add_low(keep[:half], got[:half]))

    def per_device(
        tokens, segment_ids, query_weight, query_bias, key_weight, value_weight, value_bias,
        output_weight, output_bias, attn_gain, attn_shift, inner_weight, inner_bias,
        outer_weight, outer_bias, final_gain, final_shift, cotangent,
    ):
        count, span, width = tokens.shape
        rows = count // 2
        me = lax.axis_index("blk")
        b = lax.axis_index("batch")
        core = me & 1
        y = (me >> 1) & 1

        index = jnp.arange(16, dtype=jnp.int32)
        moved = {k: ((index >> (1 + n)) ^ (b >> n)) & 1 for k, n in BITS.items()}
        moved["y"] = (index & 1) ^ y
        maps = []
        for order in ORDERS:
            steps = order[:-1]
            maps.append(sum(moved[k] << (len(steps) - 1 - i) for i, k in enumerate(steps)))
        if not direct:
            maps = [jnp.zeros_like(v) for v in maps]
        where = jnp.concatenate([jnp.stack([core, b, me, y * rows]).astype(jnp.int32)] + maps)

        def mine(v):
            return lax.dynamic_slice_in_dim(v, y * rows, rows, 0)

        def other(v):
            return lax.dynamic_slice_in_dim(v, (1 - y) * rows, rows, 0)

        def halves(own, got, axis):
            return jnp.where(
                core == 0,
                jnp.concatenate([own, got], axis=axis),
                jnp.concatenate([got, own], axis=axis),
            )

        def join_rows(keep, got):
            return jnp.where(
                y == 0, jnp.concatenate([keep, got], axis=0), jnp.concatenate([got, keep], axis=0)
            )

        t1 = blk_swap(other(tokens), 2)
        t0 = mine(tokens)
        t2 = blk_swap(t0, 1)
        t3 = blk_swap(t1, 1)
        x, q, k, v, e, inv, mix_own, mix_out = attend(
            where, (t0, t1, t2, t3), segment_ids,
            query_weight, key_weight, value_weight, query_bias, value_bias,
        )
        c1 = blk_swap(other(cotangent), 2)
        c0 = mine(cotangent)
        mix_sib = blk_swap(mix_out, 1)
        flat = lambda g: g.reshape(-1, g.shape[-1])
        (
            sums, out0, out1, dinner, norm, scale, second, outer_keep, outer_send, inner_keep, inner_send,
        ) = forward(
            where, ORDERS, shards, x, mix_own, mix_sib, c0, c1, output_weight, inner_weight, outer_weight,
            output_bias, attn_gain, attn_shift, inner_bias, outer_bias, final_gain, final_shift,
        )
        outer_keep = flat(outer_keep)
        got = blk_swap(flat(outer_send), 1)
        out_got = blk_swap(out1, 2)
        outer = split_sum(outer_keep, got)
        inner_send = flat(inner_send)
        inner = split_sum(flat(inner_keep), blk_swap(inner_send, 1))

        def hops():
            if not direct:
                return (), ()
            steps = (ORDERS[0][stage], ORDERS[1][stage])
            return (hop(outer[0], steps[0]), hop(inner[0], steps[1])), (outer[1], inner[1])

        stage = 0
        got, keeps = hops()
        (vectors, dbranch, dm_own, dm_out, o_keep, o_send), through = branch(
            where, ORDERS, shards, mix_own, mix_sib, attn_gain, sums, dinner, norm, scale,
            second, output_weight, inner_weight, after=(outer[0], inner[0]), thread=(out0,) + keeps,
        )
        out0, keeps = through[0], through[1:]
        dm_sib = blk_swap(dm_out, 1)
        o_got = blk_swap(flat(o_send), 1)
        dbranch = dbranch.reshape(rows, 2 * span, width)
        attention = (q, k, v, e, inv, mix_own, mix_out, dm_own, dm_sib)
        (d0, bias0, a_keep, a_send), keeps = pair_grads(
            where, ORDERS, shards, x, attention, (flat(o_keep), o_got), after=(out_got,), thread=keeps
        )
        if direct:
            outer, inner = (split_sum(keep, g) for keep, g in zip(keeps, got))
        stage = 1
        got, keeps = hops()
        if direct:
            got += (hop(a_send, ORDERS[2][0]),)
            keeps += (a_keep,)
        (in_own, in_out, c_keep, c_send, result), keeps = last_pair_grads(
            where, ORDERS, shards, x, attention, (d0, bias0), dbranch,
            (query_weight, key_weight, value_weight), vectors, out0, out_got, after=(outer[0], inner[0]), thread=keeps,
        )
        in_sum = fix(add_low(in_own, blk_swap(in_out, 1)))

        def join(v, axis):
            v = fix(v)
            return halves(v, blk_swap(v, 1), axis).astype(F32)

        def add_y(g):
            return fix(add_low(g, blk_swap(g, 2)))

        if direct:

            cells = lambda v: v.reshape(4, -1, width)
            pairs = [add_low(cells(keep), cells(g)) for keep, g in zip(keeps[:2], got[:2])]
            both = lambda a, b: fix(jnp.concatenate([p[a:b] for p in pairs], axis=1).reshape(-1, width))
            ffn, ffn_send = both(0, 2), both(2, 4)
            ((ab, ab_send),), (c_send, ffn_send) = next_round(
                where, [(keeps[2:], got[2:], None, True)], after=(ffn,), thread=(c_send, ffn_send)
            )
            c_got, ffn_got, ab_got = hop(c_send, "x"), hop(ffn_send, "y"), hop(ab_send, "1")
            ffn_send, ffn = split_sum(ffn, ffn_got)
            ((c, c_send), (ab, ab_send)), (ffn_send, in_sum) = next_round(
                where, [((c_keep,), (c_got,), c_send, True), ((ab,), (ab_got,), None, True)],
                after=(ffn,), thread=(ffn_send, in_sum),
            )
            in_got = blk_swap(in_sum[:, span:], 2)
            c_got, ffn_got, ab_got = hop(c_send, "1"), hop(ffn_send, "2"), hop(ab_send, "x")
            ((c, c_send), (ab, ab_send), (ffn,)), _ = next_round(
                where,
                [((c,), (c_got,), c_send, True), ((ab,), (ab_got,), None, True), ((ffn,), (ffn_got,), None, False)],
                after=(in_got,),
            )
            c_got, ab_got, ffn_got = hop(c_send, "2"), hop(ab_send, "2"), hop(ffn, "y")
            ((_, c), (ab,)), _ = next_round(
                where, [((c,), (c_got,), c_send, False), ((ab,), (ab_got,), None, False)], after=(ffn_got,)
            )
            c_got, ab_got = hop(c, "y"), hop(ab, "y")
            c = fix(add_low(c, c_got))
            ab = fix(jnp.concatenate([jnp.where(y == 0, ab, ab_got), jnp.where(y == 0, ab_got, ab)], axis=0))
            pair = jnp.stack([ffn, ffn_got])
            ffn = fix(jnp.where(y == 0, pair, pair[::-1]))
            ffn_got = blk_swap(ffn, 1)
            high = ffn.shape[1] // 2
            part = lambda v: v[:, :high].reshape(-1, width)
            outer_done = halves(part(ffn), part(ffn_got), 0).astype(F32)

            def columns(v):
                v = v[:, high:].reshape(2, 2, -1, width)
                return jnp.concatenate([v[:, 0], v[:, 1]], axis=2).reshape(-1, 2 * width)

            inner_done = halves(columns(ffn), columns(ffn_got), 1).astype(F32)
            lengths = [n // shards for n in (width,) * 3 + (inner_weight.shape[1],) + (width,) * 5]
            input_grad, query_done, key_done, value_done, output_done, *vecs = finish(
                where, (ab, c), tuple(blk_swap(g, 1) for g in (ab, c)), in_sum, in_got, lengths,
                after=(outer_done, inner_done),
            )
        else:
            input_grad = join_rows(in_sum[:, :span], blk_swap(in_sum[:, span:], 2))

            def whole(v):
                return add_y(lax.psum_scatter(v, "batch", scatter_dimension=0, tiled=True))

            join_halves = lambda pair: jnp.concatenate([pair[1], pair[0]], axis=0)
            outer_part = join_halves(outer)
            outer_done = whole(halves(outer_part, blk_swap(outer_part, 1), 0)).astype(F32)
            inner_part = join_halves(inner)
            inner_part = jnp.concatenate([inner_part[:width], inner_part[width:]], axis=1)
            inner_done = join(whole(inner_part), 1)
            cols = width // 2
            tall = cols // 3
            whole_a = jnp.concatenate([a_keep, a_send], axis=0)
            whole_c = jnp.concatenate([c_keep, c_send[: c_keep.shape[0]]], axis=0)
            groups = (whole_c[:, :cols], whole_c[:, cols:], whole_a)
            query_done, key_done, value_done = (
                join(whole(jnp.concatenate([g[:, n * tall : (n + 1) * tall] for g in groups], axis=1)), 1)
                for n in range(3)
            )
            output_done = join(whole(whole_a[:, cols:]), 1)
            total = lax.psum(c_send[c_keep.shape[0] :].astype(F32), ("batch", "blk")).reshape(-1)
            vecs = []
            at = 0
            for n in (width,) * 3 + (inner_weight.shape[1],) + (width,) * 5:
                part = total[at : at + n].reshape(batch_size, n // batch_size)
                vecs.append(lax.dynamic_index_in_dim(part, b, 0, keepdims=False))
                at += n
        g_ob, g_ag, g_as, g_b1, g_b2, g_fg, g_fs, g_vb, g_qb = vecs
        return (
            result, input_grad, query_done, g_qb, key_done, value_done, g_vb, output_done, g_ob,
            g_ag, g_as, inner_done, g_b1, outer_done, g_b2, g_fg, g_fs,
        )

    tok = P("batch", "blk", None)
    mat = P("batch", None)
    vec = P("batch")
    return jax.shard_map(
        per_device,
        mesh=mesh,
        in_specs=(tok, P("batch", None)) + (P(),) * 15 + (tok,),
        out_specs=(
            tok, tok, mat, vec, mat, mat, vec, mat, vec, vec, vec, mat, vec, mat, vec, vec, vec,
        ),
        check_vma=False,
    )
```
